512 devices in a mesh: gx: 16 (over y, x_lo), gz: 32 (over z, x_hi, core).
Axes of the slice: x: 4 (x_hi: 2, x_lo: 2; x = x_hi * 2 + x_lo), y: 8, z: 8, core: 2. Of those that a mesh axis runs over, the one named last changes fastest.
Arguments:
- tangents: float32 [8, 2, 2, 1024, 2048], P(None, None, None, 'gz', 'gx'), may hold values from -6 to 6
- baseline_mass_concentration: float32 [2, 1024, 2048], P(None, 'gz', 'gx'), may hold values from 0.5 to 2
- baseline_internal_value: float32 [2, 1024, 2048], P(None, 'gz', 'gx'), may hold values from 2.5 to 5.5
- base_velocity: float32 [2, 1024, 2048], P(None, 'gz', 'gx'), may hold values from 0.15 to 3, as said below
Outputs:
- renormalized: float32 [8, 2, 2, 1024, 2048], P(None, None, None, 'gz', 'gx')
- growth: float32 [8, 8], replicated
The draws below stay inside these ranges and needn't reach their ends.
Inputs may be any that keep to these rules, and one draw needn't show every extreme that they name: `base_velocity`: positive streamwise velocity.
All inputs are finite; a program needn't handle non-finite values.
Results may differ from the reference program's by a relative error of at most 0.000098.
Values sent between devices are 32-bit elements; how exact they have to be, the bound alone decides.
No kernel may reach another device: no remote copies, remote signals or barrier semaphores. Data moves between devices by JAX's collectives and lax.ppermute only.
A program may use at most 64 MiB of HBM per device.

```python
import jax
import jax.numpy as jnp
from jax import lax

K = 8
NEWTON = 4
NY = 2
NX = 2048
NZ = 1024


def draw_base_velocity(key, part):
    position = jnp.arange(NX, dtype=jnp.float32) / NX
    ramp_factor = 0.5 + 1.5 * position
    roughness = jax.random.uniform(key, (NY, NZ, NX), jnp.float32, 0.5, 1.5)
    return (ramp_factor * roughness).astype(jnp.float32)


def shard_levels(key, extent, split, smallest, top_value):
    factor_of = 1.0
    for axis_at, parts in split:
        draws = jax.random.uniform(jax.random.fold_in(jax.random.fold_in(key, 6), axis_at), (parts,), jnp.float32, smallest / len(split), top_value / len(split))
        factor_of = factor_of * jnp.repeat(jnp.exp(draws), extent[axis_at] // parts).reshape((-1,) + (1,) * (len(extent) - 1 - axis_at))
    return factor_of


def bell_draw(rng, dims, spread, bound, pieces=(), held_as=jnp.bfloat16):
    gain = shard_levels(rng, dims, pieces, -0.22, 0.18) if pieces else 1.0
    result = jax.random.normal(rng, dims, jnp.float32) * spread * gain
    return jnp.minimum(jnp.maximum(result, -bound), bound).astype(held_as)


def setup_inputs(seed: int = 0) -> dict:
    streams_of = jax.random.split(jax.random.key(seed), 5)
    tangents = bell_draw(streams_of[0], (K, 2, NY, NZ, NX), 1.0, 6.0, ((3, 32), (4, 16)), jnp.float32)
    baseline_mass_concentration = jnp.clip(0.5 + 1.5 * jax.random.uniform(streams_of[1], (NY, NZ, NX), jnp.float32) ** shard_levels(streams_of[1], (NY, NZ, NX), ((1, 32), (2, 16)), -0.2, 0.2), 0.5, 2.0)
    baseline_internal_value = jnp.clip(2.5 + 3.0 * jax.random.uniform(streams_of[2], (NY, NZ, NX), jnp.float32) ** shard_levels(streams_of[2], (NY, NZ, NX), ((1, 32), (2, 16)), -0.2, 0.2), 2.5, 5.5)
    base_velocity = draw_base_velocity(jax.random.fold_in(streams_of[4], 71), 0)
    return {"tangents": tangents, "baseline_mass_concentration": baseline_mass_concentration, "baseline_internal_value": baseline_internal_value, "base_velocity": base_velocity}


isochoric_warmth_coefficient = 3.0
attraction = 0.5
acentric_coefficient_gradient = 0.6
covolume = 0.15
root_two = 1.4142135623730951
viscosity = 0.2
conductivity = 1.0
courant_number = 0.5

def departure(cell_mass_concentration):
    low_term = 1.0 + (1.0 - root_two) * covolume * cell_mass_concentration
    high_term = 1.0 + (1.0 + root_two) * covolume * cell_mass_concentration
    factor = attraction * (1.0 + acentric_coefficient_gradient) / (2.0 * root_two * covolume)
    value = factor * (jnp.log(low_term) - jnp.log(high_term))
    slope = factor * ((1.0 - root_two) * covolume / low_term - (1.0 + root_two) * covolume / high_term)
    return (value, slope)

def thermal_linearized_gradients(cell_mass_concentration, cell_internal_value):
    nonideal_deviation, departure_slope = departure(cell_mass_concentration)
    converged_thermal_state = cell_internal_value / isochoric_warmth_coefficient
    for newton_step in range(NEWTON):
        thermal_zero_estimate = jnp.sqrt(converged_thermal_state)
        attractive_correction_multiplier = 1.0 + acentric_coefficient_gradient * (1.0 - thermal_zero_estimate)
        internal_mismatch = isochoric_warmth_coefficient * converged_thermal_state + nonideal_deviation * attractive_correction_multiplier - cell_internal_value
        thermal_gradient = isochoric_warmth_coefficient - nonideal_deviation * acentric_coefficient_gradient / (2.0 * thermal_zero_estimate)
        converged_thermal_state = converged_thermal_state - internal_mismatch / thermal_gradient
    thermal_zero_estimate = jnp.sqrt(converged_thermal_state)
    attractive_correction_multiplier = 1.0 + acentric_coefficient_gradient * (1.0 - thermal_zero_estimate)
    thermal_gradient = isochoric_warmth_coefficient - nonideal_deviation * acentric_coefficient_gradient / (2.0 * thermal_zero_estimate)
    internal_gradient_contribution = 1.0 / thermal_gradient
    mass_gradient_contribution = -departure_slope * attractive_correction_multiplier * internal_gradient_contribution
    return (mass_gradient_contribution, internal_gradient_contribution)

def fourth_order(minus_two, minus_one, center, plus_one, plus_two):
    return (16.0 * (minus_one + plus_one) - (minus_two + plus_two) - 30.0 * center) / 12.0

def derivative_x(field):
    return (jnp.roll(field, 2, 2) - 8.0 * jnp.roll(field, 1, 2) + 8.0 * jnp.roll(field, -1, 2) - jnp.roll(field, -2, 2)) / 12.0

def laplacian(field):
    along_x = fourth_order(jnp.roll(field, 2, 2), jnp.roll(field, 1, 2), field, jnp.roll(field, -1, 2), jnp.roll(field, -2, 2))
    along_z = fourth_order(jnp.roll(field, 2, 1), jnp.roll(field, 1, 1), field, jnp.roll(field, -1, 1), jnp.roll(field, -2, 1))
    padded = jnp.pad(field, ((2, 2), (0, 0), (0, 0)))
    along_y = fourth_order(padded[:-4], padded[1:-3], field, padded[3:-1], padded[4:])
    return along_x + along_z + along_y

def operate(tangent_pair, velocity, mass_gradient_contribution, internal_gradient_contribution):
    tangent_temp = mass_gradient_contribution * tangent_pair[0] + internal_gradient_contribution * tangent_pair[1]
    rate_density = -velocity * derivative_x(tangent_pair[0]) + viscosity * laplacian(tangent_pair[0])
    rate_energy = -velocity * derivative_x(tangent_pair[1]) + conductivity * laplacian(tangent_temp)
    return jnp.stack([rate_density, rate_energy])

def reference(tangents, baseline_mass_concentration, baseline_internal_value, base_velocity):
    mass_gradient_contribution, internal_gradient_contribution = thermal_linearized_gradients(baseline_mass_concentration, baseline_internal_value)
    step_size = courant_number / jnp.sqrt(jnp.mean(base_velocity * base_velocity) + 1e-05)

    def advance(tangent_pair):
        rate_one = operate(tangent_pair, base_velocity, mass_gradient_contribution, internal_gradient_contribution)
        predictor = tangent_pair + step_size * rate_one
        return tangent_pair + 0.5 * step_size * (rate_one + operate(predictor, base_velocity, mass_gradient_contribution, internal_gradient_contribution))
    advanced = lax.map(advance, tangents)
    vectors = advanced.shape[0]
    flattened = advanced.reshape(vectors, -1)
    entry_count = float(2 * NY * NZ * NX)
    gram_matrix = jnp.dot(flattened, flattened.T, precision=lax.Precision.HIGHEST) / entry_count
    chol_lower = jnp.linalg.cholesky(gram_matrix)
    identity = jnp.eye(vectors, dtype=jnp.float32)
    inverse = lax.linalg.triangular_solve(chol_lower, identity, left_side=True, lower=True)
    renormalized = jnp.dot(inverse, flattened, precision=lax.Precision.HIGHEST).reshape(advanced.shape)
    return (renormalized, jnp.transpose(chol_lower))
```

```python
import functools

import jax
import jax.numpy as jnp
from jax import lax
from jax.experimental import pallas as pl
from jax.experimental.pallas import tpu as pltpu
from jax.sharding import Mesh, PartitionSpec as P

NEWTON = 4
isochoric_warmth_coefficient = 3.0
attraction = 0.5
acentric_coefficient_gradient = 0.6
covolume = 0.15
root_two = 1.4142135623730951
viscosity = 0.2
conductivity = 1.0
courant_number = 0.5

K = 8
NF = 4 * K
NC = 6
NA = NF + NC
Z = 32
X = 128
TOP = 8
ZE = Z + 16
GX = ("xh", "xl")
GZ = ("zh", "zl")
NEAR = ("xl", "zl")
FAR = ("xh", "zh")
WIRE = 168


def departure(cell_mass_concentration):
    low_term = 1.0 + (1.0 - root_two) * covolume * cell_mass_concentration
    high_term = 1.0 + (1.0 + root_two) * covolume * cell_mass_concentration
    factor = attraction * (1.0 + acentric_coefficient_gradient) / (2.0 * root_two * covolume)
    value = factor * (jnp.log(low_term) - jnp.log(high_term))
    slope = factor * (
        (1.0 - root_two) * covolume / low_term - (1.0 + root_two) * covolume / high_term
    )
    return (value, slope)


def slopes(mass, internal):
    deviation, departure_slope = departure(mass)
    warmth = internal / isochoric_warmth_coefficient
    for _ in range(NEWTON):
        root = jnp.sqrt(warmth)
        multiplier = 1.0 + acentric_coefficient_gradient * (1.0 - root)
        mismatch = isochoric_warmth_coefficient * warmth + deviation * multiplier - internal
        gradient = isochoric_warmth_coefficient - deviation * acentric_coefficient_gradient / (
            2.0 * root
        )
        warmth = warmth - mismatch / gradient
    root = jnp.sqrt(warmth)
    multiplier = 1.0 + acentric_coefficient_gradient * (1.0 - root)
    gradient = isochoric_warmth_coefficient - deviation * acentric_coefficient_gradient / (
        2.0 * root
    )
    energy = 1.0 / gradient
    return (-departure_slope * multiplier * energy, energy)


def lanes():
    return lax.broadcasted_iota(jnp.int32, (8, X), 1)


def prep_kernel(q_ref, mass_ref, internal_ref, velocity_ref, coef_ref, pack_ref):
    density, energy = slopes(mass_ref[...], internal_ref[...])
    coef_ref[0:2] = density
    coef_ref[2:4] = energy
    coef_ref[4:6] = velocity_ref[...]
    group = ((lanes() + 4) >> 3) & 15
    for b in range(3):
        for t in range(Z // 8):
            rows = slice(8 * t, 8 * t + 8)
            acc = jnp.zeros((8, X), jnp.float32)
            for i in range(16 if b < 2 else NC):
                field = q_ref[16 * b + i, rows, :] if b < 2 else coef_ref[i, rows, :]
                moved = pltpu.roll(field, 8 * i, 1) if i else field
                acc = jnp.where(group == i, moved, acc)
            pack_ref[b, rows, :] = acc


def wire_kernel(q_ref, coef_ref, left_ref, right_ref, side_ref, up_ref, down_ref):
    low = (lanes() & 7) < 4
    for b in range(3):
        for t in range(Z // 8):
            rows = slice(8 * t, 8 * t + 8)
            side_ref[b, rows, :] = jnp.where(low, right_ref[b, rows, :], left_ref[b, rows, :])
    for f in range(NA):
        ref, i = (q_ref, f) if f < NF else (coef_ref, f - NF)
        up_ref[4 * f : 4 * f + 4, :] = ref[i, 0:4, :]
        down_ref[4 * f : 4 * f + 4, :] = ref[i, Z - 4 : Z, :]
    for b in range(3):
        r = 4 * NA + 4 * b
        up_ref[r : r + 4, :] = side_ref[b, 0:4, :]
        down_ref[r : r + 4, :] = side_ref[b, Z - 4 : Z, :]
    r = 4 * NA + 12
    up_ref[r:WIRE, :] = jnp.zeros((WIRE - r, X), jnp.float32)
    down_ref[r:WIRE, :] = jnp.zeros((WIRE - r, X), jnp.float32)


def shifted(main, side, lane, both):
    out_main, out_side = [], []
    for d, edge in ((1, lane < 1), (X - 1, lane >= X - 1), (2, lane < 2), (X - 2, lane >= X - 2)):
        moved, turned = pltpu.roll(main, d, 1), pltpu.roll(side, d, 1)
        out_main.append(jnp.where(edge, turned, moved))
        if both:
            out_side.append(jnp.where(edge, moved, turned))
    return out_main, out_side


def stencil_kernel(
    q_ref, coef_ref, side_ref, above_ref, below_ref, a_ref, b_ref, sums_ref,
    em, eh, sm, wm, am, ah, red,
):
    f32 = jnp.float32
    lane = lanes()
    for f in range(NA):
        ref, i = (q_ref, f) if f < NF else (coef_ref, f - NF)
        em[f, TOP - 4 : TOP, :] = above_ref[4 * f : 4 * f + 4, :]
        for t in range(Z // 8):
            em[f, TOP + 8 * t : TOP + 8 * t + 8, :] = ref[i, 8 * t : 8 * t + 8, :]
        em[f, TOP + Z : TOP + Z + 4, :] = below_ref[4 * f : 4 * f + 4, :]
    for b in range(3):
        r = 4 * NA + 4 * b
        sm[b, TOP - 4 : TOP, :] = above_ref[r : r + 4, :]
        sm[b, TOP : TOP + Z, :] = side_ref[b]
        sm[b, TOP + Z : TOP + Z + 4, :] = below_ref[r : r + 4, :]
    for f in range(NA):
        b, i = f // 16, f % 16
        for t in range(5):
            rows = slice(4 + 8 * t, 12 + 8 * t)
            part = sm[b, rows, :]
            eh[f, rows, :] = pltpu.roll(part, X - 8 * i, 1) if i else part

    chunks_t = (4, 12, 20, 28, 36)
    chunks_a = (6, 14, 22, 30, 34)

    def temperature(dst_m, dst_h, src_m, src_h, base, slot, chunks):
        for y in range(2):
            for r in chunks:
                rows = pl.ds(r, 8)
                for dst, src, coef in ((dst_m, src_m, em), (dst_h, src_h, eh)):
                    dst[slot + y, rows, :] = (
                        coef[NF + y, rows, :] * src[base + y, rows, :]
                        + coef[NF + 2 + y, rows, :] * src[base + 2 + y, rows, :]
                    )

    def operate(src_m, src_h, tm, th, base, slot, y, r, both):
        rows = pl.ds(r, 8)
        other = 1 - y
        outs = []

        def loads(pair, i):
            return [p[i, rows, :] for p in pair]

        def along_z(p, i):
            one = p[i, pl.ds(r - 1, 8), :] + p[i, pl.ds(r + 1, 8), :]
            two = p[i, pl.ds(r - 2, 8), :] + p[i, pl.ds(r + 2, 8), :]
            return one, two

        def mix(ones, twos, center):
            return 16.0 * ones - twos - 90.0 * center

        rm, rh = loads((src_m, src_h), base + y)
        dm, dh = loads((src_m, src_h), base + 2 + y)
        cm, ch = loads((tm, th), slot + y)
        xr = shifted(rm, rh, lane, both)
        xe = shifted(dm, dh, lane, both)
        xt = shifted(cm, ch, lane, both)
        for s in range(2 if both else 1):
            src, tmp, coef = ((src_m, tm, em), (src_h, th, eh))[s]
            r1, r2, r3, r4 = xr[s]
            e1, e2, e3, e4 = xe[s]
            t1, t2, t3, t4 = xt[s]
            speed = coef[NF + 4 + y, rows, :] * (-1.0 / 12.0)
            z1, z2 = along_z(src, base + y)
            lap_r = mix(r1 + r2 + z1 + src[base + other, rows, :], r3 + r4 + z2, (rm, rh)[s])
            z1, z2 = along_z(tmp, slot + y)
            lap_t = mix(t1 + t2 + z1 + tmp[slot + other, rows, :], t3 + t4 + z2, (cm, ch)[s])
            rate_r = speed * (8.0 * (r2 - r1) - (r4 - r3)) + (viscosity / 12.0) * lap_r
            rate_e = speed * (8.0 * (e2 - e1) - (e4 - e3)) + (conductivity / 12.0) * lap_t
            outs.append((rate_r, rate_e))
        return outs

    def vector(k, carry):
        base = 4 * k
        temperature(wm.at[0], wm.at[1], em, eh, base, 0, chunks_t)
        for y in range(2):
            for r in chunks_a:
                rows = pl.ds(r, 8)
                (mr, me), (hr, he) = operate(em, eh, wm.at[0], wm.at[1], base, 0, y, r, True)
                am[base + y, rows, :] = mr
                am[base + 2 + y, rows, :] = me
                ah[base + y, rows, :] = hr
                ah[base + 2 + y, rows, :] = he
        temperature(wm.at[0], wm.at[1], am, ah, base, 2, chunks_a)
        for y in range(2):
            for t in range(Z // 8):
                out = operate(am, ah, wm.at[0], wm.at[1], base, 2, y, TOP + 8 * t, False)
                for c in range(2):
                    b_ref[base + 2 * c + y, 8 * t : 8 * t + 8, :] = out[0][c]
                    a_ref[base + 2 * c + y, 8 * t : 8 * t + 8, :] = am[
                        base + 2 * c + y, TOP + 8 * t : TOP + 8 * t + 8, :
                    ]
        return carry

    lax.fori_loop(0, K, vector, 0)

    result = jnp.zeros((8, X), f32)
    red[...] = jnp.zeros_like(red)
    for k in range(K):
        for m in range(5 if k < 4 else 4):
            l = (k + m) % K

            def tile(j, acc, k=k, l=l):
                p, t = j // 4, j % 4
                rows = pl.ds(pl.multiple_of(8 * t, 8), 8)
                qk, ak, bk = (v[4 * k + p, rows, :] for v in (q_ref, a_ref, b_ref))
                ql, al, bl = (v[4 * l + p, rows, :] for v in (q_ref, a_ref, b_ref))
                s0, s1, s2, s3, s4 = acc
                return (
                    s0 + qk * ql,
                    s1 + qk * al + ak * ql,
                    s2 + ak * al + 0.5 * (qk * bl + bk * ql),
                    s3 + 0.5 * (ak * bl + bk * al),
                    s4 + 0.25 * (bk * bl),
                )

            acc = (jnp.zeros((8, X), f32),) * 5
            acc = lax.fori_loop(0, 16, tile, acc, unroll=True)
            for n in range(5):
                red[8 * n + m, k : k + 1, :] = jnp.sum(acc[n], axis=0, keepdims=True)
    for n in range(5):
        for m in range(5):
            col = jnp.sum(red[8 * n + m], axis=1, keepdims=True)
            result = jnp.where(lane == 8 * n + m, col, result)
    speed = jnp.zeros((8, X), f32)
    for y in range(2):
        for t in range(Z // 8):
            v = coef_ref[4 + y, 8 * t : 8 * t + 8, :]
            speed = speed + v * v
    result = jnp.where(lane == 40, jnp.sum(speed, axis=1, keepdims=True), result)
    for n in range(sums_ref.shape[0]):
        sums_ref[n] = result


def finish_kernel(cells, q_ref, a_ref, b_ref, sums_ref, out_ref, growth_ref):
    f32 = jnp.float32
    lane = lanes()
    row = lax.broadcasted_iota(jnp.int32, (8, X), 0)
    total = sums_ref[0]
    for n in range(1, sums_ref.shape[0]):
        total = total + sums_ref[n]
    speed = jnp.broadcast_to(jnp.sum(total[:, 40:41], axis=0, keepdims=True), (8, X))
    step = courant_number / jnp.sqrt(speed * (1.0 / cells) + 1e-05)
    gram = total
    power = step
    for n in range(1, 5):
        gram = gram + power * pltpu.roll(total, X - 8 * n, 1)
        power = power * step
    gram = gram * (1.0 / (2.0 * cells))
    cols = [jnp.broadcast_to(gram[:, m : m + 1], (8, X)) for m in range(5)]

    def entry(i, j):
        k, m = (j, i - j) if i - j <= 4 else (i, j - i + K)
        if m == 4:
            k = min(i, j)
        return jnp.broadcast_to(cols[m][k : k + 1, :], (8, X))

    low = [[None] * K for _ in range(K)]
    inv_diag = []
    for j in range(K):
        d = entry(j, j)
        for p in range(j):
            d = d - low[j][p] * low[j][p]
        root = jnp.sqrt(d)
        low[j][j] = root
        inv_diag.append(1.0 / root)
        for i in range(j + 1, K):
            v = entry(i, j)
            for p in range(j):
                v = v - low[i][p] * low[j][p]
            low[i][j] = v * inv_diag[j]
    inverse = [[None] * K for _ in range(K)]
    for j in range(K):
        inverse[j][j] = inv_diag[j]
        for i in range(j + 1, K):
            v = low[i][j] * inverse[j][j]
            for p in range(j + 1, i):
                v = v + low[i][p] * inverse[p][j]
            inverse[i][j] = -v * inv_diag[i]
    growth = jnp.zeros((8, X), f32)
    for i in range(K):
        for j in range(i + 1):
            growth = jnp.where((row == j) & (lane == i), low[i][j], growth)
    growth_ref[...] = growth
    half = 0.5 * step * step
    for p in range(4):
        for t in range(Z // 8):
            rows = slice(8 * t, 8 * t + 8)
            adv = [
                q_ref[4 * k + p, rows, :]
                + step * a_ref[4 * k + p, rows, :]
                + half * b_ref[4 * k + p, rows, :]
                for k in range(K)
            ]
            for k in range(K):
                v = inverse[k][0] * adv[0]
                for j in range(1, k + 1):
                    v = v + inverse[k][j] * adv[j]
                out_ref[4 * k + p, rows, :] = v


def call(body, outs, scratch=(), flops=1000000):
    shapes = [jax.ShapeDtypeStruct(s, jnp.float32) for s in outs]
    return pl.pallas_call(
        body,
        out_shape=shapes,
        scratch_shapes=[pltpu.VMEM(s, jnp.float32) for s in scratch],
        compiler_params=pltpu.CompilerParams(vmem_limit_bytes=24 * 1024 * 1024),
        cost_estimate=pl.CostEstimate(flops=flops, bytes_accessed=1000000, transcendentals=0),
    )


def ring(array, axes, step):
    size = lax.axis_size(axes)
    return lax.ppermute(array, axes, [(i, (i + step) % size) for i in range(size)])


def gathered(array, axes):
    return lax.all_to_all(array, axes, 0, 0)


def per_device(tangents, mass, internal, velocity):
    cells = float(2 * Z * X * lax.axis_size(GX) * lax.axis_size(GZ))
    near, far = lax.axis_size(NEAR), lax.axis_size(FAR)
    q = tangents.reshape(NF, Z, X)
    coef, pack = call(prep_kernel, [(NC, Z, X), (3, Z, X)])(q, mass, internal, velocity)
    left = ring(pack, GX, 1)
    right = ring(pack, GX, -1)
    side, up, down = call(wire_kernel, [(3, Z, X), (WIRE, X), (WIRE, X)])(q, coef, left, right)
    above = ring(down, GZ, 1)
    below = ring(up, GZ, -1)
    ext = (NA, ZE, X)
    rate, second, sums = call(
        stencil_kernel,
        [(NF, Z, X), (NF, Z, X), (near, 8, X)],
        [ext, ext, (3, ZE, X), (2, 4, ZE, X), (NF, ZE, X), (NF, ZE, X), (40, 8, X)],
    )(q, coef, side, above, below)
    sums = jnp.sum(gathered(sums, NEAR), axis=0)
    sums = gathered(jnp.broadcast_to(sums, (far, 8, X)), FAR)
    out, growth = call(functools.partial(finish_kernel, cells), [(NF, Z, X), (8, X)])(
        q, rate, second, sums
    )
    return (out.reshape(tangents.shape), growth[:, :K])


def solution(mesh):
    gx, gz = mesh.devices.shape
    fine = Mesh(mesh.devices.reshape(gx // 4, 4, gz // 4, 4), GX + GZ)
    in_specs = (P(None, None, None, GZ, GX),) + (P(None, GZ, GX),) * 3
    out_specs = (P(None, None, None, GZ, GX), P())
    return jax.shard_map(
        per_device, mesh=fine, in_specs=in_specs, out_specs=out_specs, check_vma=False
    )
```

```python
import functools

import jax
import jax.numpy as jnp
from jax import lax
from jax.experimental import pallas as pl
from jax.experimental.pallas import tpu as pltpu
from jax.sharding import Mesh, PartitionSpec as P

NEWTON = 4
isochoric_warmth_coefficient = 3.0
attraction = 0.5
acentric_coefficient_gradient = 0.6
covolume = 0.15
root_two = 1.4142135623730951
viscosity = 0.2
conductivity = 1.0
courant_number = 0.5

K = 8
NF = 4 * K
NC = 6
NA = NF + NC
Z = 32
X = 128
GX = ("xh", "xl")
GZ = ("zh", "zl")
NEAR = ("xl", "zl")
FAR = ("xh", "zh")
F32 = jnp.float32


def departure(cell_mass_concentration):
    low_term = 1.0 + (1.0 - root_two) * covolume * cell_mass_concentration
    high_term = 1.0 + (1.0 + root_two) * covolume * cell_mass_concentration
    factor = attraction * (1.0 + acentric_coefficient_gradient) / (2.0 * root_two * covolume)
    value = factor * (jnp.log(low_term) - jnp.log(high_term))
    slope = factor * (
        (1.0 - root_two) * covolume / low_term - (1.0 + root_two) * covolume / high_term
    )
    return (value, slope)


def slopes(mass, internal):
    deviation, departure_slope = departure(mass)
    warmth = internal / isochoric_warmth_coefficient
    for _ in range(NEWTON):
        root = jnp.sqrt(warmth)
        multiplier = 1.0 + acentric_coefficient_gradient * (1.0 - root)
        mismatch = isochoric_warmth_coefficient * warmth + deviation * multiplier - internal
        gradient = isochoric_warmth_coefficient - deviation * acentric_coefficient_gradient / (
            2.0 * root
        )
        warmth = warmth - mismatch / gradient
    root = jnp.sqrt(warmth)
    multiplier = 1.0 + acentric_coefficient_gradient * (1.0 - root)
    gradient = isochoric_warmth_coefficient - deviation * acentric_coefficient_gradient / (
        2.0 * root
    )
    energy = 1.0 / gradient
    return (-departure_slope * multiplier * energy, energy)


def lanes():
    return lax.broadcasted_iota(jnp.int32, (8, X), 1)


def tile(t):
    return slice(8 * t, 8 * t + 8)


def prep_kernel(
    q_hbm, mass_hbm, internal_hbm, velocity_hbm, q_ref, coef_ref, pack_ref, mass, internal, sems
):
    copies = [
        pltpu.make_async_copy(src, dst, sems.at[i])
        for i, (src, dst) in enumerate(
            (
                (mass_hbm, mass),
                (internal_hbm, internal),
                (velocity_hbm, coef_ref.at[pl.ds(4, 2)]),
                (q_hbm, q_ref),
            )
        )
    ]
    for copy in copies:
        copy.start()
    copies[0].wait()
    copies[1].wait()
    density, energy = slopes(mass[...], internal[...])
    coef_ref[0:2] = density
    coef_ref[2:4] = energy
    copies[2].wait()
    copies[3].wait()
    group = lanes() >> 3
    for b in range(3):
        for t in range(Z // 8):
            acc = jnp.zeros((8, X), F32)
            for i in range(16 if b < 2 else NC):
                field = q_ref[16 * b + i, tile(t), :] if b < 2 else coef_ref[i, tile(t), :]
                moved = pltpu.roll(field, 8 * i, 1) if i else field
                acc = jnp.where(group == i, moved, acc)
            pack_ref[b, tile(t), :] = acc


def pairs():
    return [(k, m, (k + m) % K) for k in range(K) for m in range(5 if k < 4 else 4)]


def columns(result, lane, red, sets):
    for n in sets:
        for m in range(5):
            col = jnp.sum(red[8 * n + m], axis=1, keepdims=True)
            result = jnp.where(lane == 8 * n + m, col, result)
    return result


def own_kernel(q_ref, coef_ref, warm_ref, sums_ref, red):
    lane = lanes()
    red[...] = jnp.zeros_like(red)
    for k in range(K):
        for y in range(2):
            for t in range(Z // 8):
                warm_ref[2 * k + y, tile(t), :] = (
                    coef_ref[y, tile(t), :] * q_ref[4 * k + y, tile(t), :]
                    + coef_ref[2 + y, tile(t), :] * q_ref[4 * k + 2 + y, tile(t), :]
                )
    for k, m, l in pairs():
        acc = jnp.zeros((8, X), F32)
        for p in range(4):
            for t in range(Z // 8):
                acc = acc + q_ref[4 * k + p, tile(t), :] * q_ref[4 * l + p, tile(t), :]
        red[m, k : k + 1, :] = jnp.sum(acc, axis=0, keepdims=True)
    speed = jnp.zeros((8, X), F32)
    for y in range(2):
        for t in range(Z // 8):
            v = coef_ref[4 + y, tile(t), :]
            speed = speed + v * v
    result = jnp.where(lane == 40, jnp.sum(speed, axis=1, keepdims=True), 0.0)
    sums_ref[...] = columns(result, lane, red, range(1))


def wire_kernel(q_ref, coef_ref, side_ref, up_ref):
    for f in range(NA):
        ref, i = (q_ref, f) if f < NF else (coef_ref, f - NF)
        up_ref[f] = ref[i, 0:8, :]
    for b in range(3):
        up_ref[NA + b] = side_ref[b, 0:8, :]


def wide_shifts(main, side, lane):
    m = [pltpu.roll(main, d, 1) for d in (1, X - 1, 2, X - 2)]
    s = [pltpu.roll(side, d, 1) for d in (1, X - 1, 2, X - 2)]
    out_main = (
        m[0],
        jnp.where(lane >= X - 1, s[1], m[1]),
        m[2],
        jnp.where(lane >= X - 2, s[3], m[3]),
    )
    out_side = (jnp.where(lane < 1, m[0], s[0]), s[1], jnp.where(lane < 2, m[2], s[2]), s[3])
    return (out_main, out_side)


def block_shifts(main, side, lane):
    out = []
    for d, mask in (
        (1, (lane >= 1) & (lane < 4)),
        (X - 1, (lane < 4) | (lane >= X - 1)),
        (2, (lane >= 2) & (lane < 4)),
        (X - 2, (lane < 4) | (lane >= X - 2)),
    ):
        out.append(jnp.where(mask, pltpu.roll(side, d, 1), pltpu.roll(main, d, 1)))
    return out


def rate(speed, xr, xe, xt, r_at, t_at, r_other, t_other):
    def lap(x, at, other):
        ones = x[0] + x[1] + (at(-1) + at(1)) + other
        twos = x[2] + x[3] + (at(-2) + at(2))
        return 16.0 * ones - twos - 90.0 * at(0)

    def slope(x):
        return 8.0 * (x[1] - x[0]) - (x[3] - x[2])

    rate_r = speed * slope(xr) + (viscosity / 12.0) * lap(xr, r_at, r_other)
    rate_e = speed * slope(xe) + (conductivity / 12.0) * lap(xt, t_at, t_other)
    return (rate_r, rate_e)


def cross_sums(lane, red, qd, ad, bd, tiles):
    for k, m, l in pairs():
        acc = [jnp.zeros((8, X), F32)] * 4
        for p in range(4):
            for t in range(tiles):
                qk, ak, bk = (v[4 * k + p, tile(t), :] for v in (qd, ad, bd))
                ql, al, bl = (v[4 * l + p, tile(t), :] for v in (qd, ad, bd))
                acc[0] = acc[0] + (qk * al + ak * ql)
                acc[1] = acc[1] + (ak * al + (qk * bl + bk * ql))
                acc[2] = acc[2] + (ak * bl + bk * al)
                acc[3] = acc[3] + bk * bl
        for n in range(4):
            red[8 * n + 8 + m, k : k + 1, :] = jnp.sum(acc[n], axis=0, keepdims=True)


def inner_kernel(
    q_ref, coef_ref, warm_ref, side_ref, own_ref,
    ad_ref, bd_ref, tail_ref, sums_ref,
    eh, wh, am, ah, aw, tm, th, tw, qd, red,
):
    lane = lanes()
    block = lane < 4
    red[...] = jnp.zeros_like(red)
    for f in range(NA):
        b, i = f // 16, f % 16
        for t in range(Z // 8):
            part = side_ref[b, tile(t), :]
            eh[f, tile(t), :] = pltpu.roll(part, X - 8 * i, 1) if i else part
    for f in range(NF):
        for t in range(3):
            rows = slice(8 * t + 4, 8 * t + 12)
            qd[f, tile(t), :] = jnp.where(block, eh[f, rows, :], q_ref[f, rows, :])

    def vector(k, carry):
        base = 4 * k
        for y in range(2):
            for t in range(Z // 8):
                wh[y, tile(t), :] = (
                    eh[NF + y, tile(t), :] * eh[base + y, tile(t), :]
                    + eh[NF + 2 + y, tile(t), :] * eh[base + 2 + y, tile(t), :]
                )
        for y in range(2):
            for r in (2, 10, 18, 22):
                rows = pl.ds(r, 8)
                xr = wide_shifts(q_ref[base + y, rows, :], eh[base + y, rows, :], lane)
                xe = wide_shifts(q_ref[base + 2 + y, rows, :], eh[base + 2 + y, rows, :], lane)
                xt = wide_shifts(warm_ref[2 * k + y, rows, :], wh[y, rows, :], lane)
                out = []
                for s in range(2):
                    src, off = ((q_ref, 0), (eh, 0))[s]
                    speed = coef_ref[4 + y, rows, :] if s == 0 else eh[NF + 4 + y, rows, :]

                    def r_at(d, src=src):
                        return src[base + y, pl.ds(r + d, 8), :]

                    def t_at(d, s=s, plane=y):
                        if s == 0:
                            return warm_ref[2 * k + plane, pl.ds(r + d, 8), :]
                        return wh[plane, pl.ds(r + d, 8), :]

                    out.append(
                        rate(
                            speed * (-1.0 / 12.0), xr[s], xe[s], xt[s], r_at, t_at,
                            src[base + 1 - y, rows, :], t_at(0, plane=1 - y),
                        )
                    )
                for c in range(2):
                    i = base + 2 * c + y
                    am[i, rows, :] = out[0][c]
                    ah[i, rows, :] = out[1][c]
                    aw[i, rows, :] = jnp.where(block, out[1][c], out[0][c])
        for y in range(2):
            for r in (2, 10, 18, 22):
                rows = pl.ds(r, 8)
                main = coef_ref[y, rows, :] * am[base + y, rows, :] + (
                    coef_ref[2 + y, rows, :] * am[base + 2 + y, rows, :]
                )
                side = eh[NF + y, rows, :] * ah[base + y, rows, :] + (
                    eh[NF + 2 + y, rows, :] * ah[base + 2 + y, rows, :]
                )
                tm[y, rows, :] = main
                th[y, rows, :] = side
                tw[y, rows, :] = jnp.where(block, side, main)
        for y in range(2):
            for t in range(3):
                r = 8 * t + 4
                rows = pl.ds(r, 8)
                speed = jnp.where(block, eh[NF + 4 + y, rows, :], coef_ref[4 + y, rows, :])
                out = rate(
                    speed * (-1.0 / 12.0),
                    block_shifts(am[base + y, rows, :], ah[base + y, rows, :], lane),
                    block_shifts(am[base + 2 + y, rows, :], ah[base + 2 + y, rows, :], lane),
                    block_shifts(tm[y, rows, :], th[y, rows, :], lane),
                    lambda d: aw[base + y, pl.ds(r + d, 8), :],
                    lambda d: tw[y, pl.ds(r + d, 8), :],
                    aw[base + 1 - y, rows, :],
                    tw[1 - y, rows, :],
                )
                for c in range(2):
                    i = base + 2 * c + y
                    bd_ref[i, tile(t), :] = 0.5 * out[c]
                    ad_ref[i, tile(t), :] = aw[i, rows, :]
        for p in range(4):
            tail_ref[0, base + p] = am[base + p, 22:30, :]
            tail_ref[1, base + p] = ah[base + p, 22:30, :]
        return carry

    lax.fori_loop(0, K, vector, 0)
    cross_sums(lane, red, qd, ad_ref, bd_ref, 3)
    sums_ref[...] = columns(own_ref[...], lane, red, range(1, 5))


def edge_kernel(
    q_ref, coef_ref, side_ref, below_ref, tail_ref, inner_ref,
    ad_ref, bd_ref, sums_ref,
    em, eh, wm, wh, am, ah, aw, tm, th, tw, qd, red,
):
    lane = lanes()
    block = lane < 4
    red[...] = jnp.zeros_like(red)
    for f in range(NA):
        ref, i = (q_ref, f) if f < NF else (coef_ref, f - NF)
        em[f, 0:8, :] = ref[i, 24:32, :]
        em[f, 8:16, :] = below_ref[f]
        b, i = f // 16, f % 16
        for t, part in enumerate((side_ref[b, 24:32, :], below_ref[NA + b])):
            eh[f, tile(t), :] = pltpu.roll(part, X - 8 * i, 1) if i else part
    for f in range(NF):
        qd[f] = jnp.where(block, eh[f, 4:12, :], em[f, 4:12, :])

    def vector(k, carry):
        base = 4 * k
        for y in range(2):
            for t in range(2):
                for dst, src in ((wm, em), (wh, eh)):
                    dst[y, tile(t), :] = (
                        src[NF + y, tile(t), :] * src[base + y, tile(t), :]
                        + src[NF + 2 + y, tile(t), :] * src[base + 2 + y, tile(t), :]
                    )
        for p in range(4):
            am[base + p, 0:8, :] = tail_ref[0, base + p]
            ah[base + p, 0:8, :] = tail_ref[1, base + p]
            aw[base + p, 0:8, :] = jnp.where(block, tail_ref[1, base + p], tail_ref[0, base + p])
        for y in range(2):
            rows = pl.ds(6, 8)
            xr = wide_shifts(em[base + y, rows, :], eh[base + y, rows, :], lane)
            xe = wide_shifts(em[base + 2 + y, rows, :], eh[base + 2 + y, rows, :], lane)
            xt = wide_shifts(wm[y, rows, :], wh[y, rows, :], lane)
            out = []
            for s in range(2):
                src, warm = ((em, wm), (eh, wh))[s]
                out.append(
                    rate(
                        src[NF + 4 + y, rows, :] * (-1.0 / 12.0), xr[s], xe[s], xt[s],
                        lambda d: src[base + y, pl.ds(6 + d, 8), :],
                        lambda d: warm[y, pl.ds(6 + d, 8), :],
                        src[base + 1 - y, rows, :],
                        warm[1 - y, rows, :],
                    )
                )
            for c in range(2):
                i = base + 2 * c + y
                am[i, 8:16, :] = out[0][c]
                ah[i, 8:16, :] = out[1][c]
                aw[i, 8:16, :] = jnp.where(block, out[1][c], out[0][c])
        for y in range(2):
            for r in (4, 8):
                rows, here = pl.ds(r, 8), pl.ds(r - 2, 8)
                main = em[NF + y, here, :] * am[base + y, rows, :] + (
                    em[NF + 2 + y, here, :] * am[base + 2 + y, rows, :]
                )
                side = eh[NF + y, here, :] * ah[base + y, rows, :] + (
                    eh[NF + 2 + y, here, :] * ah[base + 2 + y, rows, :]
                )
                tm[y, rows, :] = main
                th[y, rows, :] = side
                tw[y, rows, :] = jnp.where(block, side, main)
        for y in range(2):
            rows = pl.ds(6, 8)
            speed = jnp.where(block, eh[NF + 4 + y, 4:12, :], em[NF + 4 + y, 4:12, :])
            out = rate(
                speed * (-1.0 / 12.0),
                block_shifts(am[base + y, rows, :], ah[base + y, rows, :], lane),
                block_shifts(am[base + 2 + y, rows, :], ah[base + 2 + y, rows, :], lane),
                block_shifts(tm[y, rows, :], th[y, rows, :], lane),
                lambda d: aw[base + y, pl.ds(6 + d, 8), :],
                lambda d: tw[y, pl.ds(6 + d, 8), :],
                aw[base + 1 - y, rows, :],
                tw[1 - y, rows, :],
            )
            for c in range(2):
                i = base + 2 * c + y
                bd_ref[i] = 0.5 * out[c]
                ad_ref[i] = aw[i, 6:14, :]
        return carry

    lax.fori_loop(0, K, vector, 0)
    cross_sums(lane, red, qd, ad_ref, bd_ref, 1)
    result = columns(jnp.zeros((8, X), F32), lane, red, range(1, 5)) + inner_ref[...]
    for n in range(sums_ref.shape[0]):
        sums_ref[n] = result


def give_kernel(ad_ref, bd_ref, ade_ref, bde_ref, out_ref):
    group = lanes() >> 2
    for n, (ref, edge) in enumerate(((ad_ref, ade_ref), (bd_ref, bde_ref))):
        for t in range(Z // 8):
            acc = jnp.zeros((8, X), F32)
            for f in range(NF):
                part = ref[f, tile(t), :] if t < 3 else edge[f]
                acc = jnp.where(group == f, pltpu.roll(part, 4 * f, 1) if f else part, acc)
            out_ref[n, tile(t), :] = acc


def place_kernel(ad_ref, bd_ref, ade_ref, bde_ref, got_ref, a_ref, b_ref, down_ref):
    block = lanes() < 4
    for n, (ref, edge, out) in enumerate(((ad_ref, ade_ref, a_ref), (bd_ref, bde_ref, b_ref))):
        for f in range(NF):
            for t in range(Z // 8):
                part = ref[f, tile(t), :] if t < 3 else edge[f]
                got = got_ref[n, tile(t), :]
                got = pltpu.roll(got, X - 4 * f, 1) if f else got
                part = jnp.where(block, got, part)
                if t < 3:
                    out[f, 8 * t + 4 : 8 * t + 12, :] = part
                else:
                    out[f, 28:32, :] = part[0:4, :]
                    out[f, 0:4, :] = jnp.zeros((4, X), F32)
                    r = 4 * (NF * n + f)
                    down_ref[r : r + 4, :] = part[4:8, :]


def finish_kernel(cells, q_ref, a_ref, b_ref, above_ref, sums_ref, out_ref, growth_ref, first):
    lane = lanes()
    row = lax.broadcasted_iota(jnp.int32, (8, X), 0)
    for n, ref in enumerate((a_ref, b_ref)):
        for f in range(NF):
            r = 4 * (NF * n + f)
            first[n, f, 0:4, :] = above_ref[r : r + 4, :]
            first[n, f, 4:8, :] = ref[f, 4:8, :]
    total = sums_ref[0]
    for n in range(1, sums_ref.shape[0]):
        total = total + sums_ref[n]
    speed = jnp.broadcast_to(jnp.sum(total[:, 40:41], axis=0, keepdims=True), (8, X))
    step = courant_number / jnp.sqrt(speed * (1.0 / cells) + 1e-05)
    gram = total
    power = step
    for n in range(1, 5):
        gram = gram + power * pltpu.roll(total, X - 8 * n, 1)
        power = power * step
    gram = gram * (1.0 / (2.0 * cells))
    cols = [jnp.broadcast_to(gram[:, m : m + 1], (8, X)) for m in range(5)]

    def entry(i, j):
        k, m = (j, i - j) if i - j <= 4 else (i, j - i + K)
        if m == 4:
            k = min(i, j)
        return jnp.broadcast_to(cols[m][k : k + 1, :], (8, X))

    low = [[None] * K for _ in range(K)]
    inv_diag = []
    for j in range(K):
        d = entry(j, j)
        for p in range(j):
            d = d - low[j][p] * low[j][p]
        root = jnp.sqrt(d)
        low[j][j] = root
        inv_diag.append(1.0 / root)
        for i in range(j + 1, K):
            v = entry(i, j)
            for p in range(j):
                v = v - low[i][p] * low[j][p]
            low[i][j] = v * inv_diag[j]
    inverse = [[None] * K for _ in range(K)]
    for j in range(K):
        inverse[j][j] = inv_diag[j]
        for i in range(j + 1, K):
            v = low[i][j] * inverse[j][j]
            for p in range(j + 1, i):
                v = v + low[i][p] * inverse[p][j]
            inverse[i][j] = -v * inv_diag[i]
    growth = jnp.zeros((8, X), F32)
    for i in range(K):
        for j in range(i + 1):
            growth = jnp.where((row == j) & (lane == i), low[i][j], growth)
    growth_ref[...] = growth
    square = step * step
    for p in range(4):
        for t in range(Z // 8):
            adv = []
            for k in range(K):
                f = 4 * k + p
                a, b = (
                    (first[0, f], first[1, f])
                    if t == 0
                    else (a_ref[f, tile(t), :], b_ref[f, tile(t), :])
                )
                adv.append(q_ref[f, tile(t), :] + step * a + square * b)
            for k in range(K):
                v = inverse[k][0] * adv[0]
                for j in range(1, k + 1):
                    v = v + inverse[k][j] * adv[j]
                out_ref[4 * k + p, tile(t), :] = v


def call(body, outs, scratch=(), cost=2000000, limit=24, **more):
    shapes = [jax.ShapeDtypeStruct(s, F32) for s in outs]
    return pl.pallas_call(
        body,
        out_shape=shapes,
        scratch_shapes=[pltpu.VMEM(s, F32) if isinstance(s, tuple) else s for s in scratch],
        compiler_params=pltpu.CompilerParams(vmem_limit_bytes=limit * 1024 * 1024),
        cost_estimate=pl.CostEstimate(flops=cost, bytes_accessed=cost, transcendentals=0),
        **more,
    )


def ring(array, axes, step):
    size = lax.axis_size(axes)
    return lax.ppermute(array, axes, [(i, (i + step) % size) for i in range(size)])


def gathered(array, axes):
    return lax.all_to_all(array, axes, 0, 0)


def per_device(tangents, mass, internal, velocity):
    cells = float(2 * Z * X * lax.axis_size(GX) * lax.axis_size(GZ))
    near, far = lax.axis_size(NEAR), lax.axis_size(FAR)
    whole, inner, edge, tall = (NF, Z, X), (NF, 24, X), (NF, 8, X), (NA, 16, X)
    q, coef, pack = call(
        prep_kernel,
        [whole, (NC, Z, X), (3, Z, X)],
        [(2, Z, X), (2, Z, X), pltpu.SemaphoreType.DMA((4,))],
        limit=60,
        in_specs=[pl.BlockSpec(memory_space=pl.ANY)] * 4,
    )(tangents.reshape(whole), mass, internal, velocity)
    side = ring(pack, GX, -1)
    warm, own = call(own_kernel, [(2 * K, Z, X), (8, X)], [(8, 8, X)])(q, coef)
    side, warm, own = lax.optimization_barrier((side, warm, own))
    (up,) = call(wire_kernel, [(NA + 3, 8, X)])(q, coef, side)
    below = ring(up, GZ, -1)
    ad, bd, tail, part = call(
        inner_kernel,
        [inner, inner, (2, NF, 8, X), (8, X)],
        [(NA, Z, X), (2, Z, X), whole, whole, whole, (2, Z, X), (2, Z, X), (2, Z, X), inner, (40, 8, X)],
    )(q, coef, warm, side, own)
    low = (NF, 16, X)
    ade, bde, sums = call(
        edge_kernel,
        [edge, edge, (near, 8, X)],
        [tall, tall, (2, 16, X), (2, 16, X), low, low, low]
        + [(2, 16, X)] * 3
        + [edge, (40, 8, X)],
    )(q, coef, side, below, tail, part)
    sums = jnp.sum(gathered(sums, NEAR), axis=0)
    (give,) = call(give_kernel, [(2, Z, X)])(ad, bd, ade, bde)
    got = ring(give, GX, 1)
    sums, got = lax.optimization_barrier((sums, got))
    sums = gathered(jnp.broadcast_to(sums, (far, 8, X)), FAR)
    a, b, down = call(place_kernel, [whole, whole, (8 * NF, X)])(ad, bd, ade, bde, got)
    above = ring(down, GZ, 1)
    out, growth = call(
        functools.partial(finish_kernel, cells), [whole, (8, X)], [(2, NF, 8, X)]
    )(q, a, b, above, sums)
    return (out.reshape(tangents.shape), growth[:, :K])


def solution(mesh):
    gx, gz = mesh.devices.shape
    fine = Mesh(mesh.devices.reshape(gx // 4, 4, gz // 4, 4), GX + GZ)
    in_specs = (P(None, None, None, GZ, GX),) + (P(None, GZ, GX),) * 3
    out_specs = (P(None, None, None, GZ, GX), P())
    return jax.shard_map(
        per_device, mesh=fine, in_specs=in_specs, out_specs=out_specs, check_vma=False
    )
```

```python
import functools

import jax
import jax.numpy as jnp
from jax import lax
from jax.experimental import pallas as pl
from jax.experimental.pallas import tpu as pltpu
from jax.sharding import Mesh, PartitionSpec as P

NEWTON = 4
isochoric_warmth_coefficient = 3.0
attraction = 0.5
acentric_coefficient_gradient = 0.6
covolume = 0.15
root_two = 1.4142135623730951
viscosity = 0.2
conductivity = 1.0
courant_number = 0.5

K = 8
NF = 4 * K
NC = 6
NA = NF + NC
Z = 32
X = 128
GX = ("xh", "xl")
GZ = ("zh", "zl")
NEAR = ("xl", "zl")
FAR = ("xh", "zh")
F32 = jnp.float32


def departure(cell_mass_concentration):
    low_term = 1.0 + (1.0 - root_two) * covolume * cell_mass_concentration
    high_term = 1.0 + (1.0 + root_two) * covolume * cell_mass_concentration
    factor = attraction * (1.0 + acentric_coefficient_gradient) / (2.0 * root_two * covolume)
    value = factor * (jnp.log(low_term) - jnp.log(high_term))
    slope = factor * (
        (1.0 - root_two) * covolume / low_term - (1.0 + root_two) * covolume / high_term
    )
    return (value, slope)


def slopes(mass, internal):
    deviation, departure_slope = departure(mass)
    warmth = internal / isochoric_warmth_coefficient
    for _ in range(NEWTON):
        root = jnp.sqrt(warmth)
        multiplier = 1.0 + acentric_coefficient_gradient * (1.0 - root)
        mismatch = isochoric_warmth_coefficient * warmth + deviation * multiplier - internal
        gradient = isochoric_warmth_coefficient - deviation * acentric_coefficient_gradient / (
            2.0 * root
        )
        warmth = warmth - mismatch / gradient
    root = jnp.sqrt(warmth)
    multiplier = 1.0 + acentric_coefficient_gradient * (1.0 - root)
    gradient = isochoric_warmth_coefficient - deviation * acentric_coefficient_gradient / (
        2.0 * root
    )
    energy = 1.0 / gradient
    return (-departure_slope * multiplier * energy, energy)


def lanes():
    return lax.broadcasted_iota(jnp.int32, (8, X), 1)


def tile(t):
    return slice(8 * t, 8 * t + 8)


def prep_kernel(
    q_hbm, mass_hbm, internal_hbm, velocity_hbm, coef_ref, pack_ref, rows_ref, q, mass, internal, sems
):
    copies = [
        pltpu.make_async_copy(src, dst, sems.at[i])
        for i, (src, dst) in enumerate(
            (
                (mass_hbm, mass),
                (internal_hbm, internal),
                (velocity_hbm, coef_ref.at[pl.ds(4, 2)]),
                (q_hbm, q),
            )
        )
    ]
    for copy in copies:
        copy.start()
    copies[0].wait()
    copies[1].wait()
    density, energy = slopes(mass[...], internal[...])
    coef_ref[0:2] = density
    coef_ref[2:4] = energy
    copies[2].wait()
    copies[3].wait()
    group = lanes() >> 3
    for t in range(Z // 8):
        for c in range(2):
            acc = q[2 * c, tile(t), :]
            for y in range(2):
                for k in range(K):
                    i = 8 * y + k
                    if i:
                        part = pltpu.roll(q[4 * k + 2 * c + y, tile(t), :], 8 * i, 1)
                        acc = jnp.where(group == i, part, acc)
            pack_ref[c, tile(t), :] = acc
        acc = jnp.where(group == 0, coef_ref[0, tile(t), :], 0.0)
        for i in range(1, NC):
            acc = jnp.where(group == i, pltpu.roll(coef_ref[i, tile(t), :], 8 * i, 1), acc)
        pack_ref[2, tile(t), :] = acc
    for f in range(NA):
        rows_ref[f] = q[f, 0:8, :] if f < NF else coef_ref[f - NF, 0:8, :]


def pairs():
    return [(k, m, (k + m) % K) for k in range(K) for m in range(5 if k < 4 else 4)]


def clear(red, sets):
    for n in range(sets):
        for k in range(4, K):
            red[5 * n + 4, 8 * k : 8 * k + 8, :] = jnp.zeros((8, X), F32)


def columns(result, lane, red, sets):
    for n, place in enumerate(sets):
        for m in range(5):
            acc = red[5 * n + m, pl.ds(0, 8, stride=8), :]
            for s in range(1, 8):
                acc = acc + red[5 * n + m, pl.ds(s, 8, stride=8), :]
            col = jnp.sum(acc, axis=1, keepdims=True)
            result = jnp.where(lane == 8 * place + m, col, result)
    return result


def own_kernel(q_ref, coef_ref, warm_ref, last_ref, sums_ref, red):
    lane = lanes()
    clear(red, 1)
    group = lane >> 3
    for t in range(Z // 8):
        last = [None] * 3
        for y in range(2):
            for k in range(K):
                i = 8 * y + k
                fields = [q_ref[4 * k + 2 * c + y, tile(t), :] for c in range(2)]
                fields.append(
                    coef_ref[y, tile(t), :] * fields[0] + coef_ref[2 + y, tile(t), :] * fields[1]
                )
                warm_ref[2 * k + y, tile(t), :] = fields[2]
                for n in range(3):
                    part = pltpu.roll(fields[n], (8 * i + 8) % X, 1) if i < 15 else fields[n]
                    last[n] = part if i == 0 else jnp.where(group == i, part, last[n])
        for n in range(3):
            last_ref[n, tile(t), :] = last[n]
    for k, m, l in pairs():
        acc = jnp.zeros((8, X), F32)
        for p in range(4):
            for t in range(Z // 8):
                acc = acc + q_ref[4 * k + p, tile(t), :] * q_ref[4 * l + p, tile(t), :]
        red[m, 8 * k : 8 * k + 8, :] = acc
    speed = jnp.zeros((8, X), F32)
    for y in range(2):
        for t in range(Z // 8):
            v = coef_ref[4 + y, tile(t), :]
            speed = speed + v * v
    result = jnp.where(lane == 40, jnp.sum(speed, axis=1, keepdims=True), 0.0)
    sums_ref[...] = columns(result, lane, red, (0,))


def corner_kernel(side_ref, corner_ref):
    for b in range(3):
        corner_ref[b] = side_ref[b, 0:8, :]


def side_of(packed, i):
    return pltpu.roll(packed, X - 8 * i, 1) if i else packed


def spread(packed, lane, n):
    out = jnp.where(lane < 8, side_of(packed, 2 * n), 0.0)
    out = jnp.where((lane >= 64) & (lane < 72), pltpu.roll(packed, 56 - 16 * n, 1), out)
    for d in (8, 16, 32):
        out = out + pltpu.roll(out, d, 1)
    return out


def packed_shifts(side, last, lane):
    col = lane & 7
    return (
        jnp.where(col < 1, pltpu.roll(last, 121, 1), pltpu.roll(side, 1, 1)),
        pltpu.roll(side, X - 1, 1),
        jnp.where(col < 2, pltpu.roll(last, 122, 1), pltpu.roll(side, 2, 1)),
        pltpu.roll(side, X - 2, 1),
    )


def wide_shifts(main, side, lane):
    ahead = jnp.where(lane < 2, side, main)
    return (
        pltpu.roll(main, 1, 1),
        pltpu.roll(ahead, X - 1, 1),
        pltpu.roll(main, 2, 1),
        pltpu.roll(ahead, X - 2, 1),
    )


def block_shifts(main, side, lane):
    return [
        pltpu.roll(jnp.where(lane < n, side, main), d, 1)
        for n, d in ((3, 1), (5, X - 1), (2, 2), (6, X - 2))
    ]


def rate(speed, xr, xe, xt, r_at, t_at, r_other, t_other):
    def lap(x, at, other):
        ones = x[0] + x[1] + (at(-1) + at(1)) + other
        twos = x[2] + x[3] + (at(-2) + at(2))
        return 16.0 * ones - twos - 90.0 * at(0)

    def slope(x):
        return 8.0 * (x[1] - x[0]) - (x[3] - x[2])

    rate_r = speed * slope(xr) + (viscosity / 12.0) * lap(xr, r_at, r_other)
    rate_e = speed * slope(xe) + (conductivity / 12.0) * lap(xt, t_at, t_other)
    return (rate_r, rate_e)


def cross_sums(red, qd, ad, bd, tiles):
    for k, m, l in pairs():
        acc = [jnp.zeros((8, X), F32)] * 4
        for p in range(4):
            for t in range(tiles):
                qk, ak, bk = (v[4 * k + p, tile(t), :] for v in (qd, ad, bd))
                ql, al, bl = (v[4 * l + p, tile(t), :] for v in (qd, ad, bd))
                acc[0] = acc[0] + (qk * al + ak * ql)
                acc[1] = acc[1] + (ak * al + (qk * bl + bk * ql))
                acc[2] = acc[2] + (ak * bl + bk * al)
                acc[3] = acc[3] + bk * bl
        for n in range(4):
            red[5 * n + m, 8 * k : 8 * k + 8, :] = acc[n]


def packed_rate(side, last, warm, pc, out, r, to, lane):
    rows = slice(r, r + 8)
    got = rate(
        pc[2, rows, :] * (-1.0 / 12.0),
        packed_shifts(side[0, rows, :], last[0, rows, :], lane),
        packed_shifts(side[1, rows, :], last[1, rows, :], lane),
        packed_shifts(warm[rows, :], last[2, rows, :], lane),
        lambda d: side[0, r + d : r + d + 8, :],
        lambda d: warm[r + d : r + d + 8, :],
        pltpu.roll(side[0, rows, :], 64, 1),
        pltpu.roll(warm[rows, :], 64, 1),
    )
    dest = slice(to, to + 8)
    out[0, dest, :] = got[0]
    out[1, dest, :] = got[1]
    out[2, dest, :] = pc[0, rows, :] * got[0] + pc[1, rows, :] * got[1]


def first_rate(field, coef, warm, side, side_warm, am, k, y, r, to, lane):
    i, rows = 8 * y + k, slice(r, r + 8)
    got = rate(
        coef(4 + y, r) * (-1.0 / 12.0),
        wide_shifts(field(4 * k + y, r), side_of(side[0, rows, :], i), lane),
        wide_shifts(field(4 * k + 2 + y, r), side_of(side[1, rows, :], i), lane),
        wide_shifts(warm(2 * k + y, r), side_of(side_warm[rows, :], i), lane),
        lambda d: field(4 * k + y, r + d),
        lambda d: warm(2 * k + y, r + d),
        field(4 * k + 1 - y, r),
        warm(2 * k + 1 - y, r),
    )
    for c in range(2):
        am[4 * k + 2 * c + y, to : to + 8, :] = got[c]


def middle(coef, am, pa, aw, tm, tw, k, y, r, here, lane):
    i, rows = 8 * y + k, slice(r, r + 8)
    main = [am[4 * k + 2 * c + y, rows, :] for c in range(2)]
    main.append(coef(y, here) * main[0] + coef(2 + y, here) * main[1])
    tm[2 * k + y, rows, :] = main[2]
    block = lane < 4
    aw[2 * k + y, rows, :] = jnp.where(block, side_of(pa[0, rows, :], i), main[0])
    tw[2 * k + y, rows, :] = jnp.where(block, side_of(pa[2, rows, :], i), main[2])


def second_rate(speed, am, pa, aw, tm, tw, ad, bd, k, y, r, to, lane):
    i, rows, dest = 8 * y + k, slice(r, r + 8), slice(to, to + 8)
    main = [am[4 * k + y, rows, :], am[4 * k + 2 + y, rows, :], tm[2 * k + y, rows, :]]
    side = [side_of(pa[n, rows, :], i) for n in range(3)]
    got = rate(
        speed * (-1.0 / 12.0),
        *(block_shifts(main[n], side[n], lane) for n in range(3)),
        lambda d: aw[2 * k + y, r + d : r + d + 8, :],
        lambda d: tw[2 * k + y, r + d : r + d + 8, :],
        aw[2 * k + 1 - y, rows, :],
        tw[2 * k + 1 - y, rows, :],
    )
    for c in range(2):
        bd[4 * k + 2 * c + y, dest, :] = 0.5 * got[c]
    ad[4 * k + y, dest, :] = aw[2 * k + y, rows, :]
    ad[4 * k + 2 + y, dest, :] = jnp.where(lane < 4, side[1], main[1])


def each():
    return [(k, y) for k in range(K) for y in range(2)]


def inner_kernel(
    q_ref, coef_ref, warm_ref, side_ref, last_ref, own_ref,
    ad_ref, bd_ref, tail_ref, packed_ref, sums_ref,
    pc, pt, pa, am, aw, tm, tw, qd, red,
):
    lane = lanes()
    block = lane < 4
    clear(red, 4)
    for t in range(Z // 8):
        for n in range(3):
            pc[n, tile(t), :] = spread(side_ref[2, tile(t), :], lane, n)
        pt[tile(t), :] = (
            pc[0, tile(t), :] * side_ref[0, tile(t), :] + pc[1, tile(t), :] * side_ref[1, tile(t), :]
        )
    for k, y in each():
        for c in range(2):
            for t in range(3):
                rows = slice(8 * t + 4, 8 * t + 12)
                f = 4 * k + 2 * c + y
                part = side_of(side_ref[c, rows, :], 8 * y + k)
                qd[f, tile(t), :] = jnp.where(block, part, q_ref[f, rows, :])

    def field(f, r):
        return q_ref[f, r : r + 8, :]

    def coef(f, r):
        return coef_ref[f, r : r + 8, :]

    def warm(f, r):
        return warm_ref[f, r : r + 8, :]

    starts = (2, 10, 18, 22)
    for r in starts:
        packed_rate(side_ref, last_ref, pt, pc, pa, r, r, lane)
    for k, y in each():
        for r in starts:
            first_rate(field, coef, warm, side_ref, pt, am, k, y, r, r, lane)
    for k, y in each():
        for r in starts:
            middle(coef, am, pa, aw, tm, tw, k, y, r, r, lane)
    for y in range(2):
        for t in range(3):
            r = 8 * t + 4
            side = side_of(side_ref[2, r : r + 8, :], 4 + y)
            speed = jnp.where(block, side, coef(4 + y, r))
            for k in range(K):
                second_rate(
                    speed, am, pa, aw, tm, tw, ad_ref, bd_ref, k, y, r, 8 * t, lane
                )
    for f in range(NF):
        tail_ref[f] = am[f, 22:30, :]
    for n in range(3):
        packed_ref[n] = pa[n, 22:30, :]
        packed_ref[3 + n] = pc[n, 24:32, :]
    cross_sums(red, qd, ad_ref, bd_ref, 3)
    sums_ref[...] = columns(own_ref[...], lane, red, range(1, 5))


def edge_kernel(
    q_ref, coef_ref, warm_ref, side_ref, last_ref, below_ref, corner_ref, tail_ref, packed_ref,
    inner_ref, ad_ref, bd_ref, sums_ref,
    em, wm, sm, lm, pc, pt, pa, am, aw, tm, tw, qd, red,
):
    lane = lanes()
    block = lane < 4
    group = lane >> 3
    clear(red, 4)
    for f in range(NA):
        em[f, 0:8, :] = q_ref[f, 24:32, :] if f < NF else coef_ref[f - NF, 24:32, :]
        em[f, 8:16, :] = below_ref[f]
    for n in range(3):
        sm[n, 0:8, :] = side_ref[n, 24:32, :]
        sm[n, 8:16, :] = corner_ref[n]
        lm[n, 0:8, :] = last_ref[n, 24:32, :]
        pc[n, 0:8, :] = packed_ref[3 + n]
        pc[n, 8:16, :] = spread(corner_ref[2], lane, n)
        pa[n, 0:8, :] = packed_ref[n]
    last = [None] * 3
    for y in range(2):
        for k in range(K):
            i = 8 * y + k
            fields = [below_ref[4 * k + 2 * c + y] for c in range(2)]
            fields.append(
                below_ref[NF + y] * fields[0] + below_ref[NF + 2 + y] * fields[1]
            )
            wm[2 * k + y, 0:8, :] = warm_ref[2 * k + y, 24:32, :]
            wm[2 * k + y, 8:16, :] = fields[2]
            for n in range(3):
                part = pltpu.roll(fields[n], (8 * i + 8) % X, 1) if i < 15 else fields[n]
                last[n] = part if i == 0 else jnp.where(group == i, part, last[n])
    for n in range(3):
        lm[n, 8:16, :] = last[n]
    for t in range(2):
        pt[tile(t), :] = pc[0, tile(t), :] * sm[0, tile(t), :] + pc[1, tile(t), :] * sm[1, tile(t), :]
    for f in range(NF):
        am[f, 0:8, :] = tail_ref[f]

    def field(f, r):
        return em[f, r : r + 8, :]

    def coef(f, r):
        return em[NF + f, r : r + 8, :]

    def warm(f, r):
        return wm[f, r : r + 8, :]

    packed_rate(sm, lm, pt, pc, pa, 6, 8, lane)
    for k, y in each():
        for c in range(2):
            f = 4 * k + 2 * c + y
            part = side_of(sm[c, 4:12, :], 8 * y + k)
            qd[f] = jnp.where(block, part, em[f, 4:12, :])
        first_rate(field, coef, warm, sm, pt, am, k, y, 6, 8, lane)
    for k, y in each():
        for r in (4, 8):
            middle(coef, am, pa, aw, tm, tw, k, y, r, r - 2, lane)
    for y in range(2):
        speed = jnp.where(block, side_of(sm[2, 4:12, :], 4 + y), coef(4 + y, 4))
        for k in range(K):
            second_rate(speed, am, pa, aw, tm, tw, ad_ref, bd_ref, k, y, 6, 0, lane)
    cross_sums(red, qd, ad_ref, bd_ref, 1)
    result = columns(jnp.zeros((8, X), F32), lane, red, range(1, 5)) + inner_ref[...]
    for n in range(sums_ref.shape[0]):
        sums_ref[n] = result


def give_kernel(ad_ref, bd_ref, ade_ref, bde_ref, out_ref):
    group = lanes() >> 2
    for n, (ref, edge) in enumerate(((ad_ref, ade_ref), (bd_ref, bde_ref))):
        for t in range(Z // 8):
            acc = jnp.zeros((8, X), F32)
            for f in range(NF):
                part = ref[f, tile(t), :] if t < 3 else edge[f]
                acc = jnp.where(group == f, pltpu.roll(part, 4 * f, 1) if f else part, acc)
            out_ref[n, tile(t), :] = acc


def place_kernel(ad_ref, bd_ref, ade_ref, bde_ref, got_ref, a_ref, b_ref, down_ref):
    block = lanes() < 4
    for n, (ref, edge, out) in enumerate(((ad_ref, ade_ref, a_ref), (bd_ref, bde_ref, b_ref))):
        for f in range(NF):
            for t in range(Z // 8):
                part = ref[f, tile(t), :] if t < 3 else edge[f]
                got = got_ref[n, tile(t), :]
                got = pltpu.roll(got, X - 4 * f, 1) if f else got
                part = jnp.where(block, got, part)
                if t < 3:
                    out[f, 8 * t + 4 : 8 * t + 12, :] = part
                else:
                    out[f, 28:32, :] = part[0:4, :]
                    out[f, 0:4, :] = jnp.zeros((4, X), F32)
                    r = 4 * (NF * n + f)
                    down_ref[r : r + 4, :] = part[4:8, :]


def finish_kernel(cells, q_ref, a_ref, b_ref, above_ref, sums_ref, out_ref, growth_ref, first):
    lane = lanes()
    row = lax.broadcasted_iota(jnp.int32, (8, X), 0)
    for n, ref in enumerate((a_ref, b_ref)):
        for f in range(NF):
            r = 4 * (NF * n + f)
            first[n, f, 0:4, :] = above_ref[r : r + 4, :]
            first[n, f, 4:8, :] = ref[f, 4:8, :]
    total = sums_ref[0]
    for n in range(1, sums_ref.shape[0]):
        total = total + sums_ref[n]
    speed = jnp.broadcast_to(jnp.sum(total[:, 40:41], axis=0, keepdims=True), (8, X))
    step = courant_number / jnp.sqrt(speed * (1.0 / cells) + 1e-05)
    gram = total
    power = step
    for n in range(1, 5):
        gram = gram + power * pltpu.roll(total, X - 8 * n, 1)
        power = power * step
    gram = gram * (1.0 / (2.0 * cells))
    cols = [jnp.broadcast_to(gram[:, m : m + 1], (8, X)) for m in range(5)]

    def entry(i, j):
        k, m = (j, i - j) if i - j <= 4 else (i, j - i + K)
        if m == 4:
            k = min(i, j)
        return jnp.broadcast_to(cols[m][k : k + 1, :], (8, X))

    low = [[None] * K for _ in range(K)]
    inv_diag = []
    for j in range(K):
        d = entry(j, j)
        for p in range(j):
            d = d - low[j][p] * low[j][p]
        root = jnp.sqrt(d)
        low[j][j] = root
        inv_diag.append(1.0 / root)
        for i in range(j + 1, K):
            v = entry(i, j)
            for p in range(j):
                v = v - low[i][p] * low[j][p]
            low[i][j] = v * inv_diag[j]
    inverse = [[None] * K for _ in range(K)]
    for j in range(K):
        inverse[j][j] = inv_diag[j]
        for i in range(j + 1, K):
            v = low[i][j] * inverse[j][j]
            for p in range(j + 1, i):
                v = v + low[i][p] * inverse[p][j]
            inverse[i][j] = -v * inv_diag[i]
    growth = jnp.zeros((8, X), F32)
    for i in range(K):
        for j in range(i + 1):
            growth = jnp.where((row == j) & (lane == i), low[i][j], growth)
    growth_ref[...] = growth
    square = step * step
    for p in range(4):
        for t in range(Z // 8):
            adv = []
            for k in range(K):
                f = 4 * k + p
                a, b = (
                    (first[0, f], first[1, f])
                    if t == 0
                    else (a_ref[f, tile(t), :], b_ref[f, tile(t), :])
                )
                adv.append(q_ref[f, tile(t), :] + step * a + square * b)
            for k in range(K):
                v = inverse[k][0] * adv[0]
                for j in range(1, k + 1):
                    v = v + inverse[k][j] * adv[j]
                out_ref[4 * k + p, tile(t), :] = v


def call(body, outs, scratch=(), cost=2000000, limit=24, **more):
    shapes = [jax.ShapeDtypeStruct(s, F32) for s in outs]
    return pl.pallas_call(
        body,
        out_shape=shapes,
        scratch_shapes=[pltpu.VMEM(s, F32) if isinstance(s, tuple) else s for s in scratch],
        compiler_params=pltpu.CompilerParams(vmem_limit_bytes=limit * 1024 * 1024),
        cost_estimate=pl.CostEstimate(flops=cost, bytes_accessed=cost, transcendentals=0),
        **more,
    )


def ring(array, axes, step):
    size = lax.axis_size(axes)
    return lax.ppermute(array, axes, [(i, (i + step) % size) for i in range(size)])


def gathered(array, axes):
    return lax.all_to_all(array, axes, 0, 0)


def per_device(tangents, mass, internal, velocity):
    cells = float(2 * Z * X * lax.axis_size(GX) * lax.axis_size(GZ))
    near, far = lax.axis_size(NEAR), lax.axis_size(FAR)
    whole, inner, edge = (NF, Z, X), (NF, 24, X), (NF, 8, X)
    half, small, red = (2 * K, Z, X), (3, Z, X), (20, 64, X)
    q = tangents.reshape(whole)
    coef, pack, rows = call(
        prep_kernel,
        [(NC, Z, X), small, (NA, 8, X)],
        [whole, (2, Z, X), (2, Z, X), pltpu.SemaphoreType.DMA((4,))],
        limit=60,
        in_specs=[pl.BlockSpec(memory_space=pl.ANY)] * 4,
    )(q, mass, internal, velocity)
    side = ring(pack, GX, -1)
    below = ring(rows, GZ, -1)
    warm, last, own = call(own_kernel, [half, small, (8, X)], [(5, 64, X)])(q, coef)
    side, warm, last, own = lax.optimization_barrier((side, warm, last, own))
    (corner,) = call(corner_kernel, [(3, 8, X)], cost=1000)(side)
    corner = ring(corner, GZ, -1)
    ad, bd, tail, packed, part = call(
        inner_kernel,
        [inner, inner, edge, (6, 8, X), (8, X)],
        [small, (Z, X), small, whole, half, half, half, inner, red],
    )(q, coef, warm, side, last, own)
    low, slim = (2 * K, 16, X), (3, 16, X)
    ade, bde, sums = call(
        edge_kernel,
        [edge, edge, (far, 8, X)],
        [(NA, 16, X), low, slim, slim, slim, (16, X), slim, (NF, 16, X), low, low, low, edge, red],
    )(q, coef, warm, side, last, below, corner, tail, packed, part)
    sums = jnp.sum(gathered(sums, FAR), axis=0)
    (give,) = call(give_kernel, [(2, Z, X)])(ad, bd, ade, bde)
    got = ring(give, GX, 1)
    a, b, down = call(place_kernel, [whole, whole, (8 * NF, X)])(ad, bd, ade, bde, got)
    above = ring(down, GZ, 1)
    sums = gathered(jnp.broadcast_to(sums, (near, 8, X)), NEAR)
    out, growth = call(
        functools.partial(finish_kernel, cells), [whole, (8, X)], [(2, NF, 8, X)]
    )(q, a, b, above, sums)
    return (out.reshape(tangents.shape), growth[:, :K])


def solution(mesh):
    gx, gz = mesh.devices.shape
    fine = Mesh(mesh.devices.reshape(gx // 4, 4, gz // 4, 4), GX + GZ)
    in_specs = (P(None, None, None, GZ, GX),) + (P(None, GZ, GX),) * 3
    out_specs = (P(None, None, None, GZ, GX), P())
    return jax.shard_map(
        per_device, mesh=fine, in_specs=in_specs, out_specs=out_specs, check_vma=False
    )
```

```python
import functools

import jax
import jax.numpy as jnp
import numpy as np
from jax import lax
from jax.experimental import pallas as pl
from jax.experimental.pallas import tpu as pltpu
from jax.sharding import Mesh, PartitionSpec as P

NEWTON = 4
isochoric_warmth_coefficient = 3.0
attraction = 0.5
acentric_coefficient_gradient = 0.6
covolume = 0.15
root_two = 1.4142135623730951
viscosity = 0.2
conductivity = 1.0
courant_number = 0.5

K = 8
NF = 4 * K
NC = 6
NA = NF + NC
Z = 32
X = 128
GX = ("xh", "xl")
GZ = ("zh", "zl")
NEAR = ("xl", "zl")
FAR = ("xh", "zh")
F32 = jnp.float32


def bands():
    first = {-2: 1.0, -1: -8.0, 1: 8.0, 2: -1.0}
    second = {-2: -1.0, -1: 16.0, 0: -30.0, 1: 16.0, 2: -1.0}
    main, packed = [], []
    for band in (first, second):
        w, v = np.zeros((X, X), np.float32), np.zeros((2 * X, 2 * X), np.float32)
        for d, value in band.items():
            for j in range(X):
                if 0 <= j + d < X:
                    w[j + d, j] = value
            for g in range(16):
                for j in range(16):
                    if 0 <= j + d < 16:
                        at = [X * (c // 8) + 8 * g + c % 8 for c in (j + d, j)]
                        v[at[0], at[1]] = value
        main.append(np.concatenate([w, w]))
        packed.append(v)
    return [
        np.concatenate(main, axis=1).astype(jnp.bfloat16),
        np.stack(packed).astype(jnp.bfloat16),
    ]


def departure(cell_mass_concentration):
    low_term = 1.0 + (1.0 - root_two) * covolume * cell_mass_concentration
    high_term = 1.0 + (1.0 + root_two) * covolume * cell_mass_concentration
    factor = attraction * (1.0 + acentric_coefficient_gradient) / (2.0 * root_two * covolume)
    value = factor * (jnp.log(low_term) - jnp.log(high_term))
    slope = factor * (
        (1.0 - root_two) * covolume / low_term - (1.0 + root_two) * covolume / high_term
    )
    return (value, slope)


def slopes(mass, internal):
    deviation, departure_slope = departure(mass)
    warmth = internal / isochoric_warmth_coefficient
    for _ in range(NEWTON):
        root = jnp.sqrt(warmth)
        multiplier = 1.0 + acentric_coefficient_gradient * (1.0 - root)
        mismatch = isochoric_warmth_coefficient * warmth + deviation * multiplier - internal
        gradient = isochoric_warmth_coefficient - deviation * acentric_coefficient_gradient / (
            2.0 * root
        )
        warmth = warmth - mismatch / gradient
    root = jnp.sqrt(warmth)
    multiplier = 1.0 + acentric_coefficient_gradient * (1.0 - root)
    gradient = isochoric_warmth_coefficient - deviation * acentric_coefficient_gradient / (
        2.0 * root
    )
    energy = 1.0 / gradient
    return (-departure_slope * multiplier * energy, energy)


def lanes():
    return lax.broadcasted_iota(jnp.int32, (8, X), 1)


def tile(t):
    return slice(8 * t, 8 * t + 8)


def prep_kernel(
    q_hbm, mass_hbm, internal_hbm, velocity_hbm, coef_ref, pack_ref, q, mass, internal, sems
):
    copies = [
        pltpu.make_async_copy(src, dst, sems.at[i])
        for i, (src, dst) in enumerate(
            (
                (mass_hbm, mass),
                (internal_hbm, internal),
                (velocity_hbm, coef_ref.at[pl.ds(4, 2)]),
                (q_hbm, q),
            )
        )
    ]
    for copy in copies:
        copy.start()
    copies[0].wait()
    copies[1].wait()
    density, energy = slopes(mass[...], internal[...])
    coef_ref[0:2] = density
    coef_ref[2:4] = energy
    copies[2].wait()
    copies[3].wait()
    group = lanes() >> 3
    for t in range(Z // 8):
        for c in range(2):
            acc = q[2 * c, tile(t), :]
            for y in range(2):
                for k in range(K):
                    i = 8 * y + k
                    if i:
                        part = pltpu.roll(q[4 * k + 2 * c + y, tile(t), :], 8 * i, 1)
                        acc = jnp.where(group == i, part, acc)
            pack_ref[c, tile(t), :] = acc
        acc = jnp.where(group == 0, coef_ref[0, tile(t), :], 0.0)
        for i in range(1, NC):
            acc = jnp.where(group == i, pltpu.roll(coef_ref[i, tile(t), :], 8 * i, 1), acc)
        pack_ref[2, tile(t), :] = acc


def rows_kernel(q_ref, rows_ref):
    for f in range(NF):
        rows_ref[f] = q_ref[f, 0:8, :]


def pairs():
    return [(k, m, (k + m) % K) for k in range(K) for m in range(5 if k < 4 else 4)]


def columns(result, lane, red, extra, sets):
    row = lax.broadcasted_iota(jnp.int32, (8, X), 0)
    mine = ((lane >> 3) & 7) == row
    for n, place in enumerate(sets):
        for m in range(5):
            acc = red[5 * n + m]
            if extra is not None:
                part = extra[5 * n + m]
                for d in (4, 2, 1):
                    part = part + pltpu.roll(part, d, 0)
                if m == 4:
                    acc = jnp.where(row < 4, acc + jnp.where(mine, part, 0.0), 0.0)
                else:
                    acc = acc + jnp.where(mine, part, 0.0)
            col = jnp.sum(acc, axis=1, keepdims=True)
            result = jnp.where(lane == 8 * place + m, col, result)
    return result


def put(red, n, k, acc):
    red[n, k : k + 1, :] = jnp.sum(acc, axis=0, keepdims=True)


def side_of(packed, i):
    return pltpu.roll(packed, X - 8 * i, 1) if i else packed


def fill(pair, lane):
    out = jnp.where(lane < 8, pair[0], 0.0)
    out = jnp.where((lane >= 64) & (lane < 72), pltpu.roll(pair[1], 64, 1), out)
    for d in (8, 16, 32):
        out = out + pltpu.roll(out, d, 1)
    return out


def own_kernel(q_ref, coef_ref, warm_ref, last_ref, sums_ref, red):
    lane = lanes()
    red[...] = jnp.zeros_like(red)
    group = lane >> 3
    for t in range(Z // 8):
        last = [None] * 3
        for y in range(2):
            for k in range(K):
                i = 8 * y + k
                fields = [q_ref[4 * k + 2 * c + y, tile(t), :] for c in range(2)]
                fields.append(
                    coef_ref[y, tile(t), :] * fields[0] + coef_ref[2 + y, tile(t), :] * fields[1]
                )
                warm_ref[2 * k + y, tile(t), :] = fields[2]
                for n in range(2):
                    part = pltpu.roll(fields[n], (8 * i + 8) % X, 1) if i < 15 else fields[n]
                    last[n] = part if i == 0 else jnp.where(group == i, part, last[n])
        full = [
            fill([pltpu.roll(coef_ref[2 * n + y, tile(t), :], 8, 1) for y in range(2)], lane)
            for n in range(3)
        ]
        last[2] = full[0] * last[0] + full[1] * last[1]
        for n in range(3):
            last_ref[n, tile(t), :] = last[n]
            last_ref[3 + n, tile(t), :] = full[n]
    for k, m, l in pairs():
        acc = jnp.zeros((8, X), F32)
        for p in range(4):
            for t in range(Z // 8):
                acc = acc + q_ref[4 * k + p, tile(t), :] * q_ref[4 * l + p, tile(t), :]
        put(red, m, k, acc)
    speed = jnp.zeros((8, X), F32)
    for y in range(2):
        for t in range(Z // 8):
            v = coef_ref[4 + y, tile(t), :]
            speed = speed + v * v
    result = jnp.where(lane == 40, jnp.sum(speed, axis=1, keepdims=True), 0.0)
    sums_ref[...] = columns(result, lane, red, None, (0,))


def join(side_ref, last_ref, packed, t, at, lane):
    rows = slice(at, at + 8)
    got = [side_ref[c, tile(t), :] for c in range(2)]
    third = side_ref[2, tile(t), :]
    full = [fill([side_of(third, 2 * n + y) for y in range(2)], lane) for n in range(3)]
    got.append(full[0] * got[0] + full[1] * got[1])
    for n, part in enumerate(got + full):
        packed[n, rows, 0:X] = last_ref[n, tile(t), :]
        packed[n, rows, X : 2 * X] = part


def corner_kernel(side_ref, last_ref, coef_ref, corner_ref, packed):
    join(side_ref, last_ref, packed, 0, 0, lanes())
    for n in range(6):
        corner_ref[n] = packed[n, :, 0:X]
        corner_ref[6 + n] = packed[n, :, X : 2 * X]
        corner_ref[12 + n] = coef_ref[n, 0:8, :]


def split(x):
    high = x.astype(jnp.bfloat16)
    return high, (x - high.astype(F32)).astype(jnp.bfloat16)


def product(x, w):
    return jnp.dot(x, w, preferred_element_type=F32)


def rest(at, other):
    return 16.0 * (at(-1) + at(1) + other) - (at(-2) + at(2)) - 60.0 * at(0)


def main_rate(speed, weights, r_at, e_at, t_at, r_other, t_other):
    both = product(jnp.concatenate(split(r_at(0)), axis=1), weights[...])
    slope = product(jnp.concatenate(split(e_at(0)), axis=1), weights[:, 0:X])
    bend = product(jnp.concatenate(split(t_at(0)), axis=1), weights[:, X : 2 * X])
    rate_r = speed * both[:, 0:X] + (viscosity / 12.0) * (both[:, X:] + rest(r_at, r_other))
    rate_e = speed * slope + (conductivity / 12.0) * (bend + rest(t_at, t_other))
    return rate_r, rate_e


def turned(x):
    return jnp.concatenate([pltpu.roll(x[:, 0:X], 64, 1), pltpu.roll(x[:, X:], 64, 1)], axis=1)


def packed_rate(speed, weights, at):
    def along(n, w):
        high, low = split(at(n, 0))
        return product(high, weights[w]) + product(low, weights[w])

    rate_r = speed * along(0, 0) + (viscosity / 12.0) * (
        along(0, 1) + rest(lambda d: at(0, d), turned(at(0, 0)))
    )
    rate_e = speed * along(1, 0) + (conductivity / 12.0) * (
        along(2, 1) + rest(lambda d: at(2, d), turned(at(2, 0)))
    )
    return rate_r, rate_e


def packed_steps(packed, wp, pa, blocks, first, second, count, lane):
    src, dst, height = first
    rows = slice(src, src + height)
    got = packed_rate(
        packed[5, rows, :] * (-1.0 / 12.0), wp, lambda n, d: packed[n, src + d : src + d + height, :]
    )
    out = slice(dst, dst + height)
    pa[0, out, :] = got[0]
    pa[1, out, :] = got[1]
    pa[2, out, :] = packed[3, rows, :] * got[0] + packed[4, rows, :] * got[1]
    here, there = second
    rows = slice(here, here + count)
    got = packed_rate(
        packed[5, rows, :] * (-1.0 / 12.0),
        wp,
        lambda n, d: pa[n, there + d : there + d + count, :],
    )
    qp, ap, bp = blocks
    low = (lax.broadcasted_iota(jnp.int32, (count, X), 1) & 7) < 4
    for c in range(2):
        for dest, value in (
            (qp, packed[c, rows, :]),
            (ap, pa[c, there : there + count, :]),
            (bp, 0.5 * got[c]),
        ):
            dest[c] = jnp.where(low, value[:, X:], value[:, 0:X])


def main_sums(red, q_at, ad, bd, tiles):
    for k, m, l in pairs():
        acc = [jnp.zeros((8, X), F32)] * 4
        for p in range(4):
            for t in range(tiles):
                qk, ql = q_at(4 * k + p, t), q_at(4 * l + p, t)
                ak, bk = (v[4 * k + p, tile(t), :] for v in (ad, bd))
                al, bl = (v[4 * l + p, tile(t), :] for v in (ad, bd))
                acc[0] = acc[0] + (qk * al + ak * ql)
                acc[1] = acc[1] + (ak * al + (qk * bl + bk * ql))
                acc[2] = acc[2] + (ak * bl + bk * al)
                acc[3] = acc[3] + bk * bl
        for n in range(4):
            put(red, 5 * n + m, k, acc[n])


def packed_sums(extra, blocks, tiles, lane):
    acc = [jnp.zeros((8, X), F32) for _ in range(20)]
    for c in range(2):
        for t in range(tiles):
            q, a, b = (ref[c, tile(t), :] for ref in blocks)
            for m in range(5):

                def other(v, m=m):
                    if m == 0:
                        return v
                    near = pltpu.roll(v, X - 8 * m, 1)
                    return jnp.where((lane & 63) < 64 - 8 * m, near, pltpu.roll(v, 64 - 8 * m, 1))

                ql, al, bl = other(q), other(a), other(b)
                acc[m] = acc[m] + (q * al + a * ql)
                acc[5 + m] = acc[5 + m] + (a * al + (q * bl + b * ql))
                acc[10 + m] = acc[10 + m] + (a * bl + b * al)
                acc[15 + m] = acc[15 + m] + b * bl
    for n in range(20):
        extra[n] = acc[n]


def inside(rows):
    lane = lax.broadcasted_iota(jnp.int32, (rows, X), 1)
    return (lane >= 4) & (lane < 124)


def inner_kernel(
    q_ref, coef_ref, warm_ref, side_ref, last_ref, own_ref, wm_ref, wp_ref,
    ad_ref, bd_ref, ap_ref, bp_ref, tail_ref, packed_ref, sums_ref,
    packed, pa, qp, am, tm, red, extra,
):
    lane = lanes()
    red[...] = jnp.zeros_like(red)
    for t in range(Z // 8):
        join(side_ref, last_ref, packed, t, 8 * t, lane)
    packed_steps(packed, wp_ref, pa, (qp, ap_ref, bp_ref), (2, 2, 28), (4, 4), 24, lane)
    packed_sums(extra, (qp, ap_ref, bp_ref), 3, lane)
    for n in range(3):
        packed_ref[n] = pa[n, 22:30, :]
    for n in range(6):
        packed_ref[3 + n] = packed[n, 24:32, :]
    keep = inside(24)

    def vector(k, carry):
        base = 4 * k
        for y in range(2):
            got = main_rate(
                coef_ref[4 + y, 2:30, :] * (-1.0 / 12.0),
                wm_ref,
                lambda d: q_ref[base + y, 2 + d : 30 + d, :],
                lambda d: q_ref[base + 2 + y, 2 + d : 30 + d, :],
                lambda d: warm_ref[2 * k + y, 2 + d : 30 + d, :],
                q_ref[base + 1 - y, 2:30, :],
                warm_ref[2 * k + 1 - y, 2:30, :],
            )
            for c in range(2):
                am[k, 2 * c + y, 2:30, :] = got[c]
            tm[k, y, 2:30, :] = coef_ref[y, 2:30, :] * got[0] + coef_ref[2 + y, 2:30, :] * got[1]
        for y in range(2):
            got = main_rate(
                coef_ref[4 + y, 4:28, :] * (-1.0 / 12.0),
                wm_ref,
                lambda d: am[k, y, 4 + d : 28 + d, :],
                lambda d: am[k, 2 + y, 4 + d : 28 + d, :],
                lambda d: tm[k, y, 4 + d : 28 + d, :],
                am[k, 1 - y, 4:28, :],
                tm[k, 1 - y, 4:28, :],
            )
            for c in range(2):
                i = base + 2 * c + y
                bd_ref[i] = jnp.where(keep, 0.5 * got[c], 0.0)
                ad_ref[i] = jnp.where(keep, am[k, 2 * c + y, 4:28, :], 0.0)
        for p in range(4):
            tail_ref[base + p] = am[k, p, 22:30, :]
        return carry

    lax.fori_loop(0, K, vector, 0)
    main_sums(red, lambda f, t: q_ref[f, 8 * t + 4 : 8 * t + 12, :], ad_ref, bd_ref, 3)
    sums_ref[...] = columns(own_ref[...], lane, red, extra, range(1, 5))


def edge_kernel(
    q_ref, coef_ref, warm_ref, below_ref, corner_ref, tail_ref, packed_ref, inner_ref, wm_ref, wp_ref,
    ad_ref, bd_ref, ap_ref, bp_ref, sums_ref,
    em, ec, wm, packed, pa, qp, am, tm, red, extra,
):
    lane = lanes()
    red[...] = jnp.zeros_like(red)
    for n in range(NC):
        ec[n, 0:8, :] = coef_ref[n, 24:32, :]
        ec[n, 8:16, :] = corner_ref[12 + n]
        packed[n, 0:8, :] = packed_ref[3 + n]
        packed[n, 8:16, 0:X] = corner_ref[n]
        packed[n, 8:16, X : 2 * X] = corner_ref[6 + n]
    for n in range(3):
        pa[n, 0:8, :] = packed_ref[n]
    packed_steps(packed, wp_ref, pa, (qp, ap_ref, bp_ref), (6, 8, 8), (4, 6), 8, lane)
    packed_sums(extra, (qp, ap_ref, bp_ref), 1, lane)
    keep = inside(8)

    def vector(k, carry):
        base = 4 * k
        for p in range(4):
            em[base + p, 0:8, :] = q_ref[base + p, 24:32, :]
            em[base + p, 8:16, :] = below_ref[base + p]
            am[k, p, 0:8, :] = tail_ref[base + p]
        for y in range(2):
            wm[k, y, 0:8, :] = warm_ref[2 * k + y, 24:32, :]
            wm[k, y, 8:16, :] = (
                ec[y, 8:16, :] * below_ref[base + y] + ec[2 + y, 8:16, :] * below_ref[base + 2 + y]
            )
        for y in range(2):
            got = main_rate(
                ec[4 + y, 6:14, :] * (-1.0 / 12.0),
                wm_ref,
                lambda d: em[base + y, 6 + d : 14 + d, :],
                lambda d: em[base + 2 + y, 6 + d : 14 + d, :],
                lambda d: wm[k, y, 6 + d : 14 + d, :],
                em[base + 1 - y, 6:14, :],
                wm[k, 1 - y, 6:14, :],
            )
            for c in range(2):
                am[k, 2 * c + y, 8:16, :] = got[c]
            tm[k, y, 8:16, :] = ec[y, 6:14, :] * got[0] + ec[2 + y, 6:14, :] * got[1]
            tm[k, y, 4:8, :] = (
                ec[y, 2:6, :] * am[k, y, 4:8, :] + ec[2 + y, 2:6, :] * am[k, 2 + y, 4:8, :]
            )
        for y in range(2):
            got = main_rate(
                ec[4 + y, 4:12, :] * (-1.0 / 12.0),
                wm_ref,
                lambda d: am[k, y, 6 + d : 14 + d, :],
                lambda d: am[k, 2 + y, 6 + d : 14 + d, :],
                lambda d: tm[k, y, 6 + d : 14 + d, :],
                am[k, 1 - y, 6:14, :],
                tm[k, 1 - y, 6:14, :],
            )
            for c in range(2):
                i = base + 2 * c + y
                bd_ref[i] = jnp.where(keep, 0.5 * got[c], 0.0)
                ad_ref[i] = jnp.where(keep, am[k, 2 * c + y, 6:14, :], 0.0)
        return carry

    lax.fori_loop(0, K, vector, 0)
    main_sums(red, lambda f, t: em[f, 4:12, :], ad_ref, bd_ref, 1)
    result = columns(jnp.zeros((8, X), F32), lane, red, extra, range(1, 5)) + inner_ref[...]
    for n in range(sums_ref.shape[0]):
        sums_ref[n] = result


def give_kernel(ap_ref, bp_ref, ape_ref, bpe_ref, out_ref):
    for n, (ref, edge) in enumerate(((ap_ref, ape_ref), (bp_ref, bpe_ref))):
        for c in range(2):
            out_ref[n, c, 0:24, :] = ref[c]
            out_ref[n, c, 24:32, :] = edge[c]


def place_kernel(ad_ref, bd_ref, ade_ref, bde_ref, mine_ref, got_ref, a_ref, b_ref, down_ref):
    lane = lanes()
    strip = (lane < 4) | (lane >= 124)
    low = (lane & 7) < 4
    for n, (ref, edge, out) in enumerate(((ad_ref, ade_ref, a_ref), (bd_ref, bde_ref, b_ref))):
        for c in range(2):
            for t in range(Z // 8):
                mine = pltpu.roll(mine_ref[n, c, tile(t), :], X - 8, 1)
                both = jnp.where(low, got_ref[n, c, tile(t), :], mine)
                for y in range(2):
                    for k in range(K):
                        f = 4 * k + 2 * c + y
                        part = ref[f, tile(t), :] if t < 3 else edge[f]
                        part = jnp.where(strip, side_of(both, 8 * y + k), part)
                        if t < 3:
                            out[f, 8 * t + 4 : 8 * t + 12, :] = part
                        else:
                            out[f, 28:32, :] = part[0:4, :]
                            out[f, 0:4, :] = jnp.zeros((4, X), F32)
                            r = 4 * (NF * n + f)
                            down_ref[r : r + 4, :] = part[4:8, :]


def finish_kernel(cells, q_ref, a_ref, b_ref, above_ref, sums_ref, out_ref, growth_ref, first):
    lane = lanes()
    row = lax.broadcasted_iota(jnp.int32, (8, X), 0)
    for n, ref in enumerate((a_ref, b_ref)):
        for f in range(NF):
            r = 4 * (NF * n + f)
            first[n, f, 0:4, :] = above_ref[r : r + 4, :]
            first[n, f, 4:8, :] = ref[f, 4:8, :]
    total = sums_ref[0]
    for n in range(1, sums_ref.shape[0]):
        total = total + sums_ref[n]
    speed = jnp.broadcast_to(jnp.sum(total[:, 40:41], axis=0, keepdims=True), (8, X))
    step = courant_number / jnp.sqrt(speed * (1.0 / cells) + 1e-05)
    gram = total
    power = step
    for n in range(1, 5):
        gram = gram + power * pltpu.roll(total, X - 8 * n, 1)
        power = power * step
    gram = gram * (1.0 / (2.0 * cells))
    cols = [jnp.broadcast_to(gram[:, m : m + 1], (8, X)) for m in range(5)]

    def entry(i, j):
        k, m = (j, i - j) if i - j <= 4 else (i, j - i + K)
        if m == 4:
            k = min(i, j)
        return jnp.broadcast_to(cols[m][k : k + 1, :], (8, X))

    low = [[None] * K for _ in range(K)]
    inv_diag = []
    for j in range(K):
        d = entry(j, j)
        for p in range(j):
            d = d - low[j][p] * low[j][p]
        root = jnp.sqrt(d)
        low[j][j] = root
        inv_diag.append(1.0 / root)
        for i in range(j + 1, K):
            v = entry(i, j)
            for p in range(j):
                v = v - low[i][p] * low[j][p]
            low[i][j] = v * inv_diag[j]
    inverse = [[None] * K for _ in range(K)]
    for j in range(K):
        inverse[j][j] = inv_diag[j]
        for i in range(j + 1, K):
            v = low[i][j] * inverse[j][j]
            for p in range(j + 1, i):
                v = v + low[i][p] * inverse[p][j]
            inverse[i][j] = -v * inv_diag[i]
    growth = jnp.zeros((8, X), F32)
    for i in range(K):
        for j in range(i + 1):
            growth = jnp.where((row == j) & (lane == i), low[i][j], growth)
    growth_ref[...] = growth
    square = step * step
    for p in range(4):
        for t in range(Z // 8):
            adv = []
            for k in range(K):
                f = 4 * k + p
                a, b = (
                    (first[0, f], first[1, f])
                    if t == 0
                    else (a_ref[f, tile(t), :], b_ref[f, tile(t), :])
                )
                adv.append(q_ref[f, tile(t), :] + step * a + square * b)
            for k in range(K):
                v = inverse[k][0] * adv[0]
                for j in range(1, k + 1):
                    v = v + inverse[k][j] * adv[j]
                out_ref[4 * k + p, tile(t), :] = v


def call(body, outs, scratch=(), cost=2000000, limit=24, **more):
    shapes = [jax.ShapeDtypeStruct(s, F32) for s in outs]
    return pl.pallas_call(
        body,
        out_shape=shapes,
        scratch_shapes=[pltpu.VMEM(s, F32) if isinstance(s, tuple) else s for s in scratch],
        compiler_params=pltpu.CompilerParams(vmem_limit_bytes=limit * 1024 * 1024),
        cost_estimate=pl.CostEstimate(flops=cost, bytes_accessed=cost, transcendentals=0),
        **more,
    )


def ring(array, axes, step):
    size = lax.axis_size(axes)
    return lax.ppermute(array, axes, [(i, (i + step) % size) for i in range(size)])


def gathered(array, axes):
    return lax.all_to_all(array, axes, 0, 0)


def per_device(tangents, mass, internal, velocity):
    cells = float(2 * Z * X * lax.axis_size(GX) * lax.axis_size(GZ))
    near, far = lax.axis_size(NEAR), lax.axis_size(FAR)
    whole, inner, edge = (NF, Z, X), (NF, 24, X), (NF, 8, X)
    half, small, red = (2 * K, Z, X), (3, Z, X), (20, 8, X)
    wm, wp = (jnp.asarray(w) for w in bands())
    q = tangents.reshape(whole)
    coef, pack = call(
        prep_kernel,
        [(NC, Z, X), small],
        [whole, (2, Z, X), (2, Z, X), pltpu.SemaphoreType.DMA((4,))],
        limit=60,
        in_specs=[pl.BlockSpec(memory_space=pl.ANY)] * 4,
    )(q, mass, internal, velocity)
    side = ring(pack, GX, -1)
    later, _ = lax.optimization_barrier((q, pack))
    (rows,) = call(rows_kernel, [edge], cost=1000)(later)
    below = ring(rows, GZ, -1)
    warm, last, own = call(own_kernel, [half, (6, Z, X), (8, X)], [(5, 8, X)])(q, coef)
    side, warm, last, own = lax.optimization_barrier((side, warm, last, own))
    (corner,) = call(corner_kernel, [(18, 8, X)], [(6, 8, 2 * X)], cost=1000)(side, last, coef)
    corner = ring(corner, GZ, -1)
    ad, bd, ap, bp, tail, packed, part = call(
        inner_kernel,
        [inner, inner, (2, 24, X), (2, 24, X), edge, (9, 8, 2 * X), (8, X)],
        [(6, Z, 2 * X), (3, Z, 2 * X), (2, 24, X), (K, 4, Z, X), (K, 2, Z, X), red, red],
    )(q, coef, warm, side, last, own, wm, wp)
    ade, bde, ape, bpe, sums = call(
        edge_kernel,
        [edge, edge, (2, 8, X), (2, 8, X), (far, 8, X)],
        [(NF, 16, X), (NC, 16, X), (K, 2, 16, X), (6, 16, 2 * X), (3, 16, 2 * X), (2, 8, X)]
        + [(K, 4, 16, X), (K, 2, 16, X), red, red],
    )(q, coef, warm, below, corner, tail, packed, part, wm, wp)
    sums = jnp.sum(gathered(sums, FAR), axis=0)
    (give,) = call(give_kernel, [(2, 2, Z, X)])(ap, bp, ape, bpe)
    got = ring(give, GX, 1)
    a, b, down = call(place_kernel, [whole, whole, (8 * NF, X)])(ad, bd, ade, bde, give, got)
    above = ring(down, GZ, 1)
    sums = gathered(jnp.broadcast_to(sums, (near, 8, X)), NEAR)
    out, growth = call(
        functools.partial(finish_kernel, cells), [whole, (8, X)], [(2, NF, 8, X)]
    )(q, a, b, above, sums)
    return (out.reshape(tangents.shape), growth[:, :K])


def solution(mesh):
    gx, gz = mesh.devices.shape
    fine = Mesh(mesh.devices.reshape(gx // 4, 4, gz // 4, 4), GX + GZ)
    in_specs = (P(None, None, None, GZ, GX),) + (P(None, GZ, GX),) * 3
    out_specs = (P(None, None, None, GZ, GX), P())
    return jax.shard_map(
        per_device, mesh=fine, in_specs=in_specs, out_specs=out_specs, check_vma=False
    )
```

```python
import functools

import jax
import jax.numpy as jnp
import numpy as np
from jax import lax
from jax.experimental import pallas as pl
from jax.experimental.pallas import tpu as pltpu
from jax.sharding import Mesh, PartitionSpec as P

NEWTON = 4
isochoric_warmth_coefficient = 3.0
attraction = 0.5
acentric_coefficient_gradient = 0.6
covolume = 0.15
root_two = 1.4142135623730951
viscosity = 0.2
conductivity = 1.0
courant_number = 0.5

K = 8
NF = 4 * K
NC = 6
NA = NF + NC
Z = 32
X = 128
GX = ("xh", "xl")
GZ = ("zh", "zl")
NEAR = ("xl", "zl")
FAR = ("xh", "zh")
F32 = jnp.float32
STEP = 4


def bands():
    first = {-2: 1.0, -1: -8.0, 1: 8.0, 2: -1.0}
    second = {-2: -1.0, -1: 16.0, 0: -30.0, 1: 16.0, 2: -1.0}
    main, packed = [], []
    for band in (first, second):
        w, v = np.zeros((X, X), np.float32), np.zeros((2 * X, 2 * X), np.float32)
        for d, value in band.items():
            for j in range(X):
                if 0 <= j + d < X:
                    w[j + d, j] = value
            for g in range(16):
                for j in range(16):
                    if 0 <= j + d < 16:
                        at = [X * (c // 8) + 8 * g + c % 8 for c in (j + d, j)]
                        v[at[0], at[1]] = value
        main.append(np.concatenate([w, w]))
        packed.append(v)
    return [
        np.concatenate(main, axis=1).astype(jnp.bfloat16),
        np.stack(packed).astype(jnp.bfloat16),
    ]


def departure(cell_mass_concentration):
    low_term = 1.0 + (1.0 - root_two) * covolume * cell_mass_concentration
    high_term = 1.0 + (1.0 + root_two) * covolume * cell_mass_concentration
    factor = attraction * (1.0 + acentric_coefficient_gradient) / (2.0 * root_two * covolume)
    value = factor * (jnp.log(low_term) - jnp.log(high_term))
    slope = factor * (
        (1.0 - root_two) * covolume / low_term - (1.0 + root_two) * covolume / high_term
    )
    return (value, slope)


def slopes(mass, internal):
    deviation, departure_slope = departure(mass)
    warmth = internal / isochoric_warmth_coefficient
    for _ in range(NEWTON):
        root = jnp.sqrt(warmth)
        multiplier = 1.0 + acentric_coefficient_gradient * (1.0 - root)
        mismatch = isochoric_warmth_coefficient * warmth + deviation * multiplier - internal
        gradient = isochoric_warmth_coefficient - deviation * acentric_coefficient_gradient / (
            2.0 * root
        )
        warmth = warmth - mismatch / gradient
    root = jnp.sqrt(warmth)
    multiplier = 1.0 + acentric_coefficient_gradient * (1.0 - root)
    gradient = isochoric_warmth_coefficient - deviation * acentric_coefficient_gradient / (
        2.0 * root
    )
    energy = 1.0 / gradient
    return (-departure_slope * multiplier * energy, energy)


def lanes():
    return lax.broadcasted_iota(jnp.int32, (8, X), 1)


def tile(t):
    return slice(8 * t, 8 * t + 8)


def prep_kernel(
    q_hbm, mass_hbm, internal_hbm, velocity_hbm, coef_ref, pack_ref, q, mass, internal, sems
):
    copies = [
        pltpu.make_async_copy(src, dst, sems.at[i])
        for i, (src, dst) in enumerate(
            (
                (mass_hbm, mass),
                (internal_hbm, internal),
                (velocity_hbm, coef_ref.at[pl.ds(4, 2)]),
                (q_hbm, q),
            )
        )
    ]
    for copy in copies:
        copy.start()
    copies[0].wait()
    copies[1].wait()
    density, energy = slopes(mass[...], internal[...])
    coef_ref[0:2] = density
    coef_ref[2:4] = energy
    copies[2].wait()
    copies[3].wait()
    group = lanes() >> 3
    for t in range(Z // 8):
        for c in range(2):
            acc = q[2 * c, tile(t), :]
            for y in range(2):
                for k in range(K):
                    i = 8 * y + k
                    if i:
                        part = pltpu.roll(q[4 * k + 2 * c + y, tile(t), :], 8 * i, 1)
                        acc = jnp.where(group == i, part, acc)
            pack_ref[c, tile(t), :] = acc
        acc = jnp.where(group == 0, coef_ref[0, tile(t), :], 0.0)
        for i in range(1, NC):
            acc = jnp.where(group == i, pltpu.roll(coef_ref[i, tile(t), :], 8 * i, 1), acc)
        pack_ref[2, tile(t), :] = acc


def rows_kernel(q_ref, rows_ref):
    for f in range(NF):
        rows_ref[f] = q_ref[f, 0:8, :]


def pairs():
    return [(k, m, (k + m) % K) for k in range(K) for m in range(5 if k < 4 else 4)]


def columns(result, lane, red, extra, sets):
    row = lax.broadcasted_iota(jnp.int32, (8, X), 0)
    mine = ((lane >> 3) & 7) == row
    rows = []
    for n in range(len(sets)):
        for m in range(5):
            acc = red[5 * n + m]
            if extra is not None:
                part = extra[5 * n + m]
                for d in (4, 2, 1):
                    part = part + pltpu.roll(part, d, 0)
                acc = acc + jnp.where(mine, part, 0.0)
            rows.append(jnp.where(row < 4, acc, 0.0) if m == 4 else acc)
    if len(rows) % 2:
        rows.append(rows[-1])
    rows = jnp.concatenate(rows, axis=0)
    high, low = split(rows)
    last = (rows - high.astype(F32) - low.astype(F32)).astype(jnp.bfloat16)
    total = product(
        jnp.concatenate([high, low, last], axis=1), jnp.ones((3 * X, X), jnp.bfloat16)
    )
    for n, place in enumerate(sets):
        for m in range(5):
            at = 8 * (5 * n + m)
            result = jnp.where(lane == 8 * place + m, total[at : at + 8, :], result)
    return result


def put(red, n, k, acc):
    red[n, k : k + 1, :] = jnp.sum(acc, axis=0, keepdims=True)


def side_of(packed, i):
    return pltpu.roll(packed, X - 8 * i, 1) if i else packed


def fill(pair, lane):
    out = jnp.where(lane < 8, pair[0], 0.0)
    out = jnp.where((lane >= 64) & (lane < 72), pltpu.roll(pair[1], 64, 1), out)
    for d in (8, 16, 32):
        out = out + pltpu.roll(out, d, 1)
    return out


def own_kernel(q_ref, coef_ref, warm_ref, last_ref, sums_ref, red):
    lane = lanes()
    red[...] = jnp.zeros_like(red)
    group = lane >> 3
    for t in range(Z // 8):
        last = [None] * 3
        for y in range(2):
            for k in range(K):
                i = 8 * y + k
                fields = [q_ref[4 * k + 2 * c + y, tile(t), :] for c in range(2)]
                fields.append(
                    coef_ref[y, tile(t), :] * fields[0] + coef_ref[2 + y, tile(t), :] * fields[1]
                )
                warm_ref[2 * k + y, tile(t), :] = fields[2]
                for n in range(2):
                    part = pltpu.roll(fields[n], (8 * i + 8) % X, 1) if i < 15 else fields[n]
                    last[n] = part if i == 0 else jnp.where(group == i, part, last[n])
        full = [
            fill([pltpu.roll(coef_ref[2 * n + y, tile(t), :], 8, 1) for y in range(2)], lane)
            for n in range(3)
        ]
        last[2] = full[0] * last[0] + full[1] * last[1]
        for n in range(3):
            last_ref[n, tile(t), :] = last[n]
            last_ref[3 + n, tile(t), :] = full[n]
    for k, m, l in pairs():
        acc = jnp.zeros((8, X), F32)
        for p in range(4):
            for t in range(Z // 8):
                acc = acc + q_ref[4 * k + p, tile(t), :] * q_ref[4 * l + p, tile(t), :]
        put(red, m, k, acc)
    speed = jnp.zeros((8, X), F32)
    for y in range(2):
        for t in range(Z // 8):
            v = coef_ref[4 + y, tile(t), :]
            speed = speed + v * v
    result = jnp.where(lane == 40, jnp.sum(speed, axis=1, keepdims=True), 0.0)
    sums_ref[...] = columns(result, lane, red, None, (0,))


def join(side_ref, last_ref, packed, t, at, lane):
    rows = slice(at, at + 8)
    got = [side_ref[c, tile(t), :] for c in range(2)]
    third = side_ref[2, tile(t), :]
    full = [fill([side_of(third, 2 * n + y) for y in range(2)], lane) for n in range(3)]
    got.append(full[0] * got[0] + full[1] * got[1])
    for n, part in enumerate(got + full):
        packed[n, rows, 0:X] = last_ref[n, tile(t), :]
        packed[n, rows, X : 2 * X] = part


def corner_kernel(side_ref, last_ref, coef_ref, corner_ref, packed):
    join(side_ref, last_ref, packed, 0, 0, lanes())
    for n in range(6):
        corner_ref[n] = packed[n, :, 0:X]
        corner_ref[6 + n] = packed[n, :, X : 2 * X]
        corner_ref[12 + n] = coef_ref[n, 0:8, :]


def split(x):
    high = x.astype(jnp.bfloat16)
    return high, (x - high.astype(F32)).astype(jnp.bfloat16)


def product(x, w):
    return jnp.dot(x, w, preferred_element_type=F32)


def rest(at, other):
    return 16.0 * (at(-1) + at(1) + other) - (at(-2) + at(2)) - 60.0 * at(0)


def each():
    return [(k, y) for k in range(K) for y in range(2)]


def main_rates(count, weights, r_at, e_at, t_at):
    def stack(at):
        rows = jnp.concatenate([at(i) for i in range(count)], axis=0)
        return jnp.concatenate(split(rows), axis=1)

    both = product(stack(r_at), weights[...])
    slope = product(stack(e_at), weights[:, 0:X])
    bend = product(stack(t_at), weights[:, X : 2 * X])
    out = []
    for i in range(count):
        rows = slice(8 * i, 8 * i + 8)
        out.append((both[rows, 0:X], both[rows, X:], slope[rows], bend[rows]))
    return out


def main_rate(speed, parts, r_at, t_at, r_other, t_other):
    slope_r, bend_r, slope_e, bend_t = parts
    rate_r = speed * slope_r + (viscosity / 12.0) * (bend_r + rest(r_at, r_other))
    rate_e = speed * slope_e + (conductivity / 12.0) * (bend_t + rest(t_at, t_other))
    return rate_r, rate_e


def turned(x):
    return jnp.concatenate([pltpu.roll(x[:, 0:X], 64, 1), pltpu.roll(x[:, X:], 64, 1)], axis=1)


def packed_rate(speed, weights, at):
    def along(n, w):
        high, low = split(at(n, 0))
        return product(high, weights[w]) + product(low, weights[w])

    rate_r = speed * along(0, 0) + (viscosity / 12.0) * (
        along(0, 1) + rest(lambda d: at(0, d), turned(at(0, 0)))
    )
    rate_e = speed * along(1, 0) + (conductivity / 12.0) * (
        along(2, 1) + rest(lambda d: at(2, d), turned(at(2, 0)))
    )
    return rate_r, rate_e


def packed_steps(packed, wp, pa, blocks, first, second, count, lane):
    src, dst, height = first
    rows = slice(src, src + height)
    got = packed_rate(
        packed[5, rows, :] * (-1.0 / 12.0), wp, lambda n, d: packed[n, src + d : src + d + height, :]
    )
    out = slice(dst, dst + height)
    pa[0, out, :] = got[0]
    pa[1, out, :] = got[1]
    pa[2, out, :] = packed[3, rows, :] * got[0] + packed[4, rows, :] * got[1]
    here, there = second
    rows = slice(here, here + count)
    got = packed_rate(
        packed[5, rows, :] * (-1.0 / 12.0),
        wp,
        lambda n, d: pa[n, there + d : there + d + count, :],
    )
    qp, ap, bp = blocks
    low = (lax.broadcasted_iota(jnp.int32, (count, X), 1) & 7) < 4
    for c in range(2):
        for dest, value in (
            (qp, packed[c, rows, :]),
            (ap, pa[c, there : there + count, :]),
            (bp, 0.5 * got[c]),
        ):
            dest[c] = jnp.where(low, value[:, X:], value[:, 0:X])


def main_sums(red, q_at, ad, bd, tiles):
    for k, m, l in pairs():
        acc = [jnp.zeros((8, X), F32)] * 4
        for p in range(4):
            for t in range(tiles):
                qk, ql = q_at(4 * k + p, t), q_at(4 * l + p, t)
                ak, bk = (v[4 * k + p, tile(t), :] for v in (ad, bd))
                al, bl = (v[4 * l + p, tile(t), :] for v in (ad, bd))
                acc[0] = acc[0] + (qk * al + ak * ql)
                acc[1] = acc[1] + (ak * al + (qk * bl + bk * ql))
                acc[2] = acc[2] + (ak * bl + bk * al)
                acc[3] = acc[3] + bk * bl
        for n in range(4):
            put(red, 5 * n + m, k, acc[n])


def packed_sums(extra, blocks, tiles, lane):
    acc = [jnp.zeros((8, X), F32) for _ in range(20)]
    for c in range(2):
        for t in range(tiles):
            q, a, b = (ref[c, tile(t), :] for ref in blocks)
            for m in range(5):

                def other(v, m=m):
                    if m == 0:
                        return v
                    near = pltpu.roll(v, X - 8 * m, 1)
                    return jnp.where((lane & 63) < 64 - 8 * m, near, pltpu.roll(v, 64 - 8 * m, 1))

                ql, al, bl = other(q), other(a), other(b)
                acc[m] = acc[m] + (q * al + a * ql)
                acc[5 + m] = acc[5 + m] + (a * al + (q * bl + b * ql))
                acc[10 + m] = acc[10 + m] + (a * bl + b * al)
                acc[15 + m] = acc[15 + m] + b * bl
    for n in range(20):
        extra[n] = acc[n]


def inside(rows):
    lane = lax.broadcasted_iota(jnp.int32, (rows, X), 1)
    return (lane >= 4) & (lane < 124)


def inner_kernel(
    q_ref, coef_ref, warm_ref, side_ref, last_ref, own_ref, wm_ref, wp_ref,
    ad_ref, bd_ref, ap_ref, bp_ref, tail_ref, packed_ref, sums_ref,
    packed, pa, qp, am, tm, red, extra,
):
    lane = lanes()
    red[...] = jnp.zeros_like(red)
    for t in range(Z // 8):
        join(side_ref, last_ref, packed, t, 8 * t, lane)
    packed_steps(packed, wp_ref, pa, (qp, ap_ref, bp_ref), (2, 2, 28), (4, 4), 24, lane)
    packed_sums(extra, (qp, ap_ref, bp_ref), 3, lane)
    for n in range(3):
        packed_ref[n] = pa[n, 22:30, :]
    for n in range(6):
        packed_ref[3 + n] = packed[n, 24:32, :]
    keep = inside(8)

    def vectors(j, carry):
        planes = [(STEP * j + i, y) for i in range(STEP) for y in range(2)]
        order = [(k, y, r) for k, y in planes for r in (2, 10, 18, 22)]
        parts = main_rates(
            len(order),
            wm_ref,
            lambda i: q_ref[4 * order[i][0] + order[i][1], order[i][2] : order[i][2] + 8, :],
            lambda i: q_ref[4 * order[i][0] + 2 + order[i][1], order[i][2] : order[i][2] + 8, :],
            lambda i: warm_ref[2 * order[i][0] + order[i][1], order[i][2] : order[i][2] + 8, :],
        )
        for i, (k, y, r) in enumerate(order):
            rows = slice(r, r + 8)
            got = main_rate(
                coef_ref[4 + y, rows, :] * (-1.0 / 12.0),
                parts[i],
                lambda d: q_ref[4 * k + y, r + d : r + d + 8, :],
                lambda d: warm_ref[2 * k + y, r + d : r + d + 8, :],
                q_ref[4 * k + 1 - y, rows, :],
                warm_ref[2 * k + 1 - y, rows, :],
            )
            for c in range(2):
                am[k, 2 * c + y, rows, :] = got[c]
            tm[k, y, rows, :] = coef_ref[y, rows, :] * got[0] + coef_ref[2 + y, rows, :] * got[1]
        order = [(k, y, r) for k, y in planes for r in (4, 12, 20)]
        parts = main_rates(
            len(order),
            wm_ref,
            lambda i: am[order[i][0], order[i][1], order[i][2] : order[i][2] + 8, :],
            lambda i: am[order[i][0], 2 + order[i][1], order[i][2] : order[i][2] + 8, :],
            lambda i: tm[order[i][0], order[i][1], order[i][2] : order[i][2] + 8, :],
        )
        for i, (k, y, r) in enumerate(order):
            rows = slice(r, r + 8)
            got = main_rate(
                coef_ref[4 + y, rows, :] * (-1.0 / 12.0),
                parts[i],
                lambda d: am[k, y, r + d : r + d + 8, :],
                lambda d: tm[k, y, r + d : r + d + 8, :],
                am[k, 1 - y, rows, :],
                tm[k, 1 - y, rows, :],
            )
            for c in range(2):
                f = 4 * k + 2 * c + y
                bd_ref[f, r - 4 : r + 4, :] = jnp.where(keep, 0.5 * got[c], 0.0)
                ad_ref[f, r - 4 : r + 4, :] = jnp.where(keep, am[k, 2 * c + y, rows, :], 0.0)
        for k in [STEP * j + i for i in range(STEP)]:
            for p in range(4):
                tail_ref[4 * k + p] = am[k, p, 22:30, :]
        return carry

    lax.fori_loop(0, K // STEP, vectors, 0)
    main_sums(red, lambda f, t: q_ref[f, 8 * t + 4 : 8 * t + 12, :], ad_ref, bd_ref, 3)
    sums_ref[...] = columns(own_ref[...], lane, red, extra, range(1, 5))


def edge_kernel(
    q_ref, coef_ref, warm_ref, below_ref, corner_ref, tail_ref, packed_ref, inner_ref, wm_ref, wp_ref,
    ad_ref, bd_ref, ap_ref, bp_ref, sums_ref,
    em, ec, wm, packed, pa, qp, am, tm, red, extra,
):
    lane = lanes()
    red[...] = jnp.zeros_like(red)
    for n in range(NC):
        ec[n, 0:8, :] = coef_ref[n, 24:32, :]
        ec[n, 8:16, :] = corner_ref[12 + n]
        packed[n, 0:8, :] = packed_ref[3 + n]
        packed[n, 8:16, 0:X] = corner_ref[n]
        packed[n, 8:16, X : 2 * X] = corner_ref[6 + n]
    for n in range(3):
        pa[n, 0:8, :] = packed_ref[n]
    packed_steps(packed, wp_ref, pa, (qp, ap_ref, bp_ref), (6, 8, 8), (4, 6), 8, lane)
    packed_sums(extra, (qp, ap_ref, bp_ref), 1, lane)
    keep = inside(8)
    for k in range(K):
        base = 4 * k
        for p in range(4):
            em[base + p, 0:8, :] = q_ref[base + p, 24:32, :]
            em[base + p, 8:16, :] = below_ref[base + p]
            am[k, p, 0:8, :] = tail_ref[base + p]
        for y in range(2):
            wm[k, y, 0:8, :] = warm_ref[2 * k + y, 24:32, :]
            wm[k, y, 8:16, :] = (
                ec[y, 8:16, :] * below_ref[base + y] + ec[2 + y, 8:16, :] * below_ref[base + 2 + y]
            )
    order = each()
    parts = main_rates(
        16,
        wm_ref,
        lambda i: em[4 * order[i][0] + order[i][1], 6:14, :],
        lambda i: em[4 * order[i][0] + 2 + order[i][1], 6:14, :],
        lambda i: wm[order[i][0], order[i][1], 6:14, :],
    )
    for i, (k, y) in enumerate(order):
        got = main_rate(
            ec[4 + y, 6:14, :] * (-1.0 / 12.0),
            parts[i],
            lambda d: em[4 * k + y, 6 + d : 14 + d, :],
            lambda d: wm[k, y, 6 + d : 14 + d, :],
            em[4 * k + 1 - y, 6:14, :],
            wm[k, 1 - y, 6:14, :],
        )
        for c in range(2):
            am[k, 2 * c + y, 8:16, :] = got[c]
        tm[k, y, 8:16, :] = ec[y, 6:14, :] * got[0] + ec[2 + y, 6:14, :] * got[1]
        tm[k, y, 4:8, :] = (
            ec[y, 2:6, :] * am[k, y, 4:8, :] + ec[2 + y, 2:6, :] * am[k, 2 + y, 4:8, :]
        )
    parts = main_rates(
        16,
        wm_ref,
        lambda i: am[order[i][0], order[i][1], 6:14, :],
        lambda i: am[order[i][0], 2 + order[i][1], 6:14, :],
        lambda i: tm[order[i][0], order[i][1], 6:14, :],
    )
    for i, (k, y) in enumerate(order):
        got = main_rate(
            ec[4 + y, 4:12, :] * (-1.0 / 12.0),
            parts[i],
            lambda d: am[k, y, 6 + d : 14 + d, :],
            lambda d: tm[k, y, 6 + d : 14 + d, :],
            am[k, 1 - y, 6:14, :],
            tm[k, 1 - y, 6:14, :],
        )
        for c in range(2):
            f = 4 * k + 2 * c + y
            bd_ref[f] = jnp.where(keep, 0.5 * got[c], 0.0)
            ad_ref[f] = jnp.where(keep, am[k, 2 * c + y, 6:14, :], 0.0)
    main_sums(red, lambda f, t: em[f, 4:12, :], ad_ref, bd_ref, 1)
    result = columns(jnp.zeros((8, X), F32), lane, red, extra, range(1, 5)) + inner_ref[...]
    for n in range(sums_ref.shape[0]):
        sums_ref[n] = result


def give_kernel(ap_ref, bp_ref, ape_ref, bpe_ref, out_ref):
    for n, (ref, edge) in enumerate(((ap_ref, ape_ref), (bp_ref, bpe_ref))):
        for c in range(2):
            out_ref[n, c, 0:24, :] = ref[c]
            out_ref[n, c, 24:32, :] = edge[c]


def place_kernel(ad_ref, bd_ref, ade_ref, bde_ref, mine_ref, got_ref, a_ref, b_ref, down_ref):
    lane = lanes()
    strip = (lane < 4) | (lane >= 124)
    low = (lane & 7) < 4
    for n, (ref, edge, out) in enumerate(((ad_ref, ade_ref, a_ref), (bd_ref, bde_ref, b_ref))):
        for c in range(2):
            for t in range(Z // 8):
                mine = pltpu.roll(mine_ref[n, c, tile(t), :], X - 8, 1)
                both = jnp.where(low, got_ref[n, c, tile(t), :], mine)
                for y in range(2):
                    for k in range(K):
                        f = 4 * k + 2 * c + y
                        part = ref[f, tile(t), :] if t < 3 else edge[f]
                        part = jnp.where(strip, side_of(both, 8 * y + k), part)
                        if t < 3:
                            out[f, 8 * t + 4 : 8 * t + 12, :] = part
                        else:
                            out[f, 28:32, :] = part[0:4, :]
                            out[f, 0:4, :] = jnp.zeros((4, X), F32)
                            r = 4 * (NF * n + f)
                            down_ref[r : r + 4, :] = part[4:8, :]


def finish_kernel(cells, q_ref, a_ref, b_ref, above_ref, sums_ref, out_ref, growth_ref, first):
    lane = lanes()
    row = lax.broadcasted_iota(jnp.int32, (8, X), 0)
    for n, ref in enumerate((a_ref, b_ref)):
        for f in range(NF):
            r = 4 * (NF * n + f)
            first[n, f, 0:4, :] = above_ref[r : r + 4, :]
            first[n, f, 4:8, :] = ref[f, 4:8, :]
    total = sums_ref[0]
    for n in range(1, sums_ref.shape[0]):
        total = total + sums_ref[n]
    speed = jnp.broadcast_to(jnp.sum(total[:, 40:41], axis=0, keepdims=True), (8, X))
    step = courant_number / jnp.sqrt(speed * (1.0 / cells) + 1e-05)
    gram = total
    power = step
    for n in range(1, 5):
        gram = gram + power * pltpu.roll(total, X - 8 * n, 1)
        power = power * step
    gram = gram * (1.0 / (2.0 * cells))
    cols = [jnp.broadcast_to(gram[:, m : m + 1], (8, X)) for m in range(5)]

    def entry(i, j):
        k, m = (j, i - j) if i - j <= 4 else (i, j - i + K)
        if m == 4:
            k = min(i, j)
        return jnp.broadcast_to(cols[m][k : k + 1, :], (8, X))

    low = [[None] * K for _ in range(K)]
    inv_diag = []
    for j in range(K):
        d = entry(j, j)
        for p in range(j):
            d = d - low[j][p] * low[j][p]
        root = jnp.sqrt(d)
        low[j][j] = root
        inv_diag.append(1.0 / root)
        for i in range(j + 1, K):
            v = entry(i, j)
            for p in range(j):
                v = v - low[i][p] * low[j][p]
            low[i][j] = v * inv_diag[j]
    inverse = [[None] * K for _ in range(K)]
    for j in range(K):
        inverse[j][j] = inv_diag[j]
        for i in range(j + 1, K):
            v = low[i][j] * inverse[j][j]
            for p in range(j + 1, i):
                v = v + low[i][p] * inverse[p][j]
            inverse[i][j] = -v * inv_diag[i]
    growth = jnp.zeros((8, X), F32)
    for i in range(K):
        for j in range(i + 1):
            growth = jnp.where((row == j) & (lane == i), low[i][j], growth)
    growth_ref[...] = growth
    square = step * step
    for p in range(4):
        for t in range(Z // 8):
            adv = []
            for k in range(K):
                f = 4 * k + p
                a, b = (
                    (first[0, f], first[1, f])
                    if t == 0
                    else (a_ref[f, tile(t), :], b_ref[f, tile(t), :])
                )
                adv.append(q_ref[f, tile(t), :] + step * a + square * b)
            for k in range(K):
                v = inverse[k][0] * adv[0]
                for j in range(1, k + 1):
                    v = v + inverse[k][j] * adv[j]
                out_ref[4 * k + p, tile(t), :] = v


def call(body, outs, scratch=(), cost=2000000, limit=24, **more):
    shapes = [jax.ShapeDtypeStruct(s, F32) for s in outs]
    return pl.pallas_call(
        body,
        out_shape=shapes,
        scratch_shapes=[pltpu.VMEM(s, F32) if isinstance(s, tuple) else s for s in scratch],
        compiler_params=pltpu.CompilerParams(vmem_limit_bytes=limit * 1024 * 1024),
        cost_estimate=pl.CostEstimate(flops=cost, bytes_accessed=cost, transcendentals=0),
        **more,
    )


def ring(array, axes, step):
    size = lax.axis_size(axes)
    return lax.ppermute(array, axes, [(i, (i + step) % size) for i in range(size)])


def gathered(array, axes):
    return lax.all_to_all(array, axes, 0, 0)


def per_device(tangents, mass, internal, velocity):
    cells = float(2 * Z * X * lax.axis_size(GX) * lax.axis_size(GZ))
    near, far = lax.axis_size(NEAR), lax.axis_size(FAR)
    whole, inner, edge = (NF, Z, X), (NF, 24, X), (NF, 8, X)
    half, small, red = (2 * K, Z, X), (3, Z, X), (20, 8, X)
    wm, wp = (jnp.asarray(w) for w in bands())
    q = tangents.reshape(whole)
    coef, pack = call(
        prep_kernel,
        [(NC, Z, X), small],
        [whole, (2, Z, X), (2, Z, X), pltpu.SemaphoreType.DMA((4,))],
        limit=60,
        in_specs=[pl.BlockSpec(memory_space=pl.ANY)] * 4,
    )(q, mass, internal, velocity)
    side = ring(pack, GX, -1)
    later, _ = lax.optimization_barrier((q, pack))
    (rows,) = call(rows_kernel, [edge], cost=1000)(later)
    below = ring(rows, GZ, -1)
    warm, last, own = call(own_kernel, [half, (6, Z, X), (8, X)], [(5, 8, X)])(q, coef)
    side, warm, last, own = lax.optimization_barrier((side, warm, last, own))
    (corner,) = call(corner_kernel, [(18, 8, X)], [(6, 8, 2 * X)], cost=1000)(side, last, coef)
    corner = ring(corner, GZ, -1)
    ad, bd, ap, bp, tail, packed, part = call(
        inner_kernel,
        [inner, inner, (2, 24, X), (2, 24, X), edge, (9, 8, 2 * X), (8, X)],
        [(6, Z, 2 * X), (3, Z, 2 * X), (2, 24, X), (K, 4, Z, X), (K, 2, Z, X), red, red],
    )(q, coef, warm, side, last, own, wm, wp)
    ade, bde, ape, bpe, sums = call(
        edge_kernel,
        [edge, edge, (2, 8, X), (2, 8, X), (near, 8, X)],
        [(NF, 16, X), (NC, 16, X), (K, 2, 16, X), (6, 16, 2 * X), (3, 16, 2 * X), (2, 8, X)]
        + [(K, 4, 16, X), (K, 2, 16, X), red, red],
    )(q, coef, warm, below, corner, tail, packed, part, wm, wp)
    sums = jnp.sum(gathered(sums, NEAR), axis=0)
    (give,) = call(give_kernel, [(2, 2, Z, X)])(ap, bp, ape, bpe)
    got = ring(give, GX, 1)
    sums, got = lax.optimization_barrier((sums, got))
    sums = gathered(jnp.broadcast_to(sums, (far, 8, X)), FAR)
    a, b, down = call(place_kernel, [whole, whole, (8 * NF, X)])(ad, bd, ade, bde, give, got)
    above = ring(down, GZ, 1)
    out, growth = call(
        functools.partial(finish_kernel, cells), [whole, (8, X)], [(2, NF, 8, X)]
    )(q, a, b, above, sums)
    return (out.reshape(tangents.shape), growth[:, :K])


def solution(mesh):
    gx, gz = mesh.devices.shape
    fine = Mesh(mesh.devices.reshape(gx // 4, 4, gz // 4, 4), GX + GZ)
    in_specs = (P(None, None, None, GZ, GX),) + (P(None, GZ, GX),) * 3
    out_specs = (P(None, None, None, GZ, GX), P())
    return jax.shard_map(
        per_device, mesh=fine, in_specs=in_specs, out_specs=out_specs, check_vma=False
    )
```

```python
import functools

import jax
import jax.numpy as jnp
import numpy as np
from jax import lax
from jax.experimental import pallas as pl
from jax.experimental.pallas import tpu as pltpu
from jax.sharding import Mesh, PartitionSpec as P

NEWTON = 4
isochoric_warmth_coefficient = 3.0
attraction = 0.5
acentric_coefficient_gradient = 0.6
covolume = 0.15
root_two = 1.4142135623730951
viscosity = 0.2
conductivity = 1.0
courant_number = 0.5

K = 8
NF = 4 * K
NC = 6
NA = NF + NC
Z = 32
X = 128
GX = ("xh", "xl")
GZ = ("zh", "zl")
NEAR = ("xl", "zl")
FAR = ("xh", "zh")
F32 = jnp.float32
STEP = 4


def bands():
    first = {-2: 1.0, -1: -8.0, 1: 8.0, 2: -1.0}
    second = {-2: -1.0, -1: 16.0, 0: -30.0, 1: 16.0, 2: -1.0}
    main, packed = [], []
    for band in (first, second):
        w, v = np.zeros((X, X), np.float32), np.zeros((2 * X, 2 * X), np.float32)
        for d, value in band.items():
            for j in range(X):
                if 0 <= j + d < X:
                    w[j + d, j] = value
            for g in range(16):
                for j in range(16):
                    if 0 <= j + d < 16:
                        at = [X * (c // 8) + 8 * g + c % 8 for c in (j + d, j)]
                        v[at[0], at[1]] = value
        main.append(np.concatenate([w, w]))
        packed.append(v)
    return [
        np.concatenate(main, axis=1).astype(jnp.bfloat16),
        np.stack(packed).astype(jnp.bfloat16),
    ]


def departure(cell_mass_concentration):
    low_term = 1.0 + (1.0 - root_two) * covolume * cell_mass_concentration
    high_term = 1.0 + (1.0 + root_two) * covolume * cell_mass_concentration
    factor = attraction * (1.0 + acentric_coefficient_gradient) / (2.0 * root_two * covolume)
    value = factor * (jnp.log(low_term) - jnp.log(high_term))
    slope = factor * (
        (1.0 - root_two) * covolume / low_term - (1.0 + root_two) * covolume / high_term
    )
    return (value, slope)


def slopes(mass, internal):
    deviation, departure_slope = departure(mass)
    warmth = internal / isochoric_warmth_coefficient
    for _ in range(NEWTON):
        root = jnp.sqrt(warmth)
        multiplier = 1.0 + acentric_coefficient_gradient * (1.0 - root)
        mismatch = isochoric_warmth_coefficient * warmth + deviation * multiplier - internal
        gradient = isochoric_warmth_coefficient - deviation * acentric_coefficient_gradient / (
            2.0 * root
        )
        warmth = warmth - mismatch / gradient
    root = jnp.sqrt(warmth)
    multiplier = 1.0 + acentric_coefficient_gradient * (1.0 - root)
    gradient = isochoric_warmth_coefficient - deviation * acentric_coefficient_gradient / (
        2.0 * root
    )
    energy = 1.0 / gradient
    return (-departure_slope * multiplier * energy, energy)


def lanes():
    return lax.broadcasted_iota(jnp.int32, (8, X), 1)


def tile(t):
    return slice(8 * t, 8 * t + 8)


def prep_kernel(
    q_hbm, mass_hbm, internal_hbm, velocity_hbm, coef_ref, pack_ref, q, mass, internal, sems
):
    copies = [
        pltpu.make_async_copy(src, dst, sems.at[i])
        for i, (src, dst) in enumerate(
            (
                (mass_hbm, mass),
                (internal_hbm, internal),
                (velocity_hbm, coef_ref.at[pl.ds(4, 2)]),
                (q_hbm, q),
            )
        )
    ]
    for copy in copies:
        copy.start()
    copies[0].wait()
    copies[1].wait()
    density, energy = slopes(mass[...], internal[...])
    coef_ref[0:2] = density
    coef_ref[2:4] = energy
    copies[2].wait()
    copies[3].wait()
    group = lanes() >> 3
    for t in range(Z // 8):
        for c in range(2):
            acc = q[2 * c, tile(t), :]
            for y in range(2):
                for k in range(K):
                    i = 8 * y + k
                    if i:
                        part = pltpu.roll(q[4 * k + 2 * c + y, tile(t), :], 8 * i, 1)
                        acc = jnp.where(group == i, part, acc)
            pack_ref[c, tile(t), :] = acc
        acc = jnp.where(group == 0, coef_ref[0, tile(t), :], 0.0)
        for i in range(1, NC):
            acc = jnp.where(group == i, pltpu.roll(coef_ref[i, tile(t), :], 8 * i, 1), acc)
        pack_ref[2, tile(t), :] = acc


def pairs():
    return [(k, m, (k + m) % K) for k in range(K) for m in range(5 if k < 4 else 4)]


def columns(result, lane, red, extra, sets):
    row = lax.broadcasted_iota(jnp.int32, (8, X), 0)
    mine = ((lane >> 3) & 7) == row
    rows = []
    for n in range(len(sets)):
        for m in range(5):
            acc = red[5 * n + m]
            if extra is not None:
                part = extra[5 * n + m]
                for d in (4, 2, 1):
                    part = part + pltpu.roll(part, d, 0)
                acc = acc + jnp.where(mine, part, 0.0)
            rows.append(jnp.where(row < 4, acc, 0.0) if m == 4 else acc)
    if len(rows) % 2:
        rows.append(rows[-1])
    rows = jnp.concatenate(rows, axis=0)
    high, low = split(rows)
    last = (rows - high.astype(F32) - low.astype(F32)).astype(jnp.bfloat16)
    total = product(
        jnp.concatenate([high, low, last], axis=1), jnp.ones((3 * X, X), jnp.bfloat16)
    )
    for n, place in enumerate(sets):
        for m in range(5):
            at = 8 * (5 * n + m)
            result = jnp.where(lane == 8 * place + m, total[at : at + 8, :], result)
    return result


def put(red, n, k, acc):
    red[n, k : k + 1, :] = jnp.sum(acc, axis=0, keepdims=True)


def side_of(packed, i):
    return pltpu.roll(packed, X - 8 * i, 1) if i else packed


def fill(pair, lane):
    out = jnp.where(lane < 8, pair[0], 0.0)
    out = jnp.where((lane >= 64) & (lane < 72), pltpu.roll(pair[1], 64, 1), out)
    for d in (8, 16, 32):
        out = out + pltpu.roll(out, d, 1)
    return out


def own_kernel(q_ref, coef_ref, warm_ref, last_ref, sums_ref, red):
    lane = lanes()
    red[...] = jnp.zeros_like(red)
    group = lane >> 3
    for t in range(Z // 8):
        last = [None] * 3
        for y in range(2):
            for k in range(K):
                i = 8 * y + k
                fields = [q_ref[4 * k + 2 * c + y, tile(t), :] for c in range(2)]
                fields.append(
                    coef_ref[y, tile(t), :] * fields[0] + coef_ref[2 + y, tile(t), :] * fields[1]
                )
                warm_ref[2 * k + y, tile(t), :] = fields[2]
                for n in range(2):
                    part = pltpu.roll(fields[n], (8 * i + 8) % X, 1) if i < 15 else fields[n]
                    last[n] = part if i == 0 else jnp.where(group == i, part, last[n])
        full = [
            fill([pltpu.roll(coef_ref[2 * n + y, tile(t), :], 8, 1) for y in range(2)], lane)
            for n in range(3)
        ]
        last[2] = full[0] * last[0] + full[1] * last[1]
        for n in range(3):
            last_ref[n, tile(t), :] = last[n]
            last_ref[3 + n, tile(t), :] = full[n]
    for k, m, l in pairs():
        acc = jnp.zeros((8, X), F32)
        for p in range(4):
            for t in range(Z // 8):
                acc = acc + q_ref[4 * k + p, tile(t), :] * q_ref[4 * l + p, tile(t), :]
        put(red, m, k, acc)
    speed = jnp.zeros((8, X), F32)
    for y in range(2):
        for t in range(Z // 8):
            v = coef_ref[4 + y, tile(t), :]
            speed = speed + v * v
    result = jnp.where(lane == 40, jnp.sum(speed, axis=1, keepdims=True), 0.0)
    sums_ref[...] = columns(result, lane, red, None, (0,))


def join(side_ref, last_ref, packed, t, at, lane):
    rows = slice(at, at + 8)
    got = [side_ref[c, tile(t), :] for c in range(2)]
    third = side_ref[2, tile(t), :]
    full = [fill([side_of(third, 2 * n + y) for y in range(2)], lane) for n in range(3)]
    got.append(full[0] * got[0] + full[1] * got[1])
    for n, part in enumerate(got + full):
        packed[n, rows, 0:X] = last_ref[n, tile(t), :]
        packed[n, rows, X : 2 * X] = part


def wire_kernel(q_ref, side_ref, last_ref, coef_ref, rows_ref, packed):
    join(side_ref, last_ref, packed, 0, 0, lanes())
    for f in range(NF):
        rows_ref[f] = q_ref[f, 0:8, :]
    for n in range(6):
        rows_ref[NF + n] = packed[n, :, 0:X]
        rows_ref[NF + 6 + n] = packed[n, :, X : 2 * X]
        rows_ref[NF + 12 + n] = coef_ref[n, 0:8, :]


def split(x):
    high = x.astype(jnp.bfloat16)
    return high, (x - high.astype(F32)).astype(jnp.bfloat16)


def product(x, w):
    return jnp.dot(x, w, preferred_element_type=F32)


def rest(at, other):
    return 16.0 * (at(-1) + at(1) + other) - (at(-2) + at(2)) - 60.0 * at(0)


def each():
    return [(k, y) for k in range(K) for y in range(2)]


def main_rates(count, weights, r_at, e_at, t_at):
    def stack(at):
        rows = jnp.concatenate([at(i) for i in range(count)], axis=0)
        return jnp.concatenate(split(rows), axis=1)

    both = product(stack(r_at), weights[...])
    slope = product(stack(e_at), weights[:, 0:X])
    bend = product(stack(t_at), weights[:, X : 2 * X])
    out = []
    for i in range(count):
        rows = slice(8 * i, 8 * i + 8)
        out.append((both[rows, 0:X], both[rows, X:], slope[rows], bend[rows]))
    return out


def main_rate(speed, parts, r_at, t_at, r_other, t_other):
    slope_r, bend_r, slope_e, bend_t = parts
    rate_r = speed * slope_r + (viscosity / 12.0) * (bend_r + rest(r_at, r_other))
    rate_e = speed * slope_e + (conductivity / 12.0) * (bend_t + rest(t_at, t_other))
    return rate_r, rate_e


def turned(x):
    return jnp.concatenate([pltpu.roll(x[:, 0:X], 64, 1), pltpu.roll(x[:, X:], 64, 1)], axis=1)


def packed_rate(speed, weights, at):
    def along(n, w):
        high, low = split(at(n, 0))
        return product(high, weights[w]) + product(low, weights[w])

    rate_r = speed * along(0, 0) + (viscosity / 12.0) * (
        along(0, 1) + rest(lambda d: at(0, d), turned(at(0, 0)))
    )
    rate_e = speed * along(1, 0) + (conductivity / 12.0) * (
        along(2, 1) + rest(lambda d: at(2, d), turned(at(2, 0)))
    )
    return rate_r, rate_e


def packed_steps(packed, wp, pa, blocks, first, second, count, lane):
    src, dst, height = first
    rows = slice(src, src + height)
    got = packed_rate(
        packed[5, rows, :] * (-1.0 / 12.0), wp, lambda n, d: packed[n, src + d : src + d + height, :]
    )
    out = slice(dst, dst + height)
    pa[0, out, :] = got[0]
    pa[1, out, :] = got[1]
    pa[2, out, :] = packed[3, rows, :] * got[0] + packed[4, rows, :] * got[1]
    here, there = second
    rows = slice(here, here + count)
    got = packed_rate(
        packed[5, rows, :] * (-1.0 / 12.0),
        wp,
        lambda n, d: pa[n, there + d : there + d + count, :],
    )
    qp, ap, bp = blocks
    low = (lax.broadcasted_iota(jnp.int32, (count, X), 1) & 7) < 4
    for c in range(2):
        for dest, value in (
            (qp, packed[c, rows, :]),
            (ap, pa[c, there : there + count, :]),
            (bp, 0.5 * got[c]),
        ):
            dest[c] = jnp.where(low, value[:, X:], value[:, 0:X])


def main_sums(red, q_at, ad, bd, tiles):
    for k, m, l in pairs():
        acc = [jnp.zeros((8, X), F32)] * 4
        for p in range(4):
            for t in range(tiles):
                qk, ql = q_at(4 * k + p, t), q_at(4 * l + p, t)
                ak, bk = (v[4 * k + p, tile(t), :] for v in (ad, bd))
                al, bl = (v[4 * l + p, tile(t), :] for v in (ad, bd))
                acc[0] = acc[0] + (qk * al + ak * ql)
                acc[1] = acc[1] + (ak * al + (qk * bl + bk * ql))
                acc[2] = acc[2] + (ak * bl + bk * al)
                acc[3] = acc[3] + bk * bl
        for n in range(4):
            put(red, 5 * n + m, k, acc[n])


def packed_sums(extra, blocks, tiles, lane):
    acc = [jnp.zeros((8, X), F32) for _ in range(20)]
    for c in range(2):
        for t in range(tiles):
            q, a, b = (ref[c, tile(t), :] for ref in blocks)
            for m in range(5):

                def other(v, m=m):
                    if m == 0:
                        return v
                    near = pltpu.roll(v, X - 8 * m, 1)
                    return jnp.where((lane & 63) < 64 - 8 * m, near, pltpu.roll(v, 64 - 8 * m, 1))

                ql, al, bl = other(q), other(a), other(b)
                acc[m] = acc[m] + (q * al + a * ql)
                acc[5 + m] = acc[5 + m] + (a * al + (q * bl + b * ql))
                acc[10 + m] = acc[10 + m] + (a * bl + b * al)
                acc[15 + m] = acc[15 + m] + b * bl
    for n in range(20):
        extra[n] = acc[n]


def inside(rows):
    lane = lax.broadcasted_iota(jnp.int32, (rows, X), 1)
    return (lane >= 4) & (lane < 124)


def inner_kernel(
    q_ref, coef_ref, warm_ref, side_ref, last_ref, own_ref, wm_ref, wp_ref,
    ad_ref, bd_ref, ap_ref, bp_ref, tail_ref, packed_ref, sums_ref,
    packed, pa, qp, am, tm, red, extra,
):
    lane = lanes()
    red[...] = jnp.zeros_like(red)
    for t in range(Z // 8):
        join(side_ref, last_ref, packed, t, 8 * t, lane)
    packed_steps(packed, wp_ref, pa, (qp, ap_ref, bp_ref), (2, 2, 28), (4, 4), 24, lane)
    packed_sums(extra, (qp, ap_ref, bp_ref), 3, lane)
    for n in range(3):
        packed_ref[n] = pa[n, 22:30, :]
    for n in range(6):
        packed_ref[3 + n] = packed[n, 24:32, :]
    keep = inside(8)

    def vectors(j, carry):
        planes = [(STEP * j + i, y) for i in range(STEP) for y in range(2)]
        order = [(k, y, r) for k, y in planes for r in (2, 10, 18, 22)]
        parts = main_rates(
            len(order),
            wm_ref,
            lambda i: q_ref[4 * order[i][0] + order[i][1], order[i][2] : order[i][2] + 8, :],
            lambda i: q_ref[4 * order[i][0] + 2 + order[i][1], order[i][2] : order[i][2] + 8, :],
            lambda i: warm_ref[2 * order[i][0] + order[i][1], order[i][2] : order[i][2] + 8, :],
        )
        for i, (k, y, r) in enumerate(order):
            rows = slice(r, r + 8)
            got = main_rate(
                coef_ref[4 + y, rows, :] * (-1.0 / 12.0),
                parts[i],
                lambda d: q_ref[4 * k + y, r + d : r + d + 8, :],
                lambda d: warm_ref[2 * k + y, r + d : r + d + 8, :],
                q_ref[4 * k + 1 - y, rows, :],
                warm_ref[2 * k + 1 - y, rows, :],
            )
            for c in range(2):
                am[k, 2 * c + y, rows, :] = got[c]
            tm[k, y, rows, :] = coef_ref[y, rows, :] * got[0] + coef_ref[2 + y, rows, :] * got[1]
        order = [(k, y, r) for k, y in planes for r in (4, 12, 20)]
        parts = main_rates(
            len(order),
            wm_ref,
            lambda i: am[order[i][0], order[i][1], order[i][2] : order[i][2] + 8, :],
            lambda i: am[order[i][0], 2 + order[i][1], order[i][2] : order[i][2] + 8, :],
            lambda i: tm[order[i][0], order[i][1], order[i][2] : order[i][2] + 8, :],
        )
        for i, (k, y, r) in enumerate(order):
            rows = slice(r, r + 8)
            got = main_rate(
                coef_ref[4 + y, rows, :] * (-1.0 / 12.0),
                parts[i],
                lambda d: am[k, y, r + d : r + d + 8, :],
                lambda d: tm[k, y, r + d : r + d + 8, :],
                am[k, 1 - y, rows, :],
                tm[k, 1 - y, rows, :],
            )
            for c in range(2):
                f = 4 * k + 2 * c + y
                bd_ref[f, r - 4 : r + 4, :] = jnp.where(keep, 0.5 * got[c], 0.0)
                ad_ref[f, r - 4 : r + 4, :] = jnp.where(keep, am[k, 2 * c + y, rows, :], 0.0)
        for k in [STEP * j + i for i in range(STEP)]:
            for p in range(4):
                tail_ref[4 * k + p] = am[k, p, 22:30, :]
        return carry

    lax.fori_loop(0, K // STEP, vectors, 0)
    main_sums(red, lambda f, t: q_ref[f, 8 * t + 4 : 8 * t + 12, :], ad_ref, bd_ref, 3)
    sums_ref[...] = columns(own_ref[...], lane, red, extra, range(1, 5))


def edge_kernel(
    q_ref, coef_ref, warm_ref, below_ref, tail_ref, packed_ref, inner_ref, wm_ref, wp_ref,
    ad_ref, bd_ref, ap_ref, bp_ref, sums_ref,
    em, ec, wm, packed, pa, qp, am, tm, red, extra,
):
    lane = lanes()
    red[...] = jnp.zeros_like(red)
    for n in range(NC):
        ec[n, 0:8, :] = coef_ref[n, 24:32, :]
        ec[n, 8:16, :] = below_ref[NF + 12 + n]
        packed[n, 0:8, :] = packed_ref[3 + n]
        packed[n, 8:16, 0:X] = below_ref[NF + n]
        packed[n, 8:16, X : 2 * X] = below_ref[NF + 6 + n]
    for n in range(3):
        pa[n, 0:8, :] = packed_ref[n]
    packed_steps(packed, wp_ref, pa, (qp, ap_ref, bp_ref), (6, 8, 8), (4, 6), 8, lane)
    packed_sums(extra, (qp, ap_ref, bp_ref), 1, lane)
    keep = inside(8)
    for k in range(K):
        base = 4 * k
        for p in range(4):
            em[base + p, 0:8, :] = q_ref[base + p, 24:32, :]
            em[base + p, 8:16, :] = below_ref[base + p]
            am[k, p, 0:8, :] = tail_ref[base + p]
        for y in range(2):
            wm[k, y, 0:8, :] = warm_ref[2 * k + y, 24:32, :]
            wm[k, y, 8:16, :] = (
                ec[y, 8:16, :] * below_ref[base + y] + ec[2 + y, 8:16, :] * below_ref[base + 2 + y]
            )
    order = each()
    parts = main_rates(
        16,
        wm_ref,
        lambda i: em[4 * order[i][0] + order[i][1], 6:14, :],
        lambda i: em[4 * order[i][0] + 2 + order[i][1], 6:14, :],
        lambda i: wm[order[i][0], order[i][1], 6:14, :],
    )
    for i, (k, y) in enumerate(order):
        got = main_rate(
            ec[4 + y, 6:14, :] * (-1.0 / 12.0),
            parts[i],
            lambda d: em[4 * k + y, 6 + d : 14 + d, :],
            lambda d: wm[k, y, 6 + d : 14 + d, :],
            em[4 * k + 1 - y, 6:14, :],
            wm[k, 1 - y, 6:14, :],
        )
        for c in range(2):
            am[k, 2 * c + y, 8:16, :] = got[c]
        tm[k, y, 8:16, :] = ec[y, 6:14, :] * got[0] + ec[2 + y, 6:14, :] * got[1]
        tm[k, y, 4:8, :] = (
            ec[y, 2:6, :] * am[k, y, 4:8, :] + ec[2 + y, 2:6, :] * am[k, 2 + y, 4:8, :]
        )
    parts = main_rates(
        16,
        wm_ref,
        lambda i: am[order[i][0], order[i][1], 6:14, :],
        lambda i: am[order[i][0], 2 + order[i][1], 6:14, :],
        lambda i: tm[order[i][0], order[i][1], 6:14, :],
    )
    for i, (k, y) in enumerate(order):
        got = main_rate(
            ec[4 + y, 4:12, :] * (-1.0 / 12.0),
            parts[i],
            lambda d: am[k, y, 6 + d : 14 + d, :],
            lambda d: tm[k, y, 6 + d : 14 + d, :],
            am[k, 1 - y, 6:14, :],
            tm[k, 1 - y, 6:14, :],
        )
        for c in range(2):
            f = 4 * k + 2 * c + y
            bd_ref[f] = jnp.where(keep, 0.5 * got[c], 0.0)
            ad_ref[f] = jnp.where(keep, am[k, 2 * c + y, 6:14, :], 0.0)
    main_sums(red, lambda f, t: em[f, 4:12, :], ad_ref, bd_ref, 1)
    result = columns(jnp.zeros((8, X), F32), lane, red, extra, range(1, 5)) + inner_ref[...]
    for n in range(sums_ref.shape[0]):
        sums_ref[n] = result


def give_kernel(ap_ref, bp_ref, ape_ref, bpe_ref, out_ref):
    for n, (ref, edge) in enumerate(((ap_ref, ape_ref), (bp_ref, bpe_ref))):
        for c in range(2):
            out_ref[n, c, 0:24, :] = ref[c]
            out_ref[n, c, 24:32, :] = edge[c]


def place_kernel(ad_ref, bd_ref, ade_ref, bde_ref, mine_ref, got_ref, a_ref, b_ref, down_ref):
    lane = lanes()
    strip = (lane < 4) | (lane >= 124)
    low = (lane & 7) < 4
    for n, (ref, edge, out) in enumerate(((ad_ref, ade_ref, a_ref), (bd_ref, bde_ref, b_ref))):
        for c in range(2):
            for t in range(Z // 8):
                mine = pltpu.roll(mine_ref[n, c, tile(t), :], X - 8, 1)
                both = jnp.where(low, got_ref[n, c, tile(t), :], mine)
                for y in range(2):
                    for k in range(K):
                        f = 4 * k + 2 * c + y
                        part = ref[f, tile(t), :] if t < 3 else edge[f]
                        part = jnp.where(strip, side_of(both, 8 * y + k), part)
                        if t < 3:
                            out[f, 8 * t + 4 : 8 * t + 12, :] = part
                        else:
                            out[f, 28:32, :] = part[0:4, :]
                            out[f, 0:4, :] = jnp.zeros((4, X), F32)
                            r = 4 * (NF * n + f)
                            down_ref[r : r + 4, :] = part[4:8, :]


def finish_kernel(cells, q_ref, a_ref, b_ref, above_ref, sums_ref, out_ref, growth_ref, first):
    lane = lanes()
    row = lax.broadcasted_iota(jnp.int32, (8, X), 0)
    for n, ref in enumerate((a_ref, b_ref)):
        for f in range(NF):
            r = 4 * (NF * n + f)
            first[n, f, 0:4, :] = above_ref[r : r + 4, :]
            first[n, f, 4:8, :] = ref[f, 4:8, :]
    total = sums_ref[0]
    for n in range(1, sums_ref.shape[0]):
        total = total + sums_ref[n]
    speed = jnp.broadcast_to(jnp.sum(total[:, 40:41], axis=0, keepdims=True), (8, X))
    step = courant_number / jnp.sqrt(speed * (1.0 / cells) + 1e-05)
    gram = total
    power = step
    for n in range(1, 5):
        gram = gram + power * pltpu.roll(total, X - 8 * n, 1)
        power = power * step
    gram = gram * (1.0 / (2.0 * cells))
    cols = [jnp.broadcast_to(gram[:, m : m + 1], (8, X)) for m in range(5)]

    def entry(i, j):
        k, m = (j, i - j) if i - j <= 4 else (i, j - i + K)
        if m == 4:
            k = min(i, j)
        return jnp.broadcast_to(cols[m][k : k + 1, :], (8, X))

    low = [[None] * K for _ in range(K)]
    inv_diag = []
    for j in range(K):
        d = entry(j, j)
        for p in range(j):
            d = d - low[j][p] * low[j][p]
        root = jnp.sqrt(d)
        low[j][j] = root
        inv_diag.append(1.0 / root)
        for i in range(j + 1, K):
            v = entry(i, j)
            for p in range(j):
                v = v - low[i][p] * low[j][p]
            low[i][j] = v * inv_diag[j]
    inverse = [[None] * K for _ in range(K)]
    for j in range(K):
        inverse[j][j] = inv_diag[j]
        for i in range(j + 1, K):
            v = low[i][j] * inverse[j][j]
            for p in range(j + 1, i):
                v = v + low[i][p] * inverse[p][j]
            inverse[i][j] = -v * inv_diag[i]
    growth = jnp.zeros((8, X), F32)
    for i in range(K):
        for j in range(i + 1):
            growth = jnp.where((row == j) & (lane == i), low[i][j], growth)
    growth_ref[...] = growth
    square = step * step
    for p in range(4):
        for t in range(Z // 8):
            adv = []
            for k in range(K):
                f = 4 * k + p
                a, b = (
                    (first[0, f], first[1, f])
                    if t == 0
                    else (a_ref[f, tile(t), :], b_ref[f, tile(t), :])
                )
                adv.append(q_ref[f, tile(t), :] + step * a + square * b)
            for k in range(K):
                v = inverse[k][0] * adv[0]
                for j in range(1, k + 1):
                    v = v + inverse[k][j] * adv[j]
                out_ref[4 * k + p, tile(t), :] = v


def call(body, outs, scratch=(), cost=2000000, limit=24, **more):
    shapes = [jax.ShapeDtypeStruct(s, F32) for s in outs]
    return pl.pallas_call(
        body,
        out_shape=shapes,
        scratch_shapes=[pltpu.VMEM(s, F32) if isinstance(s, tuple) else s for s in scratch],
        compiler_params=pltpu.CompilerParams(vmem_limit_bytes=limit * 1024 * 1024),
        cost_estimate=pl.CostEstimate(flops=cost, bytes_accessed=cost, transcendentals=0),
        **more,
    )


def ring(array, axes, step):
    size = lax.axis_size(axes)
    return lax.ppermute(array, axes, [(i, (i + step) % size) for i in range(size)])


def gathered(array, axes):
    return lax.all_to_all(array, axes, 0, 0)


def per_device(tangents, mass, internal, velocity):
    cells = float(2 * Z * X * lax.axis_size(GX) * lax.axis_size(GZ))
    near, far = lax.axis_size(NEAR), lax.axis_size(FAR)
    whole, inner, edge = (NF, Z, X), (NF, 24, X), (NF, 8, X)
    half, small, red = (2 * K, Z, X), (3, Z, X), (20, 8, X)
    wm, wp = (jnp.asarray(w) for w in bands())
    q = tangents.reshape(whole)
    coef, pack = call(
        prep_kernel,
        [(NC, Z, X), small],
        [whole, (2, Z, X), (2, Z, X), pltpu.SemaphoreType.DMA((4,))],
        limit=60,
        in_specs=[pl.BlockSpec(memory_space=pl.ANY)] * 4,
    )(q, mass, internal, velocity)
    side = ring(pack, GX, -1)
    warm, last, own = call(own_kernel, [half, (6, Z, X), (8, X)], [(5, 8, X)])(q, coef)
    side, warm, last, own = lax.optimization_barrier((side, warm, last, own))
    (rows,) = call(wire_kernel, [(NF + 18, 8, X)], [(6, 8, 2 * X)], cost=1000)(q, side, last, coef)
    below = ring(rows, GZ, -1)
    ad, bd, ap, bp, tail, packed, part = call(
        inner_kernel,
        [inner, inner, (2, 24, X), (2, 24, X), edge, (9, 8, 2 * X), (8, X)],
        [(6, Z, 2 * X), (3, Z, 2 * X), (2, 24, X), (K, 4, Z, X), (K, 2, Z, X), red, red],
    )(q, coef, warm, side, last, own, wm, wp)
    ade, bde, ape, bpe, sums = call(
        edge_kernel,
        [edge, edge, (2, 8, X), (2, 8, X), (near, 8, X)],
        [(NF, 16, X), (NC, 16, X), (K, 2, 16, X), (6, 16, 2 * X), (3, 16, 2 * X), (2, 8, X)]
        + [(K, 4, 16, X), (K, 2, 16, X), red, red],
    )(q, coef, warm, below, tail, packed, part, wm, wp)
    sums = jnp.sum(gathered(sums, NEAR), axis=0)
    (give,) = call(give_kernel, [(2, 2, Z, X)])(ap, bp, ape, bpe)
    got = ring(give, GX, 1)
    sums, got = lax.optimization_barrier((sums, got))
    sums = gathered(jnp.broadcast_to(sums, (far, 8, X)), FAR)
    a, b, down = call(place_kernel, [whole, whole, (8 * NF, X)])(ad, bd, ade, bde, give, got)
    above = ring(down, GZ, 1)
    out, growth = call(
        functools.partial(finish_kernel, cells), [whole, (8, X)], [(2, NF, 8, X)]
    )(q, a, b, above, sums)
    return (out.reshape(tangents.shape), growth[:, :K])


def solution(mesh):
    gx, gz = mesh.devices.shape
    fine = Mesh(mesh.devices.reshape(gx // 4, 4, gz // 4, 4), GX + GZ)
    in_specs = (P(None, None, None, GZ, GX),) + (P(None, GZ, GX),) * 3
    out_specs = (P(None, None, None, GZ, GX), P())
    return jax.shard_map(
        per_device, mesh=fine, in_specs=in_specs, out_specs=out_specs, check_vma=False
    )
```

```python
import functools

import jax
import jax.numpy as jnp
import numpy as np
from jax import lax
from jax.experimental import pallas as pl
from jax.experimental.pallas import tpu as pltpu
from jax.sharding import Mesh, PartitionSpec as P

NEWTON = 4
isochoric_warmth_coefficient = 3.0
attraction = 0.5
acentric_coefficient_gradient = 0.6
covolume = 0.15
root_two = 1.4142135623730951
viscosity = 0.2
conductivity = 1.0
courant_number = 0.5

K = 8
NF = 4 * K
NC = 6
NA = NF + NC
Z = 32
X = 128
GX = ("xh", "xl")
GZ = ("zh", "zl")
NEAR = ("xl", "zl")
FAR = ("xh", "zh")
F32 = jnp.float32
STEP = 4


def bands():
    first = {-2: 1.0, -1: -8.0, 1: 8.0, 2: -1.0}
    second = {-2: -1.0, -1: 16.0, 0: -30.0, 1: 16.0, 2: -1.0}
    main, packed = [], []
    for band in (first, second):
        w, v = np.zeros((X, X), np.float32), np.zeros((2 * X, 2 * X), np.float32)
        for d, value in band.items():
            for j in range(X):
                if 0 <= j + d < X:
                    w[j + d, j] = value
            for g in range(16):
                for j in range(16):
                    if 0 <= j + d < 16:
                        at = [X * (c // 8) + 8 * g + c % 8 for c in (j + d, j)]
                        v[at[0], at[1]] = value
        main.append(np.concatenate([w, w]))
        packed.append(v)
    return [
        np.concatenate(main, axis=1).astype(jnp.bfloat16),
        np.stack(packed).astype(jnp.bfloat16),
    ]


def departure(cell_mass_concentration):
    low_term = 1.0 + (1.0 - root_two) * covolume * cell_mass_concentration
    high_term = 1.0 + (1.0 + root_two) * covolume * cell_mass_concentration
    factor = attraction * (1.0 + acentric_coefficient_gradient) / (2.0 * root_two * covolume)
    value = factor * (jnp.log(low_term) - jnp.log(high_term))
    slope = factor * (
        (1.0 - root_two) * covolume / low_term - (1.0 + root_two) * covolume / high_term
    )
    return (value, slope)


def slopes(mass, internal):
    deviation, departure_slope = departure(mass)
    warmth = internal / isochoric_warmth_coefficient
    for _ in range(NEWTON):
        root = jnp.sqrt(warmth)
        multiplier = 1.0 + acentric_coefficient_gradient * (1.0 - root)
        mismatch = isochoric_warmth_coefficient * warmth + deviation * multiplier - internal
        gradient = isochoric_warmth_coefficient - deviation * acentric_coefficient_gradient / (
            2.0 * root
        )
        warmth = warmth - mismatch / gradient
    root = jnp.sqrt(warmth)
    multiplier = 1.0 + acentric_coefficient_gradient * (1.0 - root)
    gradient = isochoric_warmth_coefficient - deviation * acentric_coefficient_gradient / (
        2.0 * root
    )
    energy = 1.0 / gradient
    return (-departure_slope * multiplier * energy, energy)


def lanes():
    return lax.broadcasted_iota(jnp.int32, (8, X), 1)


def tile(t):
    return slice(8 * t, 8 * t + 8)


def prep_kernel(
    q_hbm, mass_hbm, internal_hbm, velocity_hbm, coef_ref, pack_ref, rows_ref, corner_ref, q, mass, internal, sems
):
    copies = [
        pltpu.make_async_copy(src, dst, sems.at[i])
        for i, (src, dst) in enumerate(
            (
                (mass_hbm, mass),
                (internal_hbm, internal),
                (velocity_hbm, coef_ref.at[pl.ds(4, 2)]),
                (q_hbm, q),
            )
        )
    ]
    for copy in copies:
        copy.start()
    copies[0].wait()
    copies[1].wait()
    density, energy = slopes(mass[...], internal[...])
    coef_ref[0:2] = density
    coef_ref[2:4] = energy
    copies[2].wait()
    copies[3].wait()
    group = lanes() >> 3
    for t in range(Z // 8):
        for c in range(2):
            acc = q[2 * c, tile(t), :]
            for y in range(2):
                for k in range(K):
                    i = 8 * y + k
                    if i:
                        part = pltpu.roll(q[4 * k + 2 * c + y, tile(t), :], 8 * i, 1)
                        acc = jnp.where(group == i, part, acc)
            pack_ref[c, tile(t), :] = acc
        acc = jnp.where(group == 0, coef_ref[0, tile(t), :], 0.0)
        for i in range(1, NC):
            acc = jnp.where(group == i, pltpu.roll(coef_ref[i, tile(t), :], 8 * i, 1), acc)
        pack_ref[2, tile(t), :] = acc
    for n in range(3):
        corner_ref[n] = pack_ref[n, 0:8, :]
    for f in range(NA):
        rows_ref[f] = q[f, 0:8, :] if f < NF else coef_ref[f - NF, 0:8, :]


def pairs():
    return [(k, m, (k + m) % K) for k in range(K) for m in range(5 if k < 4 else 4)]


def columns(result, lane, red, extra, sets):
    row = lax.broadcasted_iota(jnp.int32, (8, X), 0)
    mine = ((lane >> 3) & 7) == row
    rows = []
    for n in range(len(sets)):
        for m in range(5):
            acc = red[5 * n + m]
            if extra is not None:
                part = extra[5 * n + m]
                for d in (4, 2, 1):
                    part = part + pltpu.roll(part, d, 0)
                acc = acc + jnp.where(mine, part, 0.0)
            rows.append(jnp.where(row < 4, acc, 0.0) if m == 4 else acc)
    if len(rows) % 2:
        rows.append(rows[-1])
    rows = jnp.concatenate(rows, axis=0)
    high, low = split(rows)
    last = (rows - high.astype(F32) - low.astype(F32)).astype(jnp.bfloat16)
    total = product(
        jnp.concatenate([high, low, last], axis=1), jnp.ones((3 * X, X), jnp.bfloat16)
    )
    for n, place in enumerate(sets):
        for m in range(5):
            at = 8 * (5 * n + m)
            result = jnp.where(lane == 8 * place + m, total[at : at + 8, :], result)
    return result


def put(red, n, k, acc):
    red[n, k : k + 1, :] = jnp.sum(acc, axis=0, keepdims=True)


def side_of(packed, i):
    return pltpu.roll(packed, X - 8 * i, 1) if i else packed


def fill(pair, lane):
    out = jnp.where(lane < 8, pair[0], 0.0)
    out = jnp.where((lane >= 64) & (lane < 72), pltpu.roll(pair[1], 64, 1), out)
    for d in (8, 16, 32):
        out = out + pltpu.roll(out, d, 1)
    return out


def each():
    return [(k, y) for k in range(K) for y in range(2)]


def last_columns(field, coef, last_ref, at, lane):
    group = lane >> 3
    got = []
    for c in range(2):
        acc = None
        for y in range(2):
            for k in range(K):
                i = 8 * y + k
                part = field(4 * k + 2 * c + y)
                part = pltpu.roll(part, (8 * i + 8) % X, 1) if i < 15 else part
                acc = part if i == 0 else jnp.where(group == i, part, acc)
        got.append(acc)
    full = [fill([pltpu.roll(coef(2 * n + y), 8, 1) for y in range(2)], lane) for n in range(3)]
    got.append(full[0] * got[0] + full[1] * got[1])
    for n, part in enumerate(got + full):
        last_ref[n, at : at + 8, :] = part


def own_kernel(q_ref, coef_ref, wm_ref, wp_ref, warm_ref, last_ref, sums_ref, red):
    lane = lanes()
    red[...] = jnp.zeros_like(red)
    for t in range(Z // 8):
        for k, y in each():
            warm_ref[2 * k + y, tile(t), :] = (
                coef_ref[y, tile(t), :] * q_ref[4 * k + y, tile(t), :]
                + coef_ref[2 + y, tile(t), :] * q_ref[4 * k + 2 + y, tile(t), :]
            )
        last_columns(
            lambda f: q_ref[f, tile(t), :], lambda n: coef_ref[n, tile(t), :],
            last_ref, 8 * t, lane,
        )
    for k, m, l in pairs():
        acc = jnp.zeros((8, X), F32)
        for p in range(4):
            for t in range(Z // 8):
                acc = acc + q_ref[4 * k + p, tile(t), :] * q_ref[4 * l + p, tile(t), :]
        put(red, m, k, acc)
    speed = jnp.zeros((8, X), F32)
    for y in range(2):
        for t in range(Z // 8):
            v = coef_ref[4 + y, tile(t), :]
            speed = speed + v * v
    result = jnp.where(lane == 40, jnp.sum(speed, axis=1, keepdims=True), 0.0)
    sums_ref[...] = columns(result, lane, red, None, (0,))


def join(side_ref, last_ref, packed, t, at, lane):
    rows = slice(at, at + 8)
    got = [side_ref[c, tile(t), :] for c in range(2)]
    third = side_ref[2, tile(t), :]
    full = [fill([side_of(third, 2 * n + y) for y in range(2)], lane) for n in range(3)]
    got.append(full[0] * got[0] + full[1] * got[1])
    for n, part in enumerate(got + full):
        packed[n, rows, 0:X] = last_ref[n, tile(t), :]
        packed[n, rows, X : 2 * X] = part


def split(x):
    high = x.astype(jnp.bfloat16)
    return high, (x - high.astype(F32)).astype(jnp.bfloat16)


def product(x, w):
    return jnp.dot(x, w, preferred_element_type=F32)


def rest(at, other):
    return 16.0 * (at(-1) + at(1) + other) - (at(-2) + at(2)) - 60.0 * at(0)


def main_rates(count, weights, r_at, e_at, t_at):
    def stack(at):
        rows = jnp.concatenate([at(i) for i in range(count)], axis=0)
        return jnp.concatenate(split(rows), axis=1)

    both = product(stack(r_at), weights[...])
    slope = product(stack(e_at), weights[:, 0:X])
    bend = product(stack(t_at), weights[:, X : 2 * X])
    out = []
    for i in range(count):
        rows = slice(8 * i, 8 * i + 8)
        out.append((both[rows, 0:X], both[rows, X:], slope[rows], bend[rows]))
    return out


def main_rate(speed, parts, r_at, t_at, r_other, t_other):
    slope_r, bend_r, slope_e, bend_t = parts
    rate_r = speed * slope_r + (viscosity / 12.0) * (bend_r + rest(r_at, r_other))
    rate_e = speed * slope_e + (conductivity / 12.0) * (bend_t + rest(t_at, t_other))
    return rate_r, rate_e


def turned(x):
    return jnp.concatenate([pltpu.roll(x[:, 0:X], 64, 1), pltpu.roll(x[:, X:], 64, 1)], axis=1)


def packed_rate(speed, weights, at):
    def along(n, w):
        high, low = split(at(n, 0))
        return product(high, weights[w]) + product(low, weights[w])

    rate_r = speed * along(0, 0) + (viscosity / 12.0) * (
        along(0, 1) + rest(lambda d: at(0, d), turned(at(0, 0)))
    )
    rate_e = speed * along(1, 0) + (conductivity / 12.0) * (
        along(2, 1) + rest(lambda d: at(2, d), turned(at(2, 0)))
    )
    return rate_r, rate_e


def packed_steps(packed, wp, pa, blocks, first, second, count, lane):
    src, dst, height = first
    rows = slice(src, src + height)
    got = packed_rate(
        packed[5, rows, :] * (-1.0 / 12.0), wp, lambda n, d: packed[n, src + d : src + d + height, :]
    )
    out = slice(dst, dst + height)
    pa[0, out, :] = got[0]
    pa[1, out, :] = got[1]
    pa[2, out, :] = packed[3, rows, :] * got[0] + packed[4, rows, :] * got[1]
    here, there = second
    rows = slice(here, here + count)
    got = packed_rate(
        packed[5, rows, :] * (-1.0 / 12.0),
        wp,
        lambda n, d: pa[n, there + d : there + d + count, :],
    )
    qp, ap, bp = blocks
    low = (lax.broadcasted_iota(jnp.int32, (count, X), 1) & 7) < 4
    for c in range(2):
        for dest, value in (
            (qp, packed[c, rows, :]),
            (ap, pa[c, there : there + count, :]),
            (bp, 0.5 * got[c]),
        ):
            dest[c] = jnp.where(low, value[:, X:], value[:, 0:X])


def main_sums(red, q_at, ad, bd, tiles):
    for k, m, l in pairs():
        acc = [jnp.zeros((8, X), F32)] * 4
        for p in range(4):
            for t in range(tiles):
                qk, ql = q_at(4 * k + p, t), q_at(4 * l + p, t)
                ak, bk = (v[4 * k + p, tile(t), :] for v in (ad, bd))
                al, bl = (v[4 * l + p, tile(t), :] for v in (ad, bd))
                acc[0] = acc[0] + (qk * al + ak * ql)
                acc[1] = acc[1] + (ak * al + (qk * bl + bk * ql))
                acc[2] = acc[2] + (ak * bl + bk * al)
                acc[3] = acc[3] + bk * bl
        for n in range(4):
            put(red, 5 * n + m, k, acc[n])


def packed_sums(extra, blocks, tiles, lane):
    acc = [jnp.zeros((8, X), F32) for _ in range(20)]
    for c in range(2):
        for t in range(tiles):
            q, a, b = (ref[c, tile(t), :] for ref in blocks)
            for m in range(5):

                def other(v, m=m):
                    if m == 0:
                        return v
                    near = pltpu.roll(v, X - 8 * m, 1)
                    return jnp.where((lane & 63) < 64 - 8 * m, near, pltpu.roll(v, 64 - 8 * m, 1))

                ql, al, bl = other(q), other(a), other(b)
                acc[m] = acc[m] + (q * al + a * ql)
                acc[5 + m] = acc[5 + m] + (a * al + (q * bl + b * ql))
                acc[10 + m] = acc[10 + m] + (a * bl + b * al)
                acc[15 + m] = acc[15 + m] + b * bl
    for n in range(20):
        extra[n] = acc[n]


def inside(rows):
    lane = lax.broadcasted_iota(jnp.int32, (rows, X), 1)
    return (lane >= 4) & (lane < 124)


def inner_kernel(
    q_ref, coef_ref, warm_ref, side_ref, last_ref, own_ref, below_ref, wm_ref, wp_ref,
    ad_ref, bd_ref, ap_ref, bp_ref, tail_ref, packed_ref, under_ref, kept_ref, sums_ref,
    packed, pa, qp, am, tm, red, extra,
):
    lane = lanes()
    red[...] = jnp.zeros_like(red)
    for t in range(Z // 8):
        join(side_ref, last_ref, packed, t, 8 * t, lane)
    packed_steps(packed, wp_ref, pa, (qp, ap_ref, bp_ref), (2, 2, 28), (4, 4), 24, lane)
    packed_sums(extra, (qp, ap_ref, bp_ref), 3, lane)
    for n in range(3):
        packed_ref[n] = pa[n, 22:30, :]
    for n in range(6):
        packed_ref[3 + n] = packed[n, 24:32, :]
        kept_ref[n] = coef_ref[n, 24:32, :]
    last_columns(lambda f: below_ref[f], lambda n: below_ref[NF + n], under_ref, 0, lane)
    keep = inside(8)

    def vectors(j, carry):
        planes = [(STEP * j + i, y) for i in range(STEP) for y in range(2)]
        order = [(k, y, r) for k, y in planes for r in (2, 10, 18, 22)]
        parts = main_rates(
            len(order),
            wm_ref,
            lambda i: q_ref[4 * order[i][0] + order[i][1], order[i][2] : order[i][2] + 8, :],
            lambda i: q_ref[4 * order[i][0] + 2 + order[i][1], order[i][2] : order[i][2] + 8, :],
            lambda i: warm_ref[2 * order[i][0] + order[i][1], order[i][2] : order[i][2] + 8, :],
        )
        for i, (k, y, r) in enumerate(order):
            rows = slice(r, r + 8)
            got = main_rate(
                coef_ref[4 + y, rows, :] * (-1.0 / 12.0),
                parts[i],
                lambda d: q_ref[4 * k + y, r + d : r + d + 8, :],
                lambda d: warm_ref[2 * k + y, r + d : r + d + 8, :],
                q_ref[4 * k + 1 - y, rows, :],
                warm_ref[2 * k + 1 - y, rows, :],
            )
            for c in range(2):
                am[k, 2 * c + y, rows, :] = got[c]
            tm[k, y, rows, :] = coef_ref[y, rows, :] * got[0] + coef_ref[2 + y, rows, :] * got[1]
        order = [(k, y, r) for k, y in planes for r in (4, 12, 20)]
        parts = main_rates(
            len(order),
            wm_ref,
            lambda i: am[order[i][0], order[i][1], order[i][2] : order[i][2] + 8, :],
            lambda i: am[order[i][0], 2 + order[i][1], order[i][2] : order[i][2] + 8, :],
            lambda i: tm[order[i][0], order[i][1], order[i][2] : order[i][2] + 8, :],
        )
        for i, (k, y, r) in enumerate(order):
            rows = slice(r, r + 8)
            got = main_rate(
                coef_ref[4 + y, rows, :] * (-1.0 / 12.0),
                parts[i],
                lambda d: am[k, y, r + d : r + d + 8, :],
                lambda d: tm[k, y, r + d : r + d + 8, :],
                am[k, 1 - y, rows, :],
                tm[k, 1 - y, rows, :],
            )
            for c in range(2):
                f = 4 * k + 2 * c + y
                bd_ref[f, r - 4 : r + 4, :] = jnp.where(keep, 0.5 * got[c], 0.0)
                ad_ref[f, r - 4 : r + 4, :] = jnp.where(keep, am[k, 2 * c + y, rows, :], 0.0)
        for k in [STEP * j + i for i in range(STEP)]:
            for p in range(4):
                tail_ref[4 * k + p] = am[k, p, 22:30, :]
        return carry

    lax.fori_loop(0, K // STEP, vectors, 0)
    main_sums(red, lambda f, t: q_ref[f, 8 * t + 4 : 8 * t + 12, :], ad_ref, bd_ref, 3)
    sums_ref[...] = columns(own_ref[...], lane, red, extra, range(1, 5))


def edge_kernel(
    q_ref, kept_ref, warm_ref, below_ref, corner_ref, last_ref, tail_ref, packed_ref, inner_ref, wm_ref, wp_ref,
    ad_ref, bd_ref, ap_ref, bp_ref, sums_ref,
    em, ec, wm, packed, pa, qp, am, tm, red, extra,
):
    lane = lanes()
    red[...] = jnp.zeros_like(red)
    for n in range(NC):
        ec[n, 0:8, :] = kept_ref[n]
        ec[n, 8:16, :] = below_ref[NF + n]
        packed[n, 0:8, :] = packed_ref[3 + n]
    join(corner_ref, last_ref, packed, 0, 8, lane)
    for n in range(3):
        pa[n, 0:8, :] = packed_ref[n]
    packed_steps(packed, wp_ref, pa, (qp, ap_ref, bp_ref), (6, 8, 8), (4, 6), 8, lane)
    packed_sums(extra, (qp, ap_ref, bp_ref), 1, lane)
    keep = inside(8)
    for k in range(K):
        base = 4 * k
        for p in range(4):
            em[base + p, 0:8, :] = q_ref[base + p, 24:32, :]
            em[base + p, 8:16, :] = below_ref[base + p]
            am[k, p, 0:8, :] = tail_ref[base + p]
        for y in range(2):
            wm[k, y, 0:8, :] = warm_ref[2 * k + y, 24:32, :]
            wm[k, y, 8:16, :] = (
                ec[y, 8:16, :] * below_ref[base + y] + ec[2 + y, 8:16, :] * below_ref[base + 2 + y]
            )
    order = each()
    parts = main_rates(
        16,
        wm_ref,
        lambda i: em[4 * order[i][0] + order[i][1], 6:14, :],
        lambda i: em[4 * order[i][0] + 2 + order[i][1], 6:14, :],
        lambda i: wm[order[i][0], order[i][1], 6:14, :],
    )
    for i, (k, y) in enumerate(order):
        got = main_rate(
            ec[4 + y, 6:14, :] * (-1.0 / 12.0),
            parts[i],
            lambda d: em[4 * k + y, 6 + d : 14 + d, :],
            lambda d: wm[k, y, 6 + d : 14 + d, :],
            em[4 * k + 1 - y, 6:14, :],
            wm[k, 1 - y, 6:14, :],
        )
        for c in range(2):
            am[k, 2 * c + y, 8:16, :] = got[c]
        tm[k, y, 8:16, :] = ec[y, 6:14, :] * got[0] + ec[2 + y, 6:14, :] * got[1]
        tm[k, y, 4:8, :] = (
            ec[y, 2:6, :] * am[k, y, 4:8, :] + ec[2 + y, 2:6, :] * am[k, 2 + y, 4:8, :]
        )
    parts = main_rates(
        16,
        wm_ref,
        lambda i: am[order[i][0], order[i][1], 6:14, :],
        lambda i: am[order[i][0], 2 + order[i][1], 6:14, :],
        lambda i: tm[order[i][0], order[i][1], 6:14, :],
    )
    for i, (k, y) in enumerate(order):
        got = main_rate(
            ec[4 + y, 4:12, :] * (-1.0 / 12.0),
            parts[i],
            lambda d: am[k, y, 6 + d : 14 + d, :],
            lambda d: tm[k, y, 6 + d : 14 + d, :],
            am[k, 1 - y, 6:14, :],
            tm[k, 1 - y, 6:14, :],
        )
        for c in range(2):
            f = 4 * k + 2 * c + y
            bd_ref[f] = jnp.where(keep, 0.5 * got[c], 0.0)
            ad_ref[f] = jnp.where(keep, am[k, 2 * c + y, 6:14, :], 0.0)
    main_sums(red, lambda f, t: em[f, 4:12, :], ad_ref, bd_ref, 1)
    result = columns(jnp.zeros((8, X), F32), lane, red, extra, range(1, 5)) + inner_ref[...]
    for n in range(sums_ref.shape[0]):
        sums_ref[n] = result


def give_kernel(ap_ref, bp_ref, ape_ref, bpe_ref, out_ref):
    for n, (ref, edge) in enumerate(((ap_ref, ape_ref), (bp_ref, bpe_ref))):
        for c in range(2):
            out_ref[n, c, 0:24, :] = ref[c]
            out_ref[n, c, 24:32, :] = edge[c]


def place_kernel(ad_ref, bd_ref, ade_ref, bde_ref, mine_ref, got_ref, a_ref, b_ref, down_ref):
    lane = lanes()
    strip = (lane < 4) | (lane >= 124)
    low = (lane & 7) < 4
    for n, (ref, edge, out) in enumerate(((ad_ref, ade_ref, a_ref), (bd_ref, bde_ref, b_ref))):
        for c in range(2):
            for t in range(Z // 8):
                mine = pltpu.roll(mine_ref[n, c, tile(t), :], X - 8, 1)
                both = jnp.where(low, got_ref[n, c, tile(t), :], mine)
                for y in range(2):
                    for k in range(K):
                        f = 4 * k + 2 * c + y
                        part = ref[f, tile(t), :] if t < 3 else edge[f]
                        part = jnp.where(strip, side_of(both, 8 * y + k), part)
                        if t < 3:
                            out[f, 8 * t + 4 : 8 * t + 12, :] = part
                        else:
                            out[f, 28:32, :] = part[0:4, :]
                            out[f, 0:4, :] = jnp.zeros((4, X), F32)
                            r = 4 * (NF * n + f)
                            down_ref[r : r + 4, :] = part[4:8, :]


def finish_kernel(cells, q_ref, a_ref, b_ref, above_ref, sums_ref, out_ref, growth_ref, first):
    lane = lanes()
    row = lax.broadcasted_iota(jnp.int32, (8, X), 0)
    for n, ref in enumerate((a_ref, b_ref)):
        for f in range(NF):
            r = 4 * (NF * n + f)
            first[n, f, 0:4, :] = above_ref[r : r + 4, :]
            first[n, f, 4:8, :] = ref[f, 4:8, :]
    total = sums_ref[0]
    for n in range(1, sums_ref.shape[0]):
        total = total + sums_ref[n]
    speed = jnp.broadcast_to(jnp.sum(total[:, 40:41], axis=0, keepdims=True), (8, X))
    step = courant_number / jnp.sqrt(speed * (1.0 / cells) + 1e-05)
    gram = total
    power = step
    for n in range(1, 5):
        gram = gram + power * pltpu.roll(total, X - 8 * n, 1)
        power = power * step
    gram = gram * (1.0 / (2.0 * cells))
    cols = [jnp.broadcast_to(gram[:, m : m + 1], (8, X)) for m in range(5)]

    def entry(i, j):
        k, m = (j, i - j) if i - j <= 4 else (i, j - i + K)
        if m == 4:
            k = min(i, j)
        return jnp.broadcast_to(cols[m][k : k + 1, :], (8, X))

    low = [[None] * K for _ in range(K)]
    inv_diag = []
    for j in range(K):
        d = entry(j, j)
        for p in range(j):
            d = d - low[j][p] * low[j][p]
        root = jnp.sqrt(d)
        low[j][j] = root
        inv_diag.append(1.0 / root)
        for i in range(j + 1, K):
            v = entry(i, j)
            for p in range(j):
                v = v - low[i][p] * low[j][p]
            low[i][j] = v * inv_diag[j]
    inverse = [[None] * K for _ in range(K)]
    for j in range(K):
        inverse[j][j] = inv_diag[j]
        for i in range(j + 1, K):
            v = low[i][j] * inverse[j][j]
            for p in range(j + 1, i):
                v = v + low[i][p] * inverse[p][j]
            inverse[i][j] = -v * inv_diag[i]
    growth = jnp.zeros((8, X), F32)
    for i in range(K):
        for j in range(i + 1):
            growth = jnp.where((row == j) & (lane == i), low[i][j], growth)
    growth_ref[...] = growth
    square = step * step
    for p in range(4):
        for t in range(Z // 8):
            adv = []
            for k in range(K):
                f = 4 * k + p
                a, b = (
                    (first[0, f], first[1, f])
                    if t == 0
                    else (a_ref[f, tile(t), :], b_ref[f, tile(t), :])
                )
                adv.append(q_ref[f, tile(t), :] + step * a + square * b)
            for k in range(K):
                v = inverse[k][0] * adv[0]
                for j in range(1, k + 1):
                    v = v + inverse[k][j] * adv[j]
                out_ref[4 * k + p, tile(t), :] = v


def call(body, outs, scratch=(), cost=2000000, limit=24, **more):
    shapes = [jax.ShapeDtypeStruct(s, F32) for s in outs]
    return pl.pallas_call(
        body,
        out_shape=shapes,
        scratch_shapes=[pltpu.VMEM(s, F32) if isinstance(s, tuple) else s for s in scratch],
        compiler_params=pltpu.CompilerParams(vmem_limit_bytes=limit * 1024 * 1024),
        cost_estimate=pl.CostEstimate(flops=cost, bytes_accessed=cost, transcendentals=0),
        **more,
    )


def ring(array, axes, step):
    size = lax.axis_size(axes)
    return lax.ppermute(array, axes, [(i, (i + step) % size) for i in range(size)])


def diagonal(array):
    gx, gz = lax.axis_size(GX), lax.axis_size(GZ)
    pairs_of = [
        (i * gz + j, (i - 1) % gx * gz + (j - 1) % gz) for i in range(gx) for j in range(gz)
    ]
    return lax.ppermute(array, GX + GZ, pairs_of)


def gathered(array, axes):
    return lax.all_to_all(array, axes, 0, 0)


def per_device(tangents, mass, internal, velocity):
    cells = float(2 * Z * X * lax.axis_size(GX) * lax.axis_size(GZ))
    near, far = lax.axis_size(NEAR), lax.axis_size(FAR)
    whole, inner, edge = (NF, Z, X), (NF, 24, X), (NF, 8, X)
    half, small, red = (2 * K, Z, X), (3, Z, X), (20, 8, X)
    wm, wp = (jnp.asarray(w) for w in bands())
    q = tangents.reshape(whole)
    coef, pack, rows, corner = call(
        prep_kernel,
        [(NC, Z, X), small, (NA, 8, X), (3, 8, X)],
        [whole, (2, Z, X), (2, Z, X), pltpu.SemaphoreType.DMA((4,))],
        limit=60,
        in_specs=[pl.BlockSpec(memory_space=pl.ANY)] * 4,
    )(q, mass, internal, velocity)
    side = ring(pack, GX, -1)
    below = ring(rows, GZ, -1)
    corner = diagonal(corner)
    warm, last, own = call(own_kernel, [half, (6, Z, X), (8, X)], [(5, 8, X)])(
        q, coef, wm, wp
    )
    ad, bd, ap, bp, tail, packed, under, kept, part = call(
        inner_kernel,
        [inner, inner, (2, 24, X), (2, 24, X), edge, (9, 8, 2 * X), (6, 8, X), (6, 8, X), (8, X)],
        [(6, Z, 2 * X), (3, Z, 2 * X), (2, 24, X), (K, 4, Z, X), (K, 2, Z, X), red, red],
    )(q, coef, warm, side, last, own, below, wm, wp)
    ade, bde, ape, bpe, sums = call(
        edge_kernel,
        [edge, edge, (2, 8, X), (2, 8, X), (near, 8, X)],
        [(NF, 16, X), (NC, 16, X), (K, 2, 16, X), (6, 16, 2 * X), (3, 16, 2 * X), (2, 8, X)]
        + [(K, 4, 16, X), (K, 2, 16, X), red, red],
    )(q, kept, warm, below, corner, under, tail, packed, part, wm, wp)
    sums = jnp.sum(gathered(sums, NEAR), axis=0)
    (give,) = call(give_kernel, [(2, 2, Z, X)])(ap, bp, ape, bpe)
    got = ring(give, GX, 1)
    sums, got = lax.optimization_barrier((sums, got))
    sums = gathered(jnp.broadcast_to(sums, (far, 8, X)), FAR)
    a, b, down = call(place_kernel, [whole, whole, (8 * NF, X)])(ad, bd, ade, bde, give, got)
    above = ring(down, GZ, 1)
    out, growth = call(
        functools.partial(finish_kernel, cells), [whole, (8, X)], [(2, NF, 8, X)]
    )(q, a, b, above, sums)
    return (out.reshape(tangents.shape), growth[:, :K])


def solution(mesh):
    gx, gz = mesh.devices.shape
    fine = Mesh(mesh.devices.reshape(gx // 4, 4, gz // 4, 4), GX + GZ)
    in_specs = (P(None, None, None, GZ, GX),) + (P(None, GZ, GX),) * 3
    out_specs = (P(None, None, None, GZ, GX), P())
    return jax.shard_map(
        per_device, mesh=fine, in_specs=in_specs, out_specs=out_specs, check_vma=False
    )
```

```python
import functools

import jax
import jax.numpy as jnp
import numpy as np
from jax import lax
from jax.experimental import pallas as pl
from jax.experimental.pallas import tpu as pltpu
from jax.sharding import Mesh, PartitionSpec as P

NEWTON = 4
isochoric_warmth_coefficient = 3.0
attraction = 0.5
acentric_coefficient_gradient = 0.6
covolume = 0.15
root_two = 1.4142135623730951
viscosity = 0.2
conductivity = 1.0
courant_number = 0.5

K = 8
NF = 4 * K
NC = 6
NA = NF + NC
Z = 32
X = 128
GX = ("xh", "xl")
GZ = ("zh", "zl")
NEAR = ("xl", "zl")
FAR = ("xh", "zh")
F32 = jnp.float32
STEP = 4


def bands():
    first = {-2: 1.0, -1: -8.0, 1: 8.0, 2: -1.0}
    second = {-2: -1.0, -1: 16.0, 0: -30.0, 1: 16.0, 2: -1.0}
    main, packed = [], []
    for band in (first, second):
        w, v = np.zeros((X, X), np.float32), np.zeros((2 * X, 2 * X), np.float32)
        for d, value in band.items():
            for j in range(X):
                if 0 <= j + d < X:
                    w[j + d, j] = value
            for g in range(16):
                for j in range(16):
                    if 0 <= j + d < 16:
                        at = [X * (c // 8) + 8 * g + c % 8 for c in (j + d, j)]
                        v[at[0], at[1]] = value
        main.append(np.concatenate([w, w]))
        packed.append(v)
    return [
        np.concatenate(main, axis=1).astype(jnp.bfloat16),
        *(v.astype(jnp.bfloat16) for v in packed),
    ]


def departure(cell_mass_concentration):
    low_term = 1.0 + (1.0 - root_two) * covolume * cell_mass_concentration
    high_term = 1.0 + (1.0 + root_two) * covolume * cell_mass_concentration
    factor = attraction * (1.0 + acentric_coefficient_gradient) / (2.0 * root_two * covolume)
    value = factor * (jnp.log(low_term) - jnp.log(high_term))
    slope = factor * (
        (1.0 - root_two) * covolume / low_term - (1.0 + root_two) * covolume / high_term
    )
    return (value, slope)


def slopes(mass, internal):
    deviation, departure_slope = departure(mass)
    warmth = internal / isochoric_warmth_coefficient
    for _ in range(NEWTON):
        root = jnp.sqrt(warmth)
        multiplier = 1.0 + acentric_coefficient_gradient * (1.0 - root)
        mismatch = isochoric_warmth_coefficient * warmth + deviation * multiplier - internal
        gradient = isochoric_warmth_coefficient - deviation * acentric_coefficient_gradient / (
            2.0 * root
        )
        warmth = warmth - mismatch / gradient
    root = jnp.sqrt(warmth)
    multiplier = 1.0 + acentric_coefficient_gradient * (1.0 - root)
    gradient = isochoric_warmth_coefficient - deviation * acentric_coefficient_gradient / (
        2.0 * root
    )
    energy = 1.0 / gradient
    return (-departure_slope * multiplier * energy, energy)


def lanes():
    return lax.broadcasted_iota(jnp.int32, (8, X), 1)


def tile(t):
    return slice(8 * t, 8 * t + 8)


def prep_kernel(
    q_hbm, mass_hbm, internal_hbm, velocity_hbm, coef_ref, pack_ref, rows_ref, corner_ref, q, mass, internal, sems
):
    copies = [
        pltpu.make_async_copy(src, dst, sems.at[i])
        for i, (src, dst) in enumerate(
            (
                (mass_hbm, mass),
                (internal_hbm, internal),
                (velocity_hbm, coef_ref.at[pl.ds(4, 2)]),
                (q_hbm, q),
            )
        )
    ]
    for copy in copies:
        copy.start()
    copies[0].wait()
    copies[1].wait()
    density, energy = slopes(mass[...], internal[...])
    coef_ref[0:2] = density
    coef_ref[2:4] = energy
    copies[2].wait()
    copies[3].wait()
    group = lanes() >> 3
    for t in range(Z // 8):
        for c in range(2):
            acc = q[2 * c, tile(t), :]
            for y in range(2):
                for k in range(K):
                    i = 8 * y + k
                    if i:
                        part = pltpu.roll(q[4 * k + 2 * c + y, tile(t), :], 8 * i, 1)
                        acc = jnp.where(group == i, part, acc)
            pack_ref[c, tile(t), :] = acc
        acc = jnp.where(group == 0, coef_ref[0, tile(t), :], 0.0)
        for i in range(1, NC):
            acc = jnp.where(group == i, pltpu.roll(coef_ref[i, tile(t), :], 8 * i, 1), acc)
        pack_ref[2, tile(t), :] = acc
    for n in range(3):
        corner_ref[n] = pack_ref[n, 0:8, :]
    for f in range(NA):
        rows_ref[f] = q[f, 0:8, :] if f < NF else coef_ref[f - NF, 0:8, :]


def pairs():
    return [(k, m, (k + m) % K) for k in range(K) for m in range(5 if k < 4 else 4)]


def columns(result, lane, red, extra, sets):
    row = lax.broadcasted_iota(jnp.int32, (8, X), 0)
    mine = ((lane >> 3) & 7) == row
    rows = []
    for n in range(len(sets)):
        for m in range(5):
            acc = red[5 * n + m]
            if extra is not None:
                part = extra[5 * n + m]
                for d in (4, 2, 1):
                    part = part + pltpu.roll(part, d, 0)
                acc = acc + jnp.where(mine, part, 0.0)
            rows.append(jnp.where(row < 4, acc, 0.0) if m == 4 else acc)
    if len(rows) % 2:
        rows.append(rows[-1])
    rows = jnp.concatenate(rows, axis=0)
    high, low = split(rows)
    last = (rows - high.astype(F32) - low.astype(F32)).astype(jnp.bfloat16)
    total = product(
        jnp.concatenate([high, low, last], axis=1), jnp.ones((3 * X, X), jnp.bfloat16)
    )
    for n, place in enumerate(sets):
        for m in range(5):
            at = 8 * (5 * n + m)
            result = jnp.where(lane == 8 * place + m, total[at : at + 8, :], result)
    return result


def put(red, n, k, acc):
    red[n, k : k + 1, :] = jnp.sum(acc, axis=0, keepdims=True)


def side_of(packed, i):
    return pltpu.roll(packed, X - 8 * i, 1) if i else packed


def fill(pair, lane):
    out = jnp.where(lane < 8, pair[0], 0.0)
    out = jnp.where((lane >= 64) & (lane < 72), pltpu.roll(pair[1], 64, 1), out)
    for d in (8, 16, 32):
        out = out + pltpu.roll(out, d, 1)
    return out


def each():
    return [(k, y) for k in range(K) for y in range(2)]


def last_columns(field, coef, last_ref, at, lane):
    group = lane >> 3
    got = []
    for c in range(2):
        acc = None
        for y in range(2):
            for k in range(K):
                i = 8 * y + k
                part = field(4 * k + 2 * c + y)
                part = pltpu.roll(part, (8 * i + 8) % X, 1) if i < 15 else part
                acc = part if i == 0 else jnp.where(group == i, part, acc)
        got.append(acc)
    full = [fill([pltpu.roll(coef(2 * n + y), 8, 1) for y in range(2)], lane) for n in range(3)]
    got.append(full[0] * got[0] + full[1] * got[1])
    for n, part in enumerate(got + full):
        last_ref[n, at : at + 8, :] = part


def square_kernel(q_ref, sums_ref, red):
    red[...] = jnp.zeros_like(red)
    for k, m, l in pairs():
        acc = jnp.zeros((8, X), F32)
        for p in range(4):
            for t in range(Z // 8):
                acc = acc + q_ref[4 * k + p, tile(t), :] * q_ref[4 * l + p, tile(t), :]
        put(red, m, k, acc)
    sums_ref[...] = columns(jnp.zeros((8, X), F32), lanes(), red, None, (0,))


def own_kernel(q_ref, coef_ref, square_ref, warm_ref, last_ref, sums_ref):
    lane = lanes()
    for t in range(Z // 8):
        for k, y in each():
            warm_ref[2 * k + y, tile(t), :] = (
                coef_ref[y, tile(t), :] * q_ref[4 * k + y, tile(t), :]
                + coef_ref[2 + y, tile(t), :] * q_ref[4 * k + 2 + y, tile(t), :]
            )
        last_columns(
            lambda f: q_ref[f, tile(t), :], lambda n: coef_ref[n, tile(t), :],
            last_ref, 8 * t, lane,
        )
    speed = jnp.zeros((8, X), F32)
    for y in range(2):
        for t in range(Z // 8):
            v = coef_ref[4 + y, tile(t), :]
            speed = speed + v * v
    total = jnp.sum(speed, axis=1, keepdims=True)
    sums_ref[...] = jnp.where(lane == 40, total, square_ref[...])


def join(side_ref, last_ref, packed, t, at, lane):
    rows = slice(at, at + 8)
    got = [side_ref[c, tile(t), :] for c in range(2)]
    third = side_ref[2, tile(t), :]
    full = [fill([side_of(third, 2 * n + y) for y in range(2)], lane) for n in range(3)]
    got.append(full[0] * got[0] + full[1] * got[1])
    for n, part in enumerate(got + full):
        packed[n, rows, 0:X] = last_ref[n, tile(t), :]
        packed[n, rows, X : 2 * X] = part


def split(x):
    high = x.astype(jnp.bfloat16)
    return high, (x - high.astype(F32)).astype(jnp.bfloat16)


def product(x, w):
    return jnp.dot(x, w, preferred_element_type=F32)


def rest(at, other):
    return 16.0 * (at(-1) + at(1) + other) - (at(-2) + at(2)) - 60.0 * at(0)


def main_rates(count, weights, r_at, e_at, t_at):
    def stack(at):
        rows = jnp.concatenate([at(i) for i in range(count)], axis=0)
        return jnp.concatenate(split(rows), axis=1)

    both = product(stack(r_at), weights[...])
    slope = product(stack(e_at), weights[:, 0:X])
    bend = product(stack(t_at), weights[:, X : 2 * X])
    out = []
    for i in range(count):
        rows = slice(8 * i, 8 * i + 8)
        out.append((both[rows, 0:X], both[rows, X:], slope[rows], bend[rows]))
    return out


def main_rate(speed, parts, r_at, t_at, r_other, t_other):
    slope_r, bend_r, slope_e, bend_t = parts
    rate_r = speed * slope_r + (viscosity / 12.0) * (bend_r + rest(r_at, r_other))
    rate_e = speed * slope_e + (conductivity / 12.0) * (bend_t + rest(t_at, t_other))
    return rate_r, rate_e


def turned(x):
    return jnp.concatenate([pltpu.roll(x[:, 0:X], 64, 1), pltpu.roll(x[:, X:], 64, 1)], axis=1)


def packed_rate(speed, weights, at):
    def along(n, w):
        high, low = split(at(n, 0))
        return product(high, weights[1 + w]) + product(low, weights[1 + w])

    rate_r = speed * along(0, 0) + (viscosity / 12.0) * (
        along(0, 1) + rest(lambda d: at(0, d), turned(at(0, 0)))
    )
    rate_e = speed * along(1, 0) + (conductivity / 12.0) * (
        along(2, 1) + rest(lambda d: at(2, d), turned(at(2, 0)))
    )
    return rate_r, rate_e


def packed_steps(packed, wp, pa, blocks, first, second, count, lane):
    src, dst, height = first
    rows = slice(src, src + height)
    got = packed_rate(
        packed[5, rows, :] * (-1.0 / 12.0), wp, lambda n, d: packed[n, src + d : src + d + height, :]
    )
    out = slice(dst, dst + height)
    pa[0, out, :] = got[0]
    pa[1, out, :] = got[1]
    pa[2, out, :] = packed[3, rows, :] * got[0] + packed[4, rows, :] * got[1]
    here, there = second
    rows = slice(here, here + count)
    got = packed_rate(
        packed[5, rows, :] * (-1.0 / 12.0),
        wp,
        lambda n, d: pa[n, there + d : there + d + count, :],
    )
    qp, ap, bp = blocks
    low = (lax.broadcasted_iota(jnp.int32, (count, X), 1) & 7) < 4
    for c in range(2):
        for dest, value in (
            (qp, packed[c, rows, :]),
            (ap, pa[c, there : there + count, :]),
            (bp, 0.5 * got[c]),
        ):
            dest[c] = jnp.where(low, value[:, X:], value[:, 0:X])


def main_sums(red, q_at, ad, bd, tiles):
    for k, m, l in pairs():
        acc = [jnp.zeros((8, X), F32)] * 4
        for p in range(4):
            for t in range(tiles):
                qk, ql = q_at(4 * k + p, t), q_at(4 * l + p, t)
                ak, bk = (v[4 * k + p, tile(t), :] for v in (ad, bd))
                al, bl = (v[4 * l + p, tile(t), :] for v in (ad, bd))
                acc[0] = acc[0] + (qk * al + ak * ql)
                acc[1] = acc[1] + (ak * al + (qk * bl + bk * ql))
                acc[2] = acc[2] + (ak * bl + bk * al)
                acc[3] = acc[3] + bk * bl
        for n in range(4):
            put(red, 5 * n + m, k, acc[n])


def packed_sums(extra, blocks, tiles, lane):
    acc = [jnp.zeros((8, X), F32) for _ in range(20)]
    for c in range(2):
        for t in range(tiles):
            q, a, b = (ref[c, tile(t), :] for ref in blocks)
            for m in range(5):

                def other(v, m=m):
                    if m == 0:
                        return v
                    near = pltpu.roll(v, X - 8 * m, 1)
                    return jnp.where((lane & 63) < 64 - 8 * m, near, pltpu.roll(v, 64 - 8 * m, 1))

                ql, al, bl = other(q), other(a), other(b)
                acc[m] = acc[m] + (q * al + a * ql)
                acc[5 + m] = acc[5 + m] + (a * al + (q * bl + b * ql))
                acc[10 + m] = acc[10 + m] + (a * bl + b * al)
                acc[15 + m] = acc[15 + m] + b * bl
    for n in range(20):
        extra[n] = acc[n]


def inside(rows):
    lane = lax.broadcasted_iota(jnp.int32, (rows, X), 1)
    return (lane >= 4) & (lane < 124)


def inner_kernel(
    q_ref, coef_ref, warm_ref, side_ref, last_ref, own_ref, below_ref, w_ref,
    ad_ref, bd_ref, ap_ref, bp_ref, tail_ref, packed_ref, under_ref, kept_ref, sums_ref,
    packed, pa, qp, am, tm, red, extra,
):
    lane = lanes()
    red[...] = jnp.zeros_like(red)
    for t in range(Z // 8):
        join(side_ref, last_ref, packed, t, 8 * t, lane)
    packed_steps(packed, w_ref, pa, (qp, ap_ref, bp_ref), (2, 2, 28), (4, 4), 24, lane)
    packed_sums(extra, (qp, ap_ref, bp_ref), 3, lane)
    for n in range(3):
        packed_ref[n] = pa[n, 22:30, :]
    for n in range(6):
        packed_ref[3 + n] = packed[n, 24:32, :]
        kept_ref[n] = coef_ref[n, 24:32, :]
    last_columns(lambda f: below_ref[f], lambda n: below_ref[NF + n], under_ref, 0, lane)
    keep = inside(8)

    def vectors(j, carry):
        planes = [(STEP * j + i, y) for i in range(STEP) for y in range(2)]
        order = [(k, y, r) for k, y in planes for r in (2, 10, 18, 22)]
        parts = main_rates(
            len(order),
            w_ref.at[0],
            lambda i: q_ref[4 * order[i][0] + order[i][1], order[i][2] : order[i][2] + 8, :],
            lambda i: q_ref[4 * order[i][0] + 2 + order[i][1], order[i][2] : order[i][2] + 8, :],
            lambda i: warm_ref[2 * order[i][0] + order[i][1], order[i][2] : order[i][2] + 8, :],
        )
        for i, (k, y, r) in enumerate(order):
            rows = slice(r, r + 8)
            got = main_rate(
                coef_ref[4 + y, rows, :] * (-1.0 / 12.0),
                parts[i],
                lambda d: q_ref[4 * k + y, r + d : r + d + 8, :],
                lambda d: warm_ref[2 * k + y, r + d : r + d + 8, :],
                q_ref[4 * k + 1 - y, rows, :],
                warm_ref[2 * k + 1 - y, rows, :],
            )
            for c in range(2):
                am[k, 2 * c + y, rows, :] = got[c]
            tm[k, y, rows, :] = coef_ref[y, rows, :] * got[0] + coef_ref[2 + y, rows, :] * got[1]
        order = [(k, y, r) for k, y in planes for r in (4, 12, 20)]
        parts = main_rates(
            len(order),
            w_ref.at[0],
            lambda i: am[order[i][0], order[i][1], order[i][2] : order[i][2] + 8, :],
            lambda i: am[order[i][0], 2 + order[i][1], order[i][2] : order[i][2] + 8, :],
            lambda i: tm[order[i][0], order[i][1], order[i][2] : order[i][2] + 8, :],
        )
        for i, (k, y, r) in enumerate(order):
            rows = slice(r, r + 8)
            got = main_rate(
                coef_ref[4 + y, rows, :] * (-1.0 / 12.0),
                parts[i],
                lambda d: am[k, y, r + d : r + d + 8, :],
                lambda d: tm[k, y, r + d : r + d + 8, :],
                am[k, 1 - y, rows, :],
                tm[k, 1 - y, rows, :],
            )
            for c in range(2):
                f = 4 * k + 2 * c + y
                bd_ref[f, r - 4 : r + 4, :] = jnp.where(keep, 0.5 * got[c], 0.0)
                ad_ref[f, r - 4 : r + 4, :] = jnp.where(keep, am[k, 2 * c + y, rows, :], 0.0)
        for k in [STEP * j + i for i in range(STEP)]:
            for p in range(4):
                tail_ref[4 * k + p] = am[k, p, 22:30, :]
        return carry

    lax.fori_loop(0, K // STEP, vectors, 0)
    main_sums(red, lambda f, t: q_ref[f, 8 * t + 4 : 8 * t + 12, :], ad_ref, bd_ref, 3)
    sums_ref[...] = columns(own_ref[...], lane, red, extra, range(1, 5))


def edge_kernel(
    q_ref, kept_ref, warm_ref, below_ref, corner_ref, last_ref, tail_ref, packed_ref, inner_ref, w_ref,
    ad_ref, bd_ref, ap_ref, bp_ref, sums_ref,
    em, ec, wm, packed, pa, qp, am, tm, red, extra,
):
    lane = lanes()
    red[...] = jnp.zeros_like(red)
    for n in range(NC):
        ec[n, 0:8, :] = kept_ref[n]
        ec[n, 8:16, :] = below_ref[NF + n]
        packed[n, 0:8, :] = packed_ref[3 + n]
    join(corner_ref, last_ref, packed, 0, 8, lane)
    for n in range(3):
        pa[n, 0:8, :] = packed_ref[n]
    packed_steps(packed, w_ref, pa, (qp, ap_ref, bp_ref), (6, 8, 8), (4, 6), 8, lane)
    packed_sums(extra, (qp, ap_ref, bp_ref), 1, lane)
    keep = inside(8)
    for k in range(K):
        base = 4 * k
        for p in range(4):
            em[base + p, 0:8, :] = q_ref[base + p, 24:32, :]
            em[base + p, 8:16, :] = below_ref[base + p]
            am[k, p, 0:8, :] = tail_ref[base + p]
        for y in range(2):
            wm[k, y, 0:8, :] = warm_ref[2 * k + y, 24:32, :]
            wm[k, y, 8:16, :] = (
                ec[y, 8:16, :] * below_ref[base + y] + ec[2 + y, 8:16, :] * below_ref[base + 2 + y]
            )
    order = each()
    parts = main_rates(
        16,
        w_ref.at[0],
        lambda i: em[4 * order[i][0] + order[i][1], 6:14, :],
        lambda i: em[4 * order[i][0] + 2 + order[i][1], 6:14, :],
        lambda i: wm[order[i][0], order[i][1], 6:14, :],
    )
    for i, (k, y) in enumerate(order):
        got = main_rate(
            ec[4 + y, 6:14, :] * (-1.0 / 12.0),
            parts[i],
            lambda d: em[4 * k + y, 6 + d : 14 + d, :],
            lambda d: wm[k, y, 6 + d : 14 + d, :],
            em[4 * k + 1 - y, 6:14, :],
            wm[k, 1 - y, 6:14, :],
        )
        for c in range(2):
            am[k, 2 * c + y, 8:16, :] = got[c]
        tm[k, y, 8:16, :] = ec[y, 6:14, :] * got[0] + ec[2 + y, 6:14, :] * got[1]
        tm[k, y, 4:8, :] = (
            ec[y, 2:6, :] * am[k, y, 4:8, :] + ec[2 + y, 2:6, :] * am[k, 2 + y, 4:8, :]
        )
    parts = main_rates(
        16,
        w_ref.at[0],
        lambda i: am[order[i][0], order[i][1], 6:14, :],
        lambda i: am[order[i][0], 2 + order[i][1], 6:14, :],
        lambda i: tm[order[i][0], order[i][1], 6:14, :],
    )
    for i, (k, y) in enumerate(order):
        got = main_rate(
            ec[4 + y, 4:12, :] * (-1.0 / 12.0),
            parts[i],
            lambda d: am[k, y, 6 + d : 14 + d, :],
            lambda d: tm[k, y, 6 + d : 14 + d, :],
            am[k, 1 - y, 6:14, :],
            tm[k, 1 - y, 6:14, :],
        )
        for c in range(2):
            f = 4 * k + 2 * c + y
            bd_ref[f] = jnp.where(keep, 0.5 * got[c], 0.0)
            ad_ref[f] = jnp.where(keep, am[k, 2 * c + y, 6:14, :], 0.0)
    main_sums(red, lambda f, t: em[f, 4:12, :], ad_ref, bd_ref, 1)
    result = columns(jnp.zeros((8, X), F32), lane, red, extra, range(1, 5)) + inner_ref[...]
    for n in range(sums_ref.shape[0]):
        sums_ref[n] = result


def give_kernel(ap_ref, bp_ref, ape_ref, bpe_ref, out_ref):
    for n, (ref, edge) in enumerate(((ap_ref, ape_ref), (bp_ref, bpe_ref))):
        for c in range(2):
            out_ref[n, c, 0:24, :] = ref[c]
            out_ref[n, c, 24:32, :] = edge[c]


def place_kernel(ad_ref, bd_ref, ade_ref, bde_ref, mine_ref, got_ref, a_ref, b_ref, down_ref):
    lane = lanes()
    strip = (lane < 4) | (lane >= 124)
    low = (lane & 7) < 4
    for n, (ref, edge, out) in enumerate(((ad_ref, ade_ref, a_ref), (bd_ref, bde_ref, b_ref))):
        for c in range(2):
            for t in range(Z // 8):
                mine = pltpu.roll(mine_ref[n, c, tile(t), :], X - 8, 1)
                both = jnp.where(low, got_ref[n, c, tile(t), :], mine)
                for y in range(2):
                    for k in range(K):
                        f = 4 * k + 2 * c + y
                        part = ref[f, tile(t), :] if t < 3 else edge[f]
                        part = jnp.where(strip, side_of(both, 8 * y + k), part)
                        if t < 3:
                            out[f, 8 * t + 4 : 8 * t + 12, :] = part
                        else:
                            out[f, 28:32, :] = part[0:4, :]
                            out[f, 0:4, :] = jnp.zeros((4, X), F32)
                            r = 4 * (NF * n + f)
                            down_ref[r : r + 4, :] = part[4:8, :]


def finish_kernel(cells, q_ref, a_ref, b_ref, above_ref, sums_ref, out_hbm, growth_ref, first, out, sems):
    lane = lanes()
    row = lax.broadcasted_iota(jnp.int32, (8, X), 0)
    for n, ref in enumerate((a_ref, b_ref)):
        for f in range(NF):
            r = 4 * (NF * n + f)
            first[n, f, 0:4, :] = above_ref[r : r + 4, :]
            first[n, f, 4:8, :] = ref[f, 4:8, :]
    total = sums_ref[0]
    for n in range(1, sums_ref.shape[0]):
        total = total + sums_ref[n]
    speed = jnp.broadcast_to(jnp.sum(total[:, 40:41], axis=0, keepdims=True), (8, X))
    step = courant_number / jnp.sqrt(speed * (1.0 / cells) + 1e-05)
    gram = total
    power = step
    for n in range(1, 5):
        gram = gram + power * pltpu.roll(total, X - 8 * n, 1)
        power = power * step
    gram = gram * (1.0 / (2.0 * cells))
    cols = [jnp.broadcast_to(gram[:, m : m + 1], (8, X)) for m in range(5)]

    def entry(i, j):
        k, m = (j, i - j) if i - j <= 4 else (i, j - i + K)
        if m == 4:
            k = min(i, j)
        return jnp.broadcast_to(cols[m][k : k + 1, :], (8, X))

    low = [[None] * K for _ in range(K)]
    inv_diag = []
    for j in range(K):
        d = entry(j, j)
        for p in range(j):
            d = d - low[j][p] * low[j][p]
        root = jnp.sqrt(d)
        low[j][j] = root
        inv_diag.append(1.0 / root)
        for i in range(j + 1, K):
            v = entry(i, j)
            for p in range(j):
                v = v - low[i][p] * low[j][p]
            low[i][j] = v * inv_diag[j]
    inverse = [[None] * K for _ in range(K)]
    for j in range(K):
        inverse[j][j] = inv_diag[j]
        for i in range(j + 1, K):
            v = low[i][j] * inverse[j][j]
            for p in range(j + 1, i):
                v = v + low[i][p] * inverse[p][j]
            inverse[i][j] = -v * inv_diag[i]
    growth = jnp.zeros((8, X), F32)
    for i in range(K):
        for j in range(i + 1):
            growth = jnp.where((row == j) & (lane == i), low[i][j], growth)
    growth_ref[...] = growth
    square = step * step
    copies = []
    for p in range(4):
        for t in range(Z // 8):
            adv = []
            for k in range(K):
                f = 4 * k + p
                a, b = (
                    (first[0, f], first[1, f])
                    if t == 0
                    else (a_ref[f, tile(t), :], b_ref[f, tile(t), :])
                )
                adv.append(q_ref[f, tile(t), :] + step * a + square * b)
            for k in range(K):
                v = inverse[k][0] * adv[0]
                for j in range(1, k + 1):
                    v = v + inverse[k][j] * adv[j]
                out[p, k, tile(t), :] = v
        copies.append(pltpu.make_async_copy(out.at[p], out_hbm.at[:, p], sems.at[p]))
        copies[p].start()
    for copy in copies:
        copy.wait()


def call(body, outs, scratch=(), cost=2000000, limit=24, **more):
    shapes = [jax.ShapeDtypeStruct(s, F32) for s in outs]
    return pl.pallas_call(
        body,
        out_shape=shapes,
        scratch_shapes=[pltpu.VMEM(s, F32) if isinstance(s, tuple) else s for s in scratch],
        compiler_params=pltpu.CompilerParams(vmem_limit_bytes=limit * 1024 * 1024),
        cost_estimate=pl.CostEstimate(flops=cost, bytes_accessed=cost, transcendentals=0),
        **more,
    )


def ring(array, axes, step):
    size = lax.axis_size(axes)
    return lax.ppermute(array, axes, [(i, (i + step) % size) for i in range(size)])


def diagonal(array):
    gx, gz = lax.axis_size(GX), lax.axis_size(GZ)
    pairs_of = [
        (i * gz + j, (i - 1) % gx * gz + (j - 1) % gz) for i in range(gx) for j in range(gz)
    ]
    return lax.ppermute(array, GX + GZ, pairs_of)


def gathered(array, axes):
    return lax.all_to_all(array, axes, 0, 0)


def per_device(tangents, mass, internal, velocity):
    cells = float(2 * Z * X * lax.axis_size(GX) * lax.axis_size(GZ))
    near, far = lax.axis_size(NEAR), lax.axis_size(FAR)
    whole, inner, edge = (NF, Z, X), (NF, 24, X), (NF, 8, X)
    half, small, red = (2 * K, Z, X), (3, Z, X), (20, 8, X)
    weights = jnp.asarray(np.stack(bands()))
    q = tangents.reshape(whole)
    coef, pack, rows, corner = call(
        prep_kernel,
        [(NC, Z, X), small, (NA, 8, X), (3, 8, X)],
        [whole, (2, Z, X), (2, Z, X), pltpu.SemaphoreType.DMA((4,))],
        limit=60,
        in_specs=[pl.BlockSpec(memory_space=pl.ANY)] * 4,
    )(q, mass, internal, velocity)
    side = ring(pack, GX, -1)
    below = ring(rows, GZ, -1)
    corner = diagonal(corner)
    (square,) = call(square_kernel, [(8, X)], [(5, 8, X)])(q)
    warm, last, own = call(own_kernel, [half, (6, Z, X), (8, X)])(q, coef, square)
    ad, bd, ap, bp, tail, packed, under, kept, part = call(
        inner_kernel,
        [inner, inner, (2, 24, X), (2, 24, X), edge, (9, 8, 2 * X), (6, 8, X), (6, 8, X), (8, X)],
        [(6, Z, 2 * X), (3, Z, 2 * X), (2, 24, X), (K, 4, Z, X), (K, 2, Z, X), red, red],
    )(q, coef, warm, side, last, own, below, weights)
    ade, bde, ape, bpe, sums = call(
        edge_kernel,
        [edge, edge, (2, 8, X), (2, 8, X), (near, 8, X)],
        [(NF, 16, X), (NC, 16, X), (K, 2, 16, X), (6, 16, 2 * X), (3, 16, 2 * X), (2, 8, X)]
        + [(K, 4, 16, X), (K, 2, 16, X), red, red],
    )(q, kept, warm, below, corner, under, tail, packed, part, weights)
    sums = jnp.sum(gathered(sums, NEAR), axis=0)
    (give,) = call(give_kernel, [(2, 2, Z, X)])(ap, bp, ape, bpe)
    got = ring(give, GX, 1)
    sums, got = lax.optimization_barrier((sums, got))
    sums = gathered(jnp.broadcast_to(sums, (far, 8, X)), FAR)
    a, b, down = call(place_kernel, [whole, whole, (8 * NF, X)])(ad, bd, ade, bde, give, got)
    above = ring(down, GZ, 1)
    out, growth = call(
        functools.partial(finish_kernel, cells),
        [(K, 4, Z, X), (8, X)],
        [(2, NF, 8, X), (4, K, Z, X), pltpu.SemaphoreType.DMA((4,))],
        out_specs=[pl.BlockSpec(memory_space=pl.ANY), pl.BlockSpec(memory_space=pltpu.VMEM)],
    )(q, a, b, above, sums)
    return (out.reshape(tangents.shape), growth[:, :K])


def solution(mesh):
    gx, gz = mesh.devices.shape
    fine = Mesh(mesh.devices.reshape(gx // 4, 4, gz // 4, 4), GX + GZ)
    in_specs = (P(None, None, None, GZ, GX),) + (P(None, GZ, GX),) * 3
    out_specs = (P(None, None, None, GZ, GX), P())
    return jax.shard_map(
        per_device, mesh=fine, in_specs=in_specs, out_specs=out_specs, check_vma=False
    )
```

```python
import functools

import jax
import jax.numpy as jnp
import numpy as np
from jax import lax
from jax.experimental import pallas as pl
from jax.experimental.pallas import tpu as pltpu
from jax.sharding import Mesh, PartitionSpec as P

NEWTON = 4
isochoric_warmth_coefficient = 3.0
attraction = 0.5
acentric_coefficient_gradient = 0.6
covolume = 0.15
root_two = 1.4142135623730951
viscosity = 0.2
conductivity = 1.0
courant_number = 0.5

K = 8
NF = 4 * K
NC = 6
NA = NF + NC
Z = 32
X = 128
GX = ("xh", "xl")
GZ = ("zh", "zl")
NEAR = ("xl", "zl")
FAR = ("xh", "zh")
F32 = jnp.float32
STEP = 4


def bands():
    first = {-2: 1.0, -1: -8.0, 1: 8.0, 2: -1.0}
    second = {-2: -1.0, -1: 16.0, 0: -30.0, 1: 16.0, 2: -1.0}
    main, packed = [], []
    for band in (first, second):
        w, v = np.zeros((X, X), np.float32), np.zeros((2 * X, 2 * X), np.float32)
        for d, value in band.items():
            for j in range(X):
                if 0 <= j + d < X:
                    w[j + d, j] = value
            for g in range(16):
                for j in range(16):
                    if 0 <= j + d < 16:
                        at = [X * (c // 8) + 8 * g + c % 8 for c in (j + d, j)]
                        v[at[0], at[1]] = value
        main.append(np.concatenate([w, w]))
        packed.append(v)
    return [
        np.concatenate(main, axis=1).astype(jnp.bfloat16),
        *(v.astype(jnp.bfloat16) for v in packed),
    ]


def departure(cell_mass_concentration):
    low_term = 1.0 + (1.0 - root_two) * covolume * cell_mass_concentration
    high_term = 1.0 + (1.0 + root_two) * covolume * cell_mass_concentration
    factor = attraction * (1.0 + acentric_coefficient_gradient) / (2.0 * root_two * covolume)
    value = factor * (jnp.log(low_term) - jnp.log(high_term))
    slope = factor * (
        (1.0 - root_two) * covolume / low_term - (1.0 + root_two) * covolume / high_term
    )
    return (value, slope)


def slopes(mass, internal):
    deviation, departure_slope = departure(mass)
    warmth = internal / isochoric_warmth_coefficient
    for _ in range(NEWTON):
        root = jnp.sqrt(warmth)
        multiplier = 1.0 + acentric_coefficient_gradient * (1.0 - root)
        mismatch = isochoric_warmth_coefficient * warmth + deviation * multiplier - internal
        gradient = isochoric_warmth_coefficient - deviation * acentric_coefficient_gradient / (
            2.0 * root
        )
        warmth = warmth - mismatch / gradient
    root = jnp.sqrt(warmth)
    multiplier = 1.0 + acentric_coefficient_gradient * (1.0 - root)
    gradient = isochoric_warmth_coefficient - deviation * acentric_coefficient_gradient / (
        2.0 * root
    )
    energy = 1.0 / gradient
    return (-departure_slope * multiplier * energy, energy)


def lanes():
    return lax.broadcasted_iota(jnp.int32, (8, X), 1)


def tile(t):
    return slice(8 * t, 8 * t + 8)


def prep_kernel(
    q_hbm, mass_hbm, internal_hbm, velocity_hbm, coef_ref, pack_ref, rows_ref, corner_ref, q, mass, internal, sems
):
    copies = [
        pltpu.make_async_copy(src, dst, sems.at[i])
        for i, (src, dst) in enumerate(
            (
                (mass_hbm, mass),
                (internal_hbm, internal),
                (velocity_hbm, coef_ref.at[pl.ds(4, 2)]),
                (q_hbm, q),
            )
        )
    ]
    for copy in copies:
        copy.start()
    copies[0].wait()
    copies[1].wait()
    density, energy = slopes(mass[...], internal[...])
    coef_ref[0:2] = density
    coef_ref[2:4] = energy
    copies[2].wait()
    copies[3].wait()
    group = lanes() >> 3
    for t in range(Z // 8):
        for c in range(2):
            acc = q[2 * c, tile(t), :]
            for y in range(2):
                for k in range(K):
                    i = 8 * y + k
                    if i:
                        part = pltpu.roll(q[4 * k + 2 * c + y, tile(t), :], 8 * i, 1)
                        acc = jnp.where(group == i, part, acc)
            pack_ref[c, tile(t), :] = acc
        acc = jnp.where(group == 0, coef_ref[0, tile(t), :], 0.0)
        for i in range(1, NC):
            acc = jnp.where(group == i, pltpu.roll(coef_ref[i, tile(t), :], 8 * i, 1), acc)
        pack_ref[2, tile(t), :] = acc
    for n in range(3):
        corner_ref[n] = pack_ref[n, 0:8, :]
    for f in range(NA):
        rows_ref[f] = q[f, 0:8, :] if f < NF else coef_ref[f - NF, 0:8, :]


def pairs():
    return [(k, m, (k + m) % K) for k in range(K) for m in range(5 if k < 4 else 4)]


def columns(result, lane, red, extra, sets):
    row = lax.broadcasted_iota(jnp.int32, (8, X), 0)
    mine = ((lane >> 3) & 7) == row
    rows = []
    for n in range(len(sets)):
        for m in range(5):
            acc = red[5 * n + m]
            if extra is not None:
                part = extra[5 * n + m]
                for d in (4, 2, 1):
                    part = part + pltpu.roll(part, d, 0)
                acc = acc + jnp.where(mine, part, 0.0)
            rows.append(jnp.where(row < 4, acc, 0.0) if m == 4 else acc)
    if len(rows) % 2:
        rows.append(rows[-1])
    rows = jnp.concatenate(rows, axis=0)
    high, low = split(rows)
    last = (rows - high.astype(F32) - low.astype(F32)).astype(jnp.bfloat16)
    total = product(
        jnp.concatenate([high, low, last], axis=1), jnp.ones((3 * X, X), jnp.bfloat16)
    )
    for n, place in enumerate(sets):
        for m in range(5):
            at = 8 * (5 * n + m)
            result = jnp.where(lane == 8 * place + m, total[at : at + 8, :], result)
    return result


def put(red, n, k, acc):
    red[n, k : k + 1, :] = jnp.sum(acc, axis=0, keepdims=True)


def side_of(packed, i):
    return pltpu.roll(packed, X - 8 * i, 1) if i else packed


def fill(pair, lane):
    out = jnp.where(lane < 8, pair[0], 0.0)
    out = jnp.where((lane >= 64) & (lane < 72), pltpu.roll(pair[1], 64, 1), out)
    for d in (8, 16, 32):
        out = out + pltpu.roll(out, d, 1)
    return out


def each():
    return [(k, y) for k in range(K) for y in range(2)]


def last_columns(field, coef, last_ref, at, lane):
    group = lane >> 3
    got = []
    for c in range(2):
        acc = None
        for y in range(2):
            for k in range(K):
                i = 8 * y + k
                part = field(4 * k + 2 * c + y)
                part = pltpu.roll(part, (8 * i + 8) % X, 1) if i < 15 else part
                acc = part if i == 0 else jnp.where(group == i, part, acc)
        got.append(acc)
    full = [fill([pltpu.roll(coef(2 * n + y), 8, 1) for y in range(2)], lane) for n in range(3)]
    got.append(full[0] * got[0] + full[1] * got[1])
    for n, part in enumerate(got + full):
        last_ref[n, at : at + 8, :] = part


def square_kernel(q_ref, sums_ref, red):
    red[...] = jnp.zeros_like(red)
    for k, m, l in pairs():
        acc = jnp.zeros((8, X), F32)
        for p in range(4):
            for t in range(Z // 8):
                acc = acc + q_ref[4 * k + p, tile(t), :] * q_ref[4 * l + p, tile(t), :]
        put(red, m, k, acc)
    sums_ref[...] = columns(jnp.zeros((8, X), F32), lanes(), red, None, (0,))


def own_kernel(q_ref, coef_ref, square_ref, warm_ref, last_ref, sums_ref):
    lane = lanes()
    for t in range(Z // 8):
        for k, y in each():
            warm_ref[2 * k + y, tile(t), :] = (
                coef_ref[y, tile(t), :] * q_ref[4 * k + y, tile(t), :]
                + coef_ref[2 + y, tile(t), :] * q_ref[4 * k + 2 + y, tile(t), :]
            )
        last_columns(
            lambda f: q_ref[f, tile(t), :], lambda n: coef_ref[n, tile(t), :],
            last_ref, 8 * t, lane,
        )
    speed = jnp.zeros((8, X), F32)
    for y in range(2):
        for t in range(Z // 8):
            v = coef_ref[4 + y, tile(t), :]
            speed = speed + v * v
    total = jnp.sum(speed, axis=1, keepdims=True)
    sums_ref[...] = jnp.where(lane == 40, total, square_ref[...])


def join(side_ref, last_ref, packed, t, at, lane):
    rows = slice(at, at + 8)
    got = [side_ref[c, tile(t), :] for c in range(2)]
    third = side_ref[2, tile(t), :]
    full = [fill([side_of(third, 2 * n + y) for y in range(2)], lane) for n in range(3)]
    got.append(full[0] * got[0] + full[1] * got[1])
    for n, part in enumerate(got + full):
        packed[n, rows, 0:X] = last_ref[n, tile(t), :]
        packed[n, rows, X : 2 * X] = part


def split(x):
    high = x.astype(jnp.bfloat16)
    return high, (x - high.astype(F32)).astype(jnp.bfloat16)


def product(x, w):
    return jnp.dot(x, w, preferred_element_type=F32)


def rest(at, other):
    return 16.0 * (at(-1) + at(1) + other) - (at(-2) + at(2)) - 60.0 * at(0)


def main_rates(count, weights, r_at, e_at, t_at):
    def stack(at):
        rows = jnp.concatenate([at(i) for i in range(count)], axis=0)
        return jnp.concatenate(split(rows), axis=1)

    both = product(stack(r_at), weights[...])
    slope = product(stack(e_at), weights[:, 0:X])
    bend = product(stack(t_at), weights[:, X : 2 * X])
    out = []
    for i in range(count):
        rows = slice(8 * i, 8 * i + 8)
        out.append((both[rows, 0:X], both[rows, X:], slope[rows], bend[rows]))
    return out


def main_rate(speed, parts, r_at, t_at, r_other, t_other):
    slope_r, bend_r, slope_e, bend_t = parts
    rate_r = speed * slope_r + (viscosity / 12.0) * (bend_r + rest(r_at, r_other))
    rate_e = speed * slope_e + (conductivity / 12.0) * (bend_t + rest(t_at, t_other))
    return rate_r, rate_e


def turned(x):
    return jnp.concatenate([pltpu.roll(x[:, 0:X], 64, 1), pltpu.roll(x[:, X:], 64, 1)], axis=1)


def packed_rate(speed, weights, at):
    def along(n, w):
        high, low = split(at(n, 0))
        return product(high, weights[1 + w]) + product(low, weights[1 + w])

    rate_r = speed * along(0, 0) + (viscosity / 12.0) * (
        along(0, 1) + rest(lambda d: at(0, d), turned(at(0, 0)))
    )
    rate_e = speed * along(1, 0) + (conductivity / 12.0) * (
        along(2, 1) + rest(lambda d: at(2, d), turned(at(2, 0)))
    )
    return rate_r, rate_e


def packed_steps(packed, wp, pa, blocks, first, second, count, lane):
    src, dst, height = first
    rows = slice(src, src + height)
    got = packed_rate(
        packed[5, rows, :] * (-1.0 / 12.0), wp, lambda n, d: packed[n, src + d : src + d + height, :]
    )
    out = slice(dst, dst + height)
    pa[0, out, :] = got[0]
    pa[1, out, :] = got[1]
    pa[2, out, :] = packed[3, rows, :] * got[0] + packed[4, rows, :] * got[1]
    here, there = second
    rows = slice(here, here + count)
    got = packed_rate(
        packed[5, rows, :] * (-1.0 / 12.0),
        wp,
        lambda n, d: pa[n, there + d : there + d + count, :],
    )
    qp, ap, bp = blocks
    low = (lax.broadcasted_iota(jnp.int32, (count, X), 1) & 7) < 4
    for c in range(2):
        for dest, value in (
            (qp, packed[c, rows, :]),
            (ap, pa[c, there : there + count, :]),
            (bp, 0.5 * got[c]),
        ):
            dest[c] = jnp.where(low, value[:, X:], value[:, 0:X])


def main_sums(red, q_at, ad, bd, tiles):
    for k, m, l in pairs():
        acc = [jnp.zeros((8, X), F32)] * 4
        for p in range(4):
            for t in range(tiles):
                qk, ql = q_at(4 * k + p, t), q_at(4 * l + p, t)
                ak, bk = (v[4 * k + p, tile(t), :] for v in (ad, bd))
                al, bl = (v[4 * l + p, tile(t), :] for v in (ad, bd))
                acc[0] = acc[0] + (qk * al + ak * ql)
                acc[1] = acc[1] + (ak * al + (qk * bl + bk * ql))
                acc[2] = acc[2] + (ak * bl + bk * al)
                acc[3] = acc[3] + bk * bl
        for n in range(4):
            put(red, 5 * n + m, k, acc[n])


def packed_sums(extra, blocks, tiles, lane):
    acc = [jnp.zeros((8, X), F32) for _ in range(20)]
    for c in range(2):
        for t in range(tiles):
            q, a, b = (ref[c, tile(t), :] for ref in blocks)
            for m in range(5):

                def other(v, m=m):
                    if m == 0:
                        return v
                    near = pltpu.roll(v, X - 8 * m, 1)
                    return jnp.where((lane & 63) < 64 - 8 * m, near, pltpu.roll(v, 64 - 8 * m, 1))

                ql, al, bl = other(q), other(a), other(b)
                acc[m] = acc[m] + (q * al + a * ql)
                acc[5 + m] = acc[5 + m] + (a * al + (q * bl + b * ql))
                acc[10 + m] = acc[10 + m] + (a * bl + b * al)
                acc[15 + m] = acc[15 + m] + b * bl
    for n in range(20):
        extra[n] = acc[n]


def inside(rows):
    lane = lax.broadcasted_iota(jnp.int32, (rows, X), 1)
    return (lane >= 4) & (lane < 124)


def inner_kernel(
    q_ref, coef_ref, warm_ref, side_ref, last_ref, own_ref, below_ref, w_ref,
    ad_ref, bd_ref, ap_ref, bp_ref, tail_ref, packed_ref, under_ref, kept_ref, sums_ref,
    packed, pa, qp, am, tm, red, extra,
):
    lane = lanes()
    red[...] = jnp.zeros_like(red)
    for t in range(Z // 8):
        join(side_ref, last_ref, packed, t, 8 * t, lane)
    packed_steps(packed, w_ref, pa, (qp, ap_ref, bp_ref), (2, 2, 28), (4, 4), 24, lane)
    packed_sums(extra, (qp, ap_ref, bp_ref), 3, lane)
    for n in range(3):
        packed_ref[n] = pa[n, 22:30, :]
    for n in range(6):
        packed_ref[3 + n] = packed[n, 24:32, :]
        kept_ref[n] = coef_ref[n, 24:32, :]
    last_columns(lambda f: below_ref[f], lambda n: below_ref[NF + n], under_ref, 0, lane)
    keep = inside(8)

    def vectors(j, carry):
        planes = [(STEP * j + i, y) for i in range(STEP) for y in range(2)]
        order = [(k, y, r) for k, y in planes for r in (2, 10, 18, 22)]
        parts = main_rates(
            len(order),
            w_ref.at[0],
            lambda i: q_ref[4 * order[i][0] + order[i][1], order[i][2] : order[i][2] + 8, :],
            lambda i: q_ref[4 * order[i][0] + 2 + order[i][1], order[i][2] : order[i][2] + 8, :],
            lambda i: warm_ref[2 * order[i][0] + order[i][1], order[i][2] : order[i][2] + 8, :],
        )
        for i, (k, y, r) in enumerate(order):
            rows = slice(r, r + 8)
            got = main_rate(
                coef_ref[4 + y, rows, :] * (-1.0 / 12.0),
                parts[i],
                lambda d: q_ref[4 * k + y, r + d : r + d + 8, :],
                lambda d: warm_ref[2 * k + y, r + d : r + d + 8, :],
                q_ref[4 * k + 1 - y, rows, :],
                warm_ref[2 * k + 1 - y, rows, :],
            )
            for c in range(2):
                am[k, 2 * c + y, rows, :] = got[c]
            tm[k, y, rows, :] = coef_ref[y, rows, :] * got[0] + coef_ref[2 + y, rows, :] * got[1]
        order = [(k, y, r) for k, y in planes for r in (4, 12, 20)]
        parts = main_rates(
            len(order),
            w_ref.at[0],
            lambda i: am[order[i][0], order[i][1], order[i][2] : order[i][2] + 8, :],
            lambda i: am[order[i][0], 2 + order[i][1], order[i][2] : order[i][2] + 8, :],
            lambda i: tm[order[i][0], order[i][1], order[i][2] : order[i][2] + 8, :],
        )
        for i, (k, y, r) in enumerate(order):
            rows = slice(r, r + 8)
            got = main_rate(
                coef_ref[4 + y, rows, :] * (-1.0 / 12.0),
                parts[i],
                lambda d: am[k, y, r + d : r + d + 8, :],
                lambda d: tm[k, y, r + d : r + d + 8, :],
                am[k, 1 - y, rows, :],
                tm[k, 1 - y, rows, :],
            )
            for c in range(2):
                f = 4 * k + 2 * c + y
                bd_ref[f, r - 4 : r + 4, :] = jnp.where(keep, 0.5 * got[c], 0.0)
                ad_ref[f, r - 4 : r + 4, :] = jnp.where(keep, am[k, 2 * c + y, rows, :], 0.0)
        for k in [STEP * j + i for i in range(STEP)]:
            for p in range(4):
                tail_ref[4 * k + p] = am[k, p, 22:30, :]
        return carry

    lax.fori_loop(0, K // STEP, vectors, 0)
    main_sums(red, lambda f, t: q_ref[f, 8 * t + 4 : 8 * t + 12, :], ad_ref, bd_ref, 3)
    sums_ref[...] = columns(own_ref[...], lane, red, extra, range(1, 5))


def edge_kernel(
    q_ref, kept_ref, warm_ref, below_ref, corner_ref, last_ref, tail_ref, packed_ref, inner_ref, w_ref,
    ad_ref, bd_ref, ap_ref, bp_ref, sums_ref,
    em, ec, wm, packed, pa, qp, am, tm, red, extra,
):
    lane = lanes()
    red[...] = jnp.zeros_like(red)
    for n in range(NC):
        ec[n, 0:8, :] = kept_ref[n]
        ec[n, 8:16, :] = below_ref[NF + n]
        packed[n, 0:8, :] = packed_ref[3 + n]
    join(corner_ref, last_ref, packed, 0, 8, lane)
    for n in range(3):
        pa[n, 0:8, :] = packed_ref[n]
    packed_steps(packed, w_ref, pa, (qp, ap_ref, bp_ref), (6, 8, 8), (4, 6), 8, lane)
    packed_sums(extra, (qp, ap_ref, bp_ref), 1, lane)
    keep = inside(8)
    for k in range(K):
        base = 4 * k
        for p in range(4):
            em[base + p, 0:8, :] = q_ref[base + p, 24:32, :]
            em[base + p, 8:16, :] = below_ref[base + p]
            am[k, p, 0:8, :] = tail_ref[base + p]
        for y in range(2):
            wm[k, y, 0:8, :] = warm_ref[2 * k + y, 24:32, :]
            wm[k, y, 8:16, :] = (
                ec[y, 8:16, :] * below_ref[base + y] + ec[2 + y, 8:16, :] * below_ref[base + 2 + y]
            )
    order = each()
    parts = main_rates(
        16,
        w_ref.at[0],
        lambda i: em[4 * order[i][0] + order[i][1], 6:14, :],
        lambda i: em[4 * order[i][0] + 2 + order[i][1], 6:14, :],
        lambda i: wm[order[i][0], order[i][1], 6:14, :],
    )
    for i, (k, y) in enumerate(order):
        got = main_rate(
            ec[4 + y, 6:14, :] * (-1.0 / 12.0),
            parts[i],
            lambda d: em[4 * k + y, 6 + d : 14 + d, :],
            lambda d: wm[k, y, 6 + d : 14 + d, :],
            em[4 * k + 1 - y, 6:14, :],
            wm[k, 1 - y, 6:14, :],
        )
        for c in range(2):
            am[k, 2 * c + y, 8:16, :] = got[c]
        tm[k, y, 8:16, :] = ec[y, 6:14, :] * got[0] + ec[2 + y, 6:14, :] * got[1]
        tm[k, y, 4:8, :] = (
            ec[y, 2:6, :] * am[k, y, 4:8, :] + ec[2 + y, 2:6, :] * am[k, 2 + y, 4:8, :]
        )
    parts = main_rates(
        16,
        w_ref.at[0],
        lambda i: am[order[i][0], order[i][1], 6:14, :],
        lambda i: am[order[i][0], 2 + order[i][1], 6:14, :],
        lambda i: tm[order[i][0], order[i][1], 6:14, :],
    )
    for i, (k, y) in enumerate(order):
        got = main_rate(
            ec[4 + y, 4:12, :] * (-1.0 / 12.0),
            parts[i],
            lambda d: am[k, y, 6 + d : 14 + d, :],
            lambda d: tm[k, y, 6 + d : 14 + d, :],
            am[k, 1 - y, 6:14, :],
            tm[k, 1 - y, 6:14, :],
        )
        for c in range(2):
            f = 4 * k + 2 * c + y
            bd_ref[f] = jnp.where(keep, 0.5 * got[c], 0.0)
            ad_ref[f] = jnp.where(keep, am[k, 2 * c + y, 6:14, :], 0.0)
    main_sums(red, lambda f, t: em[f, 4:12, :], ad_ref, bd_ref, 1)
    result = columns(jnp.zeros((8, X), F32), lane, red, extra, range(1, 5)) + inner_ref[...]
    for n in range(sums_ref.shape[0]):
        sums_ref[n] = result


def give_kernel(ap_ref, bp_ref, ape_ref, bpe_ref, out_ref):
    for n, (ref, edge) in enumerate(((ap_ref, ape_ref), (bp_ref, bpe_ref))):
        for c in range(2):
            out_ref[n, c, 0:24, :] = ref[c]
            out_ref[n, c, 24:32, :] = edge[c]


def place_kernel(ad_ref, bd_ref, ade_ref, bde_ref, mine_ref, got_ref, a_ref, b_ref, down_ref):
    lane = lanes()
    strip = (lane < 4) | (lane >= 124)
    low = (lane & 7) < 4
    for n, (ref, edge, out) in enumerate(((ad_ref, ade_ref, a_ref), (bd_ref, bde_ref, b_ref))):
        for c in range(2):
            for t in range(Z // 8):
                mine = pltpu.roll(mine_ref[n, c, tile(t), :], X - 8, 1)
                both = jnp.where(low, got_ref[n, c, tile(t), :], mine)
                for y in range(2):
                    for k in range(K):
                        f = 4 * k + 2 * c + y
                        part = ref[f, tile(t), :] if t < 3 else edge[f]
                        part = jnp.where(strip, side_of(both, 8 * y + k), part)
                        if t < 3:
                            out[f, 8 * t + 4 : 8 * t + 12, :] = part
                        else:
                            out[f, 28:32, :] = part[0:4, :]
                            out[f, 0:4, :] = jnp.zeros((4, X), F32)
                            r = 4 * (NF * n + f)
                            down_ref[r : r + 4, :] = part[4:8, :]


def finish_kernel(cells, q_ref, a_ref, b_ref, above_ref, sums_ref, out_ref, growth_ref, first):
    lane = lanes()
    row = lax.broadcasted_iota(jnp.int32, (8, X), 0)
    for n, ref in enumerate((a_ref, b_ref)):
        for f in range(NF):
            r = 4 * (NF * n + f)
            first[n, f, 0:4, :] = above_ref[r : r + 4, :]
            first[n, f, 4:8, :] = ref[f, 4:8, :]
    total = sums_ref[0]
    for n in range(1, sums_ref.shape[0]):
        total = total + sums_ref[n]
    speed = jnp.broadcast_to(jnp.sum(total[:, 40:41], axis=0, keepdims=True), (8, X))
    step = courant_number / jnp.sqrt(speed * (1.0 / cells) + 1e-05)
    gram = total
    power = step
    for n in range(1, 5):
        gram = gram + power * pltpu.roll(total, X - 8 * n, 1)
        power = power * step
    gram = gram * (1.0 / (2.0 * cells))
    cols = [jnp.broadcast_to(gram[:, m : m + 1], (8, X)) for m in range(5)]

    def entry(i, j):
        k, m = (j, i - j) if i - j <= 4 else (i, j - i + K)
        if m == 4:
            k = min(i, j)
        return jnp.broadcast_to(cols[m][k : k + 1, :], (8, X))

    low = [[None] * K for _ in range(K)]
    inv_diag = []
    for j in range(K):
        d = entry(j, j)
        for p in range(j):
            d = d - low[j][p] * low[j][p]
        root = jnp.sqrt(d)
        low[j][j] = root
        inv_diag.append(1.0 / root)
        for i in range(j + 1, K):
            v = entry(i, j)
            for p in range(j):
                v = v - low[i][p] * low[j][p]
            low[i][j] = v * inv_diag[j]
    inverse = [[None] * K for _ in range(K)]
    for j in range(K):
        inverse[j][j] = inv_diag[j]
        for i in range(j + 1, K):
            v = low[i][j] * inverse[j][j]
            for p in range(j + 1, i):
                v = v + low[i][p] * inverse[p][j]
            inverse[i][j] = -v * inv_diag[i]
    growth = jnp.zeros((8, X), F32)
    for i in range(K):
        for j in range(i + 1):
            growth = jnp.where((row == j) & (lane == i), low[i][j], growth)
    growth_ref[...] = growth
    square = step * step
    for p in range(4):
        for t in range(Z // 8):
            adv = []
            for k in range(K):
                f = 4 * k + p
                a, b = (
                    (first[0, f], first[1, f])
                    if t == 0
                    else (a_ref[f, tile(t), :], b_ref[f, tile(t), :])
                )
                adv.append(q_ref[f, tile(t), :] + step * a + square * b)
            for k in range(K):
                v = inverse[k][0] * adv[0]
                for j in range(1, k + 1):
                    v = v + inverse[k][j] * adv[j]
                out_ref[4 * k + p, tile(t), :] = v


def call(body, outs, scratch=(), cost=2000000, limit=24, **more):
    shapes = [jax.ShapeDtypeStruct(s, F32) for s in outs]
    return pl.pallas_call(
        body,
        out_shape=shapes,
        scratch_shapes=[pltpu.VMEM(s, F32) if isinstance(s, tuple) else s for s in scratch],
        compiler_params=pltpu.CompilerParams(vmem_limit_bytes=limit * 1024 * 1024),
        cost_estimate=pl.CostEstimate(flops=cost, bytes_accessed=cost, transcendentals=0),
        **more,
    )


def ring(array, axes, step):
    size = lax.axis_size(axes)
    return lax.ppermute(array, axes, [(i, (i + step) % size) for i in range(size)])


def diagonal(array):
    gx, gz = lax.axis_size(GX), lax.axis_size(GZ)
    pairs_of = [
        (i * gz + j, (i - 1) % gx * gz + (j - 1) % gz) for i in range(gx) for j in range(gz)
    ]
    return lax.ppermute(array, GX + GZ, pairs_of)


def gathered(array, axes):
    return lax.all_to_all(array, axes, 0, 0)


def per_device(tangents, mass, internal, velocity):
    cells = float(2 * Z * X * lax.axis_size(GX) * lax.axis_size(GZ))
    near, far = lax.axis_size(NEAR), lax.axis_size(FAR)
    whole, inner, edge = (NF, Z, X), (NF, 24, X), (NF, 8, X)
    half, small, red = (2 * K, Z, X), (3, Z, X), (20, 8, X)
    weights = jnp.asarray(np.stack(bands()))
    q = tangents.reshape(whole)
    coef, pack, rows, corner = call(
        prep_kernel,
        [(NC, Z, X), small, (NA, 8, X), (3, 8, X)],
        [whole, (2, Z, X), (2, Z, X), pltpu.SemaphoreType.DMA((4,))],
        limit=60,
        in_specs=[pl.BlockSpec(memory_space=pl.ANY)] * 4,
    )(q, mass, internal, velocity)
    side = ring(pack, GX, -1)
    below = ring(rows, GZ, -1)
    corner = diagonal(corner)
    (square,) = call(square_kernel, [(8, X)], [(5, 8, X)])(q)
    warm, last, own = call(own_kernel, [half, (6, Z, X), (8, X)])(q, coef, square)
    ad, bd, ap, bp, tail, packed, under, kept, part = call(
        inner_kernel,
        [inner, inner, (2, 24, X), (2, 24, X), edge, (9, 8, 2 * X), (6, 8, X), (6, 8, X), (8, X)],
        [(6, Z, 2 * X), (3, Z, 2 * X), (2, 24, X), (K, 4, Z, X), (K, 2, Z, X), red, red],
    )(q, coef, warm, side, last, own, below, weights)
    ade, bde, ape, bpe, sums = call(
        edge_kernel,
        [edge, edge, (2, 8, X), (2, 8, X), (near, 8, X)],
        [(NF, 16, X), (NC, 16, X), (K, 2, 16, X), (6, 16, 2 * X), (3, 16, 2 * X), (2, 8, X)]
        + [(K, 4, 16, X), (K, 2, 16, X), red, red],
    )(q, kept, warm, below, corner, under, tail, packed, part, weights)
    sums = jnp.sum(gathered(sums, NEAR), axis=0)
    (give,) = call(give_kernel, [(2, 2, Z, X)])(ap, bp, ape, bpe)
    got = ring(give, GX, 1)
    sums, got = lax.optimization_barrier((sums, got))
    sums = gathered(jnp.broadcast_to(sums, (far, 8, X)), FAR)
    a, b, down = call(place_kernel, [whole, whole, (8 * NF, X)])(ad, bd, ade, bde, give, got)
    above = ring(down, GZ, 1)
    out, growth = call(
        functools.partial(finish_kernel, cells), [whole, (8, X)], [(2, NF, 8, X)]
    )(q, a, b, above, sums)
    return (out.reshape(tangents.shape), growth[:, :K])


def solution(mesh):
    gx, gz = mesh.devices.shape
    fine = Mesh(mesh.devices.reshape(gx // 4, 4, gz // 4, 4), GX + GZ)
    in_specs = (P(None, None, None, GZ, GX),) + (P(None, GZ, GX),) * 3
    out_specs = (P(None, None, None, GZ, GX), P())
    return jax.shard_map(
        per_device, mesh=fine, in_specs=in_specs, out_specs=out_specs, check_vma=False
    )
```
